32 devices in a mesh: wide: 4 (over y, x), narrow: 8 (over z, core).
Axes of the slice: x: 2, y: 2, z: 4, core: 2. Of those that a mesh axis runs over, the one named last changes fastest.
Arguments:
- coeff: bfloat16 [4096, 2048], P('wide', 'narrow'), may hold values from -6 to 6
- groupb_row_energy: float32 [4096], P('wide'), may hold values from 0.2 to 2
- groupa_energy: float32 [2048], P('narrow'), may hold values from 0.2 to 2
- groupb_basis_values: bfloat16 [4, 1024, 64], replicated, may hold values from -0.1875 to 0.1875
- basis_a: bfloat16 [2048, 2048], replicated, may hold values from -0.125 to 0.125
- potential: float32 [1024, 2048], P(('wide', 'narrow')), may hold values from 0.1 to 3
- slot_sparse_level: int32 [64], P('wide'), may hold values from 0 to 3
- block_pad: int32 [64], P('wide'), may hold values from 0 to 64, as said below
- slot_grid_offset: int32 [64], P('wide'), may hold values from 0 to 1023
Outputs:
- product: float32 [4096, 2048], P('wide', 'narrow')
The draws below stay inside these ranges and needn't reach their ends.
Inputs may be any that keep to these rules, and one draw needn't show every extreme that they name: `block_pad`: A value of 64 marks an empty slot; one index of wide has all 16 slots filled and another only its first.
All inputs are finite; a program needn't handle non-finite values.
Results may differ from the reference program's by a relative error of at most 0.0023.
Values may be sent and summed in bfloat16 or wider, within the bound.
No kernel may reach another device: no remote copies, remote signals or barrier semaphores. Data moves between devices by JAX's collectives and lax.ppermute only.
A program may use at most 128 MiB of HBM per device.

```python
import math
import jax
import jax.numpy as jnp
from jax import lax

GROUPA_FUNCTIONS = 2048
GA = 2048
BLOCK_FUNCTIONS = 64
SPARSE_LEVELS = 4
SLOTS = 16
GROUPB_POINTS = 1024
SLOT_TOTAL = 64
BROWS = 4096
N_WIDE = 4


def draw_block_pad(key, part):
    key = jax.random.fold_in(key, 3)
    keys = jax.random.split(key, 4)
    first = jax.random.randint(keys[0], (N_WIDE,), 1, SLOTS + 1)
    second = jax.random.randint(keys[1], (N_WIDE,), 1, SLOTS + 1)
    filled = jnp.minimum(first, second)
    fullest = jax.random.randint(keys[2], (), 0, N_WIDE)
    devices = jnp.arange(N_WIDE)
    filled = jnp.where(devices == fullest, SLOTS, filled)
    filled = jnp.where(devices == (fullest + 1) % N_WIDE, 1, filled)
    alive = jnp.arange(SLOTS)[None, :] < filled[:, None]
    padding = jax.random.randint(keys[3], (N_WIDE, SLOTS), 0, BLOCK_FUNCTIONS)
    padding = padding.at[fullest, 0].set(0)
    return jnp.where(alive, padding, BLOCK_FUNCTIONS).reshape(-1).astype(jnp.int32)


def set_ends(result, own_key, least, largest):
    longest = result.shape.index(max(result.shape))
    spots = []
    for shift in (0, 1):
        where = [jax.random.randint(jax.random.fold_in(own_key, axis), (), 0, length) for axis, length in enumerate(result.shape)]
        where[longest] = (where[longest] + shift) % result.shape[longest]
        spots.append(tuple(where))
    return result.at[spots[0]].set(least).at[spots[1]].set(largest)


def levels(rng, shape, cuts, least, high):
    loudness, own = 1.0, jax.random.fold_in(rng, 6)
    for position, blocks in cuts:
        heights = jnp.exp(jax.random.uniform(jax.random.fold_in(own, position), (blocks,), jnp.float32, least / len(cuts), high / len(cuts)))
        loudness = loudness * jnp.repeat(heights, shape[position] // blocks).reshape([-1 if axis == position else 1 for axis in range(len(shape))])
    return loudness


def centred(key, extent, deviation, limit, shards=(), kind=jnp.bfloat16):
    drawn = deviation * jax.random.normal(key, extent, jnp.float32)
    if shards:
        drawn = drawn * levels(key, extent, shards, -0.22, 0.18)
    return jnp.clip(drawn, -limit, limit).astype(kind)


def setup_inputs(seed: int = 0) -> dict:
    key_of = jax.random.split(jax.random.key(seed), 10)
    return {
        "coeff": centred(key_of[0], (BROWS, GROUPA_FUNCTIONS), 1.0, 6.0, ((0, 4), (1, 8))),
        "groupb_row_energy": jnp.clip(jnp.exp(math.log(2.0) - 2.3025851 * jax.random.uniform(key_of[1], (BROWS,), jnp.float32) ** levels(key_of[1], (BROWS,), ((0, 4),), -0.2, 0.2)), 0.2, 2.0),
        "groupa_energy": jnp.clip(jnp.exp(math.log(2.0) - 2.3025851 * jax.random.uniform(key_of[2], (GROUPA_FUNCTIONS,), jnp.float32) ** levels(key_of[2], (GROUPA_FUNCTIONS,), ((0, 8),), -0.2, 0.2)), 0.2, 2.0),
        "groupb_basis_values": centred(key_of[3], (SPARSE_LEVELS, GROUPB_POINTS, BLOCK_FUNCTIONS), (SLOT_TOTAL * 16) ** -0.5, 0.1875),
        "basis_a": centred(key_of[4], (GROUPA_FUNCTIONS, GA), GROUPA_FUNCTIONS ** -0.5, 0.125),
        "potential": jnp.clip(jnp.exp(math.log(3.0) - 3.4011974 * jax.random.uniform(key_of[5], (GROUPB_POINTS, GA), jnp.float32) ** levels(key_of[5], (GROUPB_POINTS, GA), ((0, 32),), -0.2, 0.2)), 0.1, 3.0),
        "slot_sparse_level": set_ends(jax.random.randint(key_of[6], (SLOT_TOTAL,), 0, SPARSE_LEVELS), jax.random.fold_in(key_of[6], 1), 0, SPARSE_LEVELS - 1).astype(jnp.int32),
        "block_pad": draw_block_pad(jax.random.fold_in(key_of[9], 71), 0),
        "slot_grid_offset": set_ends(jax.random.randint(key_of[8], (SLOT_TOTAL,), 0, GROUPB_POINTS), jax.random.fold_in(key_of[8], 1), 0, GROUPB_POINTS - 1).astype(jnp.int32),
    }


def reference(coeff, groupb_row_energy, groupa_energy, groupb_basis_values, basis_a, potential, slot_sparse_level, block_pad, slot_grid_offset):
    positions = jnp.arange(BLOCK_FUNCTIONS)
    level_blocks = coeff.reshape(SLOT_TOTAL, BLOCK_FUNCTIONS, GROUPA_FUNCTIONS)
    alive_rows = positions[None, :] < (BLOCK_FUNCTIONS - block_pad)[:, None]
    masked = jnp.where(alive_rows[:, :, None], level_blocks, jnp.zeros((), jnp.bfloat16))

    def forward(total, entry):
        piece, level, shift, padding = entry

        def accumulate(current):
            rolled = jnp.roll(groupb_basis_values[level], shift, axis=0)
            return current + jnp.dot(rolled, piece, preferred_element_type=jnp.float32)

        return lax.cond(padding < BLOCK_FUNCTIONS, accumulate, lambda current: current, total), None

    initial = jnp.zeros((GROUPB_POINTS, GROUPA_FUNCTIONS), jnp.float32)
    summed, _ = lax.scan(forward, initial, (masked, slot_sparse_level, slot_grid_offset, block_pad))
    grid_b = summed.astype(jnp.bfloat16)
    on_grid = jnp.dot(grid_b, basis_a, preferred_element_type=jnp.float32)
    acted = (potential * on_grid).astype(jnp.bfloat16)
    returned = lax.dot_general(acted, basis_a, (((1,), (1,)), ((), ())), preferred_element_type=jnp.float32).astype(jnp.bfloat16)

    def backward(entry):
        level, shift, padding = entry

        def project(unused):
            rolled = jnp.roll(groupb_basis_values[level], shift, axis=0)
            return lax.dot_general(rolled, returned, (((0,), (0,)), ((), ())), preferred_element_type=jnp.float32)

        def nothing(unused):
            return jnp.zeros((BLOCK_FUNCTIONS, GROUPA_FUNCTIONS), jnp.float32)

        return lax.cond(padding < BLOCK_FUNCTIONS, project, nothing, 0)

    projected = lax.map(backward, (slot_sparse_level, slot_grid_offset, block_pad))
    diagonal_energy = groupb_row_energy.reshape(SLOT_TOTAL, BLOCK_FUNCTIONS)[:, :, None] + groupa_energy[None, None, :]
    hamiltonian_output = jnp.where(alive_rows[:, :, None], diagonal_energy * level_blocks.astype(jnp.float32) + projected, jnp.float32(0.0))
    return hamiltonian_output.reshape(SLOT_TOTAL * BLOCK_FUNCTIONS, GROUPA_FUNCTIONS)
```

```python
import functools

import jax
import jax.numpy as jnp
from jax import lax
from jax.experimental import pallas as pl
from jax.experimental.pallas import tpu as pltpu
from jax.sharding import PartitionSpec as P

VMEM_LIMIT = 40 * 1024 * 1024


def params():
    return pltpu.CompilerParams(vmem_limit_bytes=VMEM_LIMIT)


def forward_kernel(level_ref, pad_ref, shift_ref, coeff_ref, table_ref, partial_ref, rolled_ref):
    slots = pad_ref.shape[0]
    width = table_ref.shape[1]
    row = lax.broadcasted_iota(jnp.int32, (width, coeff_ref.shape[1]), 0)
    pieces = []
    for s in range(slots):
        rows = slice(s * width, (s + 1) * width)
        table = table_ref[level_ref[s]].astype(jnp.float32)
        rolled_ref[rows, :] = pltpu.roll(table, shift_ref[s], 1).astype(jnp.bfloat16)
        piece = coeff_ref[rows, :].astype(jnp.float32)
        pieces.append(jnp.where(row < width - pad_ref[s], piece, 0.0))
    masked = jnp.concatenate(pieces, axis=0)
    turned = masked.T.astype(jnp.bfloat16)
    total = jnp.dot(turned, rolled_ref[...], preferred_element_type=jnp.float32)
    partial_ref[...] = total.T.astype(jnp.bfloat16)


def forward(level, pad, shift, coeff, tables):
    rows, columns = coeff.shape
    points = tables.shape[2]
    smem = pl.BlockSpec(memory_space=pltpu.SMEM)
    vmem = pl.BlockSpec(memory_space=pltpu.VMEM)
    return pl.pallas_call(
        forward_kernel,
        out_shape=(
            jax.ShapeDtypeStruct((points, columns), jnp.bfloat16),
            jax.ShapeDtypeStruct((rows, points), jnp.bfloat16),
        ),
        in_specs=[smem, smem, smem, vmem, vmem],
        out_specs=(vmem, vmem),
        compiler_params=params(),
        name="forward",
    )(level, pad, shift, coeff, tables)


def grid_kernel(x_ref, basis_ref, potential_ref, out_ref, rows_ref, acted_ref):
    sources, groups, rows, columns = x_ref.shape
    for n in range(groups):
        total = x_ref[0, n].astype(jnp.float32)
        for w in range(1, sources):
            total = total + x_ref[w, n].astype(jnp.float32)
        rows_ref[:, n * columns : (n + 1) * columns] = total.astype(jnp.bfloat16)
    points = basis_ref.shape[1]
    step = min(points, 512)
    for p in range(0, points, step):
        on_grid = jnp.dot(
            rows_ref[...], basis_ref[:, p : p + step], preferred_element_type=jnp.float32
        )
        acted_ref[:, p : p + step] = (potential_ref[:, p : p + step] * on_grid).astype(jnp.bfloat16)
    for n in range(groups):
        returned = lax.dot_general(
            acted_ref[...],
            basis_ref[n * columns : (n + 1) * columns, :],
            (((1,), (1,)), ((), ())),
            preferred_element_type=jnp.float32,
        )
        out_ref[n] = returned.astype(jnp.bfloat16)


def grid_step(x, basis, potential):
    sources, groups, rows, columns = x.shape
    vmem = pl.BlockSpec(memory_space=pltpu.VMEM)
    return pl.pallas_call(
        grid_kernel,
        out_shape=jax.ShapeDtypeStruct((groups, rows, columns), jnp.bfloat16),
        in_specs=[vmem, vmem, vmem],
        out_specs=vmem,
        scratch_shapes=[
            pltpu.VMEM((rows, groups * columns), jnp.bfloat16),
            pltpu.VMEM((rows, basis.shape[1]), jnp.bfloat16),
        ],
        compiler_params=params(),
        name="grid_step",
    )(x, basis, potential)


def backward_kernel(pad_ref, rolled_ref, grid_ref, coeff_ref, row_ref, column_ref, out_ref):
    slots = pad_ref.shape[0]
    width = rolled_ref.shape[0] // slots
    out_ref[...] = jnp.dot(rolled_ref[...], grid_ref[...], preferred_element_type=jnp.float32)
    row = lax.broadcasted_iota(jnp.int32, (width, coeff_ref.shape[1]), 0)
    for s in range(slots):
        rows = slice(s * width, (s + 1) * width)
        energy = row_ref[rows, :] + column_ref[...]
        value = energy * coeff_ref[rows, :].astype(jnp.float32) + out_ref[rows, :]
        out_ref[rows, :] = jnp.where(row < width - pad_ref[s], value, 0.0)


def backward(pad, rolled, grid, coeff, row_energy, column_energy):
    smem = pl.BlockSpec(memory_space=pltpu.SMEM)
    vmem = pl.BlockSpec(memory_space=pltpu.VMEM)
    return pl.pallas_call(
        backward_kernel,
        out_shape=jax.ShapeDtypeStruct(coeff.shape, jnp.float32),
        in_specs=[smem, vmem, vmem, vmem, vmem, vmem],
        out_specs=vmem,
        compiler_params=params(),
        name="backward",
    )(pad, rolled, grid, coeff, row_energy[:, None], column_energy[None, :])


def body(
    wide,
    narrow,
    coeff,
    groupb_row_energy,
    groupa_energy,
    groupb_basis_values,
    basis_a,
    potential,
    slot_sparse_level,
    block_pad,
    slot_grid_offset,
):
    tables = jnp.swapaxes(groupb_basis_values, 1, 2)
    points = tables.shape[2]
    columns = coeff.shape[1]
    own = points // (wide * narrow)
    partial_value, rolled = forward(
        slot_sparse_level, block_pad, slot_grid_offset, coeff, tables
    )
    pieces = partial_value.reshape(wide * narrow, own, columns)
    x = lax.all_to_all(pieces, ("wide", "narrow"), split_axis=0, concat_axis=0, tiled=True)
    x = x.reshape(wide, narrow, own, columns)
    returned = grid_step(x, basis_a, potential)
    by_columns = lax.all_to_all(returned, "narrow", split_axis=0, concat_axis=0, tiled=True)
    whole_grid = lax.all_gather(
        by_columns.reshape(narrow * own, columns), "wide", axis=0, tiled=True
    )
    return backward(block_pad, rolled, whole_grid, coeff, groupb_row_energy, groupa_energy)


def solution(mesh):
    return jax.shard_map(
        functools.partial(body, mesh.shape["wide"], mesh.shape["narrow"]),
        mesh=mesh,
        in_specs=(
            P("wide", "narrow"),
            P("wide"),
            P("narrow"),
            P(),
            P(),
            P(("wide", "narrow"), None),
            P("wide"),
            P("wide"),
            P("wide"),
        ),
        out_specs=P("wide", "narrow"),
        check_vma=False,
    )
```

```python
import functools

import jax
import jax.numpy as jnp
from jax import lax
from jax.experimental import pallas as pl
from jax.experimental.pallas import tpu as pltpu
from jax.sharding import PartitionSpec as P

MIB = 1024 * 1024
HBM = pl.BlockSpec(memory_space=pltpu.HBM)
VMEM = pl.BlockSpec(memory_space=pltpu.VMEM)


def params(mib):
    return pltpu.CompilerParams(vmem_limit_bytes=mib * MIB)


def forward_kernel(
    wide,
    level_hbm,
    pad_hbm,
    shift_hbm,
    coeff_hbm,
    table_hbm,
    *rest,
):
    outs = rest[:wide]
    rolled_ref = rest[wide]
    level_ref, pad_ref, shift_ref, coeff_ref, table_ref, sems = rest[wide + 1 :]
    copies = [
        pltpu.make_async_copy(source, target, sems.at[i])
        for i, (source, target) in enumerate(
            (
                (level_hbm, level_ref),
                (pad_hbm, pad_ref),
                (shift_hbm, shift_ref),
                (table_hbm, table_ref),
                (coeff_hbm, coeff_ref),
            )
        )
    ]
    for copy in copies:
        copy.start()
    for copy in copies[:4]:
        copy.wait()
    slots = pad_ref.shape[0]
    width = table_ref.shape[1]
    for s in range(slots):
        rows = slice(s * width, (s + 1) * width)
        table = table_ref[level_ref[s]].astype(jnp.float32)
        rolled_ref[rows, :] = pltpu.roll(table, shift_ref[s], 1).astype(jnp.bfloat16)
    copies[4].wait()
    row = lax.broadcasted_iota(jnp.int32, (width, coeff_ref.shape[1]), 0)
    pieces = []
    for s in range(slots):
        rows = slice(s * width, (s + 1) * width)
        piece = coeff_ref[rows, :].astype(jnp.float32)
        pieces.append(jnp.where(row < width - pad_ref[s], piece, 0.0))
    masked = jnp.concatenate(pieces, axis=0)
    turned = masked.T.astype(jnp.bfloat16)
    me = lax.axis_index("wide")
    own = rolled_ref.shape[1] // wide
    for k in reversed(range(wide)):
        place = pl.multiple_of((me ^ k) * own, own)
        total = jnp.dot(
            turned, rolled_ref[:, pl.ds(place, own)], preferred_element_type=jnp.float32
        )
        outs[k][...] = total.T.astype(outs[k].dtype)


def forward(wide, level, pad, shift, coeff, tables):
    rows, columns = coeff.shape
    points = tables.shape[2]
    own = points // wide
    slots = pad.shape[0]
    return pl.pallas_call(
        functools.partial(forward_kernel, wide),
        out_shape=tuple(
            jax.ShapeDtypeStruct((own, columns), jnp.bfloat16 if k else jnp.float32)
            for k in range(wide)
        )
        + (jax.ShapeDtypeStruct((rows, points), jnp.bfloat16),),
        in_specs=[HBM] * 5,
        out_specs=(VMEM,) * (wide + 1),
        scratch_shapes=[
            pltpu.SMEM((slots,), jnp.int32),
            pltpu.SMEM((slots,), jnp.int32),
            pltpu.SMEM((slots,), jnp.int32),
            pltpu.VMEM(coeff.shape, coeff.dtype),
            pltpu.VMEM(tables.shape, tables.dtype),
            pltpu.SemaphoreType.DMA((5,)),
        ],
        compiler_params=params(32),
        name="forward",
    )(*(in_hbm(value) for value in (level, pad, shift, coeff, tables)))


def grid_kernel(x_ref, basis_hbm, potential_hbm, out_ref, basis_ref, potential_ref, acted_ref, sems):
    groups, rows, columns = x_ref.shape
    points = basis_ref.shape[1]
    step = 256
    pieces = points // step
    copies = [
        pltpu.make_async_copy(
            basis_hbm.at[:, pl.ds(p * step, step)],
            basis_ref.at[:, pl.ds(p * step, step)],
            sems.at[p],
        )
        for p in range(pieces)
    ]
    potential_copy = pltpu.make_async_copy(potential_hbm, potential_ref, sems.at[pieces])
    copies[0].start()
    potential_copy.start()
    for copy in copies[1:]:
        copy.start()
    x = jnp.concatenate([x_ref[n] for n in range(groups)], axis=1)
    for p in range(pieces):
        span = slice(p * step, (p + 1) * step)
        copies[p].wait()
        on_grid = jnp.dot(x, basis_ref[:, span], preferred_element_type=jnp.float32)
        if p == 0:
            potential_copy.wait()
        acted_ref[:, span] = (potential_ref[:, span] * on_grid).astype(jnp.bfloat16)
    for n in range(groups):
        returned = lax.dot_general(
            acted_ref[...],
            basis_ref[n * columns : (n + 1) * columns, :],
            (((1,), (1,)), ((), ())),
            preferred_element_type=jnp.float32,
        )
        out_ref[n] = returned.astype(jnp.bfloat16)


def grid_step(x, basis, potential):
    groups, rows, columns = x.shape
    return pl.pallas_call(
        grid_kernel,
        out_shape=jax.ShapeDtypeStruct((groups, rows, columns), jnp.bfloat16),
        in_specs=[VMEM, HBM, HBM],
        out_specs=VMEM,
        scratch_shapes=[
            pltpu.VMEM(basis.shape, basis.dtype),
            pltpu.VMEM(potential.shape, potential.dtype),
            pltpu.VMEM((rows, basis.shape[1]), jnp.bfloat16),
            pltpu.SemaphoreType.DMA((basis.shape[1] // 256 + 1,)),
        ],
        compiler_params=params(32),
        name="grid_step",
    )(x, in_hbm(basis), in_hbm(potential))


def backward_kernel(wide, *refs):
    pad_ref, rolled_ref = refs[:2]
    grids = refs[2 : 2 + wide]
    coeff_ref, row_ref, column_ref, out_ref = refs[2 + wide :]
    slots = pad_ref.shape[0]
    width = rolled_ref.shape[0] // slots
    me = lax.axis_index("wide")
    own = rolled_ref.shape[1] // wide
    total = None
    for k in range(wide):
        place = pl.multiple_of((me ^ k) * own, own)
        part = jnp.dot(
            rolled_ref[:, pl.ds(place, own)], grids[k][...], preferred_element_type=jnp.float32
        )
        total = part if total is None else total + part
    out_ref[...] = total
    row = lax.broadcasted_iota(jnp.int32, (width, coeff_ref.shape[1]), 0)
    for s in range(slots):
        rows = slice(s * width, (s + 1) * width)
        energy = row_ref[rows, :] + column_ref[...]
        value = energy * coeff_ref[rows, :].astype(jnp.float32) + out_ref[rows, :]
        out_ref[rows, :] = jnp.where(row < width - pad_ref[s], value, 0.0)


def backward(wide, pad, rolled, grids, coeff, row_energy, column_energy):
    smem = pl.BlockSpec(memory_space=pltpu.SMEM)
    return pl.pallas_call(
        functools.partial(backward_kernel, wide),
        out_shape=jax.ShapeDtypeStruct(coeff.shape, jnp.float32),
        in_specs=[smem] + [VMEM] * (wide + 4),
        out_specs=VMEM,
        compiler_params=params(32),
        name="backward",
    )(pad, rolled, *grids, coeff, row_energy[:, None], column_energy[None, :])


def in_hbm(value):
    return pltpu.with_memory_space_constraint(value, pltpu.HBM)


def exchange(value, step, size, axis):
    return lax.ppermute(value, axis, [(i, i ^ step) for i in range(size)])


def body(
    wide,
    narrow,
    coeff,
    groupb_row_energy,
    groupa_energy,
    groupb_basis_values,
    basis_a,
    potential,
    slot_sparse_level,
    block_pad,
    slot_grid_offset,
):
    tables = jnp.swapaxes(groupb_basis_values, 1, 2)
    points = tables.shape[2]
    columns = coeff.shape[1]
    own = points // (wide * narrow)
    *parts, rolled = forward(
        wide, slot_sparse_level, block_pad, slot_grid_offset, coeff, tables
    )
    summed = parts[0]
    for k in reversed(range(1, wide)):
        summed = summed + exchange(parts[k], k, wide, "wide").astype(jnp.float32)
    pieces = summed.astype(jnp.bfloat16).reshape(narrow, own, columns)
    x = lax.all_to_all(pieces, "narrow", split_axis=0, concat_axis=0, tiled=True)
    returned = grid_step(x, basis_a, potential)
    by_columns = lax.all_to_all(returned, "narrow", split_axis=0, concat_axis=0, tiled=True)
    mine = by_columns.reshape(narrow * own, columns)
    grids = [mine] + [exchange(mine, k, wide, "wide") for k in range(1, wide)]
    return backward(wide, block_pad, rolled, grids, coeff, groupb_row_energy, groupa_energy)


def solution(mesh):
    return jax.shard_map(
        functools.partial(body, mesh.shape["wide"], mesh.shape["narrow"]),
        mesh=mesh,
        in_specs=(
            P("wide", "narrow"),
            P("wide"),
            P("narrow"),
            P(),
            P(),
            P(("wide", "narrow"), None),
            P("wide"),
            P("wide"),
            P("wide"),
        ),
        out_specs=P("wide", "narrow"),
        check_vma=False,
    )
```

```python
import functools

import jax
import jax.numpy as jnp
from jax import lax
from jax.experimental import pallas as pl
from jax.experimental.pallas import tpu as pltpu
from jax.sharding import PartitionSpec as P

MIB = 1024 * 1024
HBM = pl.BlockSpec(memory_space=pltpu.HBM)
VMEM = pl.BlockSpec(memory_space=pltpu.VMEM)
BF16 = jnp.bfloat16
F32 = jnp.float32


def call(kernel, name, out_shape, in_specs, out_specs, scratch=(), flops=0, moved=0, mib=16):
    return pl.pallas_call(
        kernel,
        out_shape=out_shape,
        in_specs=in_specs,
        out_specs=out_specs,
        scratch_shapes=scratch,
        compiler_params=pltpu.CompilerParams(vmem_limit_bytes=mib * MIB),
        cost_estimate=pl.CostEstimate(flops=flops, bytes_accessed=moved, transcendentals=0),
        name=name,
    )


def in_hbm(value):
    return pltpu.with_memory_space_constraint(value, pltpu.HBM)


def array(shape, dtype):
    return jax.ShapeDtypeStruct(shape, dtype)


def dot(left, right):
    return jnp.dot(left, right, preferred_element_type=F32)


def dot_turned(left, right):
    return lax.dot_general(left, right, (((1,), (1,)), ((), ())), preferred_element_type=F32)


def first_kernel(
    wide,
    chips,
    level_hbm,
    pad_hbm,
    shift_hbm,
    coeff_hbm,
    table_hbm,
    basis_hbm,
    potential_hbm,
    out_ref,
    turned_ref,
    rolled_ref,
    basis_ref,
    potential_ref,
    level_ref,
    pad_ref,
    shift_ref,
    coeff_ref,
    table_ref,
    sems,
):
    place = lax.axis_index("narrow")
    core, chip = place % 2, place // 2
    columns = coeff_ref.shape[1]
    pairs = [
        (level_hbm, level_ref),
        (shift_hbm, shift_ref),
        (pad_hbm, pad_ref),
        (table_hbm, table_ref),
        (coeff_hbm, coeff_ref),
        (potential_hbm, potential_ref),
    ]
    for j in range(chips):
        start = pl.multiple_of(((chip ^ j) * 2 + core) * columns, columns)
        pairs.append((basis_hbm.at[pl.ds(start, columns), :], basis_ref.at[j]))
    copies = [
        pltpu.make_async_copy(source, target, sems.at[i])
        for i, (source, target) in enumerate(pairs)
    ]
    for copy in copies:
        copy.start()
    for copy in copies[:4]:
        copy.wait()
    slots = pad_ref.shape[0]
    width = table_ref.shape[1]
    for s in range(slots):
        rows = slice(s * width, (s + 1) * width)
        table = table_ref[level_ref[s]].astype(F32)
        rolled_ref[rows, :] = pltpu.roll(table, shift_ref[s], 1).astype(BF16)
    copies[4].wait()
    row = lax.broadcasted_iota(jnp.int32, (width, columns), 0)
    pieces = []
    for s in range(slots):
        rows = slice(s * width, (s + 1) * width)
        piece = coeff_ref[rows, :].astype(F32)
        pieces.append(jnp.where(row < width - pad_ref[s], piece, 0.0))
    turned_ref[...] = jnp.concatenate(pieces, axis=0).T.astype(BF16)
    me = lax.axis_index("wide")
    own = rolled_ref.shape[1] // wide
    start = pl.multiple_of((me ^ (wide - 1)) * own, own)
    total = dot(turned_ref[...], rolled_ref[:, pl.ds(start, own)])
    out_ref[...] = total.T.astype(BF16)
    for copy in copies[5:]:
        copy.wait()


def first(wide, chips, level, pad, shift, coeff, tables, basis, potential):
    rows, columns = coeff.shape
    points = tables.shape[2]
    own = points // wide
    slots = pad.shape[0]
    inputs = (level, pad, shift, coeff, tables, basis, potential)
    return call(
        functools.partial(first_kernel, wide, chips),
        "forward_first",
        (
            array((own, columns), BF16),
            array((columns, rows), BF16),
            array((rows, points), BF16),
            array((chips, columns, basis.shape[1]), BF16),
            array(potential.shape, F32),
        ),
        [HBM] * 7,
        (VMEM,) * 5,
        [
            pltpu.SMEM((slots,), jnp.int32),
            pltpu.SMEM((slots,), jnp.int32),
            pltpu.SMEM((slots,), jnp.int32),
            pltpu.VMEM(coeff.shape, coeff.dtype),
            pltpu.VMEM(tables.shape, tables.dtype),
            pltpu.SemaphoreType.DMA((6 + chips,)),
        ],
        flops=2 * rows * own * columns,
        moved=8 * MIB,
    )(*(in_hbm(value) for value in inputs))


def second_kernel(wide, turned_ref, rolled_ref, *outs):
    me = lax.axis_index("wide")
    own = rolled_ref.shape[1] // wide
    for k in range(wide - 1):
        start = pl.multiple_of((me ^ k) * own, own)
        total = dot(turned_ref[...], rolled_ref[:, pl.ds(start, own)])
        outs[k][...] = total.T.astype(outs[k].dtype)


def second(wide, turned, rolled):
    columns, rows = turned.shape
    own = rolled.shape[1] // wide
    return call(
        functools.partial(second_kernel, wide),
        "forward_rest",
        tuple(array((own, columns), BF16 if k else F32) for k in range(wide - 1)),
        [VMEM] * 2,
        (VMEM,) * (wide - 1),
        flops=2 * rows * own * columns * (wide - 1),
        moved=3 * MIB,
    )(turned, rolled)


def combine_kernel(wide, chips, *refs):
    parts, outs = refs[:wide], refs[wide:]
    chip = lax.axis_index("narrow") // 2
    rows = outs[0].shape[0]
    for j in range(chips):
        start = pl.multiple_of((chip ^ j) * rows, rows)
        total = parts[0][pl.ds(start, rows), :]
        for part in parts[1:]:
            total = total + part[pl.ds(start, rows), :].astype(F32)
        outs[j][...] = total.astype(BF16)


def combine(chips, parts):
    rows, columns = parts[0].shape
    wide = len(parts)
    return call(
        functools.partial(combine_kernel, wide, chips),
        "wide_sum",
        tuple(array((rows // chips, columns), BF16) for _ in range(chips)),
        [VMEM] * wide,
        (VMEM,) * chips,
        moved=MIB,
    )(*parts)


def early_kernel(x_ref, basis_ref, out_ref):
    out_ref[...] = dot(x_ref[...], basis_ref[0])


def early(x, basis):
    rows = x.shape[0]
    points = basis.shape[2]
    return call(
        early_kernel,
        "points_own",
        array((rows, points), F32),
        [VMEM] * 2,
        VMEM,
        flops=2 * rows * points * x.shape[1],
        moved=2 * MIB,
    )(x, basis)


def points_kernel(chips, total_ref, *refs):
    xs = refs[: chips - 1]
    basis_ref, mine_ref, theirs_ref, sum_ref = refs[chips - 1 :]
    core = lax.axis_index("narrow") % 2
    rows = mine_ref.shape[0]
    points = mine_ref.shape[1]
    step = min(points, 512)
    for p in range(0, points, step):
        span = slice(p, p + step)
        total = total_ref[:, span]
        for j in range(1, chips):
            total = total + dot(xs[j - 1][...], basis_ref[j, :, span])
        sum_ref[:, span] = total
    mine_ref[...] = sum_ref[pl.ds(pl.multiple_of(core * rows, rows), rows), :]
    theirs_ref[...] = sum_ref[pl.ds(pl.multiple_of((1 - core) * rows, rows), rows), :]


def to_points(total, xs, basis):
    rows, points = total.shape
    half = array((rows // 2, points), F32)
    chips = len(xs) + 1
    return call(
        functools.partial(points_kernel, chips),
        "points_rest",
        (half, half),
        [VMEM] * (chips + 1),
        (VMEM, VMEM),
        [pltpu.VMEM((rows, points), F32)],
        flops=2 * rows * points * xs[0].shape[1] * (chips - 1),
        moved=4 * MIB,
    )(total, *xs, basis)


def act_kernel(mine_ref, other_ref, potential_ref, out_ref):
    on_grid = mine_ref[...] + other_ref[...]
    out_ref[...] = (potential_ref[...] * on_grid).astype(BF16)


def act(mine, other, potential):
    return call(
        act_kernel, "act", array(mine.shape, BF16), [VMEM] * 3, VMEM, moved=MIB
    )(mine, other, potential)


def back_kernel(chips, mine_ref, other_ref, basis_ref, *refs):
    outs, both_ref, rows_ref = refs[:chips - 1], refs[chips - 1], refs[chips]
    core = lax.axis_index("narrow") % 2
    rows = mine_ref.shape[0]
    rows_ref[pl.ds(pl.multiple_of(core * rows, rows), rows), :] = mine_ref[...].astype(F32)
    rows_ref[pl.ds(pl.multiple_of((1 - core) * rows, rows), rows), :] = other_ref[...].astype(F32)
    both_ref[...] = rows_ref[...].astype(BF16)
    for j in range(1, chips):
        outs[j - 1][...] = dot_turned(both_ref[...], basis_ref[j]).astype(BF16)


def to_functions(mine, other, basis):
    rows, points = mine.shape
    chips, columns, _ = basis.shape
    return call(
        functools.partial(back_kernel, chips),
        "functions_rest",
        tuple(array((2 * rows, columns), BF16) for _ in range(chips - 1))
        + (array((2 * rows, points), BF16),),
        [VMEM] * 3,
        (VMEM,) * chips,
        [pltpu.VMEM((2 * rows, points), F32)],
        flops=4 * rows * points * columns * (chips - 1),
        moved=4 * MIB,
    )(mine, other, basis)


def late_kernel(both_ref, basis_ref, out_ref):
    out_ref[...] = dot_turned(both_ref[...], basis_ref[0]).astype(BF16)


def late(both, basis):
    rows, points = both.shape
    columns = basis.shape[1]
    return call(
        late_kernel,
        "functions_own",
        array((rows, columns), BF16),
        [VMEM] * 2,
        VMEM,
        flops=2 * rows * points * columns,
        moved=2 * MIB,
    )(both, basis)


def assemble_kernel(*refs):
    parts, out_ref = refs[:-1], refs[-1]
    chip = lax.axis_index("narrow") // 2
    rows = parts[0].shape[0]
    for j, part in enumerate(parts):
        start = pl.multiple_of((chip ^ j) * rows, rows)
        out_ref[pl.ds(start, rows), :] = part[...]


def assemble(parts):
    rows, columns = parts[0].shape
    chips = len(parts)
    return call(
        assemble_kernel,
        "assemble",
        array((rows * chips, columns), BF16),
        [VMEM] * chips,
        VMEM,
        moved=MIB // 4,
    )(*parts)


def own_kernel(wide, pad_ref, rolled_ref, grid_ref, coeff_ref, row_ref, column_ref, out_ref):
    slots = pad_ref.shape[0]
    width = rolled_ref.shape[0] // slots
    me = lax.axis_index("wide")
    own = rolled_ref.shape[1] // wide
    start = pl.multiple_of(me * own, own)
    out_ref[...] = dot(rolled_ref[:, pl.ds(start, own)], grid_ref[...])
    for s in range(slots):
        rows = slice(s * width, (s + 1) * width)
        energy = row_ref[rows, :] + column_ref[...]
        out_ref[rows, :] += energy * coeff_ref[rows, :].astype(F32)


def backward_own(wide, pad, rolled, grid, coeff, row_energy, column_energy):
    smem = pl.BlockSpec(memory_space=pltpu.SMEM)
    rows, columns = coeff.shape
    return call(
        functools.partial(own_kernel, wide),
        "backward_own",
        array(coeff.shape, F32),
        [smem] + [VMEM] * 5,
        VMEM,
        flops=2 * rows * columns * rolled.shape[1] // wide,
        moved=4 * MIB,
    )(pad, rolled, grid, coeff, row_energy[:, None], column_energy[None, :])


def rest_kernel(wide, pad_ref, total_ref, rolled_ref, *refs):
    grids, (out_hbm, out_ref, sems) = refs[: wide - 1], refs[wide - 1 :]
    slots = pad_ref.shape[0]
    width = rolled_ref.shape[0] // slots
    me = lax.axis_index("wide")
    own = rolled_ref.shape[1] // wide
    starts = [pl.multiple_of((me ^ k) * own, own) for k in range(wide)]
    steps = sems.shape[0]
    rows = rolled_ref.shape[0] // steps
    row = lax.broadcasted_iota(jnp.int32, (width, out_ref.shape[1]), 0)
    copies = []
    for i in range(steps):
        span = pl.ds(i * rows, rows)
        total = total_ref[span, :]
        for k in range(1, wide):
            total = total + dot(rolled_ref[span, pl.ds(starts[k], own)], grids[k - 1][...])
        for s in range(rows // width):
            slot = i * (rows // width) + s
            value = total[s * width : (s + 1) * width, :]
            out_ref[pl.ds(slot * width, width), :] = jnp.where(
                row < width - pad_ref[slot], value, 0.0
            )
        copies.append(pltpu.make_async_copy(out_ref.at[span, :], out_hbm.at[span, :], sems.at[i]))
        copies[-1].start()
    for copy in copies:
        copy.wait()


def backward_rest(wide, pad, total, rolled, grids):
    smem = pl.BlockSpec(memory_space=pltpu.SMEM)
    rows, columns = total.shape
    return call(
        functools.partial(rest_kernel, wide),
        "backward_rest",
        array(total.shape, F32),
        [smem] + [VMEM] * (wide + 1),
        HBM,
        [pltpu.VMEM(total.shape, F32), pltpu.SemaphoreType.DMA((4,))],
        flops=2 * rows * columns * rolled.shape[1],
        moved=4 * MIB,
    )(pad, total, rolled, *grids)


def exchange(value, step, size, axis):
    return lax.ppermute(value, axis, [(i, i ^ step) for i in range(size)])


def body(
    wide,
    narrow,
    coeff,
    groupb_row_energy,
    groupa_energy,
    groupb_basis_values,
    basis_a,
    potential,
    slot_sparse_level,
    block_pad,
    slot_grid_offset,
):
    chips = narrow // 2
    tables = jnp.swapaxes(groupb_basis_values, 1, 2)
    far, turned, rolled, basis, pot = first(
        wide,
        chips,
        slot_sparse_level,
        block_pad,
        slot_grid_offset,
        coeff,
        tables,
        basis_a,
        potential,
    )
    arrived = {wide - 1: exchange(far, wide - 1, wide, "wide")}
    parts = second(wide, turned, rolled)
    for k in range(1, wide - 1):
        arrived[k] = exchange(parts[k], k, wide, "wide")
    pieces = combine(chips, [parts[0]] + [arrived[k] for k in range(1, wide)])
    xs = [exchange(pieces[j], 2 * j, narrow, "narrow") for j in range(1, chips)]
    total = early(pieces[0], basis)
    mine, theirs = to_points(total, xs, basis)
    acted = act(mine, exchange(theirs, 1, narrow, "narrow"), pot)
    other = exchange(acted, 1, narrow, "narrow")
    *blocks, both = to_functions(acted, other, basis)
    sent = [exchange(blocks[j - 1], 2 * j, narrow, "narrow") for j in range(1, chips)]
    grid = assemble([late(both, basis)] + sent)
    grids = [exchange(grid, k, wide, "wide") for k in range(1, wide)]
    start = backward_own(
        wide, block_pad, rolled, grid, coeff, groupb_row_energy, groupa_energy
    )
    return backward_rest(wide, block_pad, start, rolled, grids)


def solution(mesh):
    return jax.shard_map(
        functools.partial(body, mesh.shape["wide"], mesh.shape["narrow"]),
        mesh=mesh,
        in_specs=(
            P("wide", "narrow"),
            P("wide"),
            P("narrow"),
            P(),
            P(),
            P(("wide", "narrow"), None),
            P("wide"),
            P("wide"),
            P("wide"),
        ),
        out_specs=P("wide", "narrow"),
        check_vma=False,
    )
```

```python
import functools

import jax
import jax.numpy as jnp
from jax import lax
from jax.experimental import pallas as pl
from jax.experimental.pallas import tpu as pltpu
from jax.sharding import PartitionSpec as P

MIB = 1024 * 1024
HBM = pl.BlockSpec(memory_space=pltpu.HBM)
VMEM = pl.BlockSpec(memory_space=pltpu.VMEM)
BF16 = jnp.bfloat16
F32 = jnp.float32


def call(kernel, name, out_shape, in_specs, out_specs, scratch=(), flops=0, moved=0, mib=16):
    return pl.pallas_call(
        kernel,
        out_shape=out_shape,
        in_specs=in_specs,
        out_specs=out_specs,
        scratch_shapes=scratch,
        compiler_params=pltpu.CompilerParams(vmem_limit_bytes=mib * MIB),
        cost_estimate=pl.CostEstimate(flops=flops, bytes_accessed=moved, transcendentals=0),
        name=name,
    )


def in_hbm(value):
    return pltpu.with_memory_space_constraint(value, pltpu.HBM)


def array(shape, dtype):
    return jax.ShapeDtypeStruct(shape, dtype)


def dot(left, right):
    return jnp.dot(left, right, preferred_element_type=F32)


def dot_turned(left, right):
    return lax.dot_general(left, right, (((1,), (1,)), ((), ())), preferred_element_type=F32)


def first_kernel(
    wide,
    chips,
    level_hbm,
    pad_hbm,
    shift_hbm,
    coeff_hbm,
    table_hbm,
    basis_hbm,
    potential_hbm,
    out_ref,
    rolled_ref,
    basis_ref,
    potential_ref,
    level_ref,
    pad_ref,
    shift_ref,
    coeff_ref,
    table_ref,
    turned_ref,
    sems,
):
    place = lax.axis_index("narrow")
    core = place % 2
    columns = coeff_ref.shape[1]
    pairs = [
        (level_hbm, level_ref),
        (shift_hbm, shift_ref),
        (pad_hbm, pad_ref),
        (table_hbm, table_ref),
        (coeff_hbm, coeff_ref),
        (potential_hbm, potential_ref),
    ]
    for j in range(chips):
        start = pl.multiple_of((j * 2 + core) * columns, columns)
        pairs.append((basis_hbm.at[pl.ds(start, columns), :], basis_ref.at[j]))
    copies = [
        pltpu.make_async_copy(source, target, sems.at[i])
        for i, (source, target) in enumerate(pairs)
    ]
    for copy in copies:
        copy.start()
    for copy in copies[:4]:
        copy.wait()
    slots = pad_ref.shape[0]
    width = table_ref.shape[1]
    for s in range(slots):
        rows = slice(s * width, (s + 1) * width)
        table = table_ref[level_ref[s]].astype(F32)
        rolled_ref[rows, :] = pltpu.roll(table, shift_ref[s], 1).astype(BF16)
    copies[4].wait()
    row = lax.broadcasted_iota(jnp.int32, (width, columns), 0)
    pieces = []
    for s in range(slots):
        rows = slice(s * width, (s + 1) * width)
        piece = coeff_ref[rows, :].astype(F32)
        pieces.append(jnp.where(row < width - pad_ref[s], piece, 0.0))
    turned_ref[...] = jnp.concatenate(pieces, axis=0).T.astype(BF16)
    own = rolled_ref.shape[1] // wide
    for d in range(wide):
        total = dot(turned_ref[...], rolled_ref[:, d * own : (d + 1) * own])
        out_ref[d] = total.T.astype(BF16)
    for copy in copies[5:]:
        copy.wait()


def first(wide, chips, level, pad, shift, coeff, tables, basis, potential):
    rows, columns = coeff.shape
    points = tables.shape[2]
    own = points // wide
    slots = pad.shape[0]
    inputs = (level, pad, shift, coeff, tables, basis, potential)
    return call(
        functools.partial(first_kernel, wide, chips),
        "forward_first",
        (
            array((wide, own, columns), BF16),
            array((rows, points), BF16),
            array((chips, columns, basis.shape[1]), BF16),
            array(potential.shape, F32),
        ),
        [HBM] * 7,
        (VMEM,) * 4,
        [
            pltpu.SMEM((slots,), jnp.int32),
            pltpu.SMEM((slots,), jnp.int32),
            pltpu.SMEM((slots,), jnp.int32),
            pltpu.VMEM(coeff.shape, coeff.dtype),
            pltpu.VMEM(tables.shape, tables.dtype),
            pltpu.VMEM((columns, rows), BF16),
            pltpu.SemaphoreType.DMA((6 + chips,)),
        ],
        flops=2 * rows * own * columns,
        moved=8 * MIB,
    )(*(in_hbm(value) for value in inputs))


def points_kernel(x_ref, basis_ref, mine_ref, theirs_ref, sum_ref):
    core = lax.axis_index("narrow") % 2
    chips = x_ref.shape[0]
    rows, points = mine_ref.shape
    step = min(points, 512)
    for p in range(0, points, step):
        span = slice(p, p + step)
        total = dot(x_ref[0], basis_ref[0, :, span])
        for j in range(1, chips):
            total = total + dot(x_ref[j], basis_ref[j, :, span])
        sum_ref[:, span] = total
    mine_ref[...] = sum_ref[pl.ds(pl.multiple_of(core * rows, rows), rows), :]
    theirs_ref[...] = sum_ref[pl.ds(pl.multiple_of((1 - core) * rows, rows), rows), :]


def to_points(x, basis):
    chips, rows, columns = x.shape
    points = basis.shape[2]
    half = array((rows // 2, points), F32)
    return call(
        points_kernel,
        "points",
        (half, half),
        [VMEM] * 2,
        (VMEM, VMEM),
        [pltpu.VMEM((rows, points), F32)],
        flops=2 * rows * points * columns * chips,
        moved=4 * MIB,
    )(x, basis)


def act_kernel(mine_ref, other_ref, potential_ref, out_ref):
    on_grid = mine_ref[...] + other_ref[...]
    out_ref[...] = (potential_ref[...] * on_grid).astype(BF16)


def act(mine, other, potential):
    return call(
        act_kernel, "act", array(mine.shape, BF16), [VMEM] * 3, VMEM, moved=MIB
    )(mine, other, potential)


def back_kernel(mine_ref, other_ref, basis_ref, out_ref, rows_ref):
    core = lax.axis_index("narrow") % 2
    rows = mine_ref.shape[0]
    rows_ref[pl.ds(pl.multiple_of(core * rows, rows), rows), :] = mine_ref[...].astype(F32)
    rows_ref[pl.ds(pl.multiple_of((1 - core) * rows, rows), rows), :] = other_ref[...].astype(F32)
    both = rows_ref[...].astype(BF16)
    for j in range(out_ref.shape[0]):
        out_ref[j] = dot_turned(both, basis_ref[j]).astype(BF16)


def to_functions(mine, other, basis):
    rows, points = mine.shape
    chips, columns, _ = basis.shape
    return call(
        back_kernel,
        "functions",
        array((chips, 2 * rows, columns), BF16),
        [VMEM] * 3,
        VMEM,
        [pltpu.VMEM((2 * rows, points), F32)],
        flops=4 * rows * points * columns * chips,
        moved=4 * MIB,
    )(mine, other, basis)


def own_kernel(wide, pad_ref, rolled_ref, grid_ref, coeff_ref, row_ref, column_ref, out_ref):
    slots = pad_ref.shape[0]
    width = rolled_ref.shape[0] // slots
    me = lax.axis_index("wide")
    own = rolled_ref.shape[1] // wide
    start = pl.multiple_of(me * own, own)
    out_ref[...] = dot(rolled_ref[:, pl.ds(start, own)], grid_ref[...])
    for s in range(slots):
        rows = slice(s * width, (s + 1) * width)
        energy = row_ref[rows, :] + column_ref[...]
        out_ref[rows, :] += energy * coeff_ref[rows, :].astype(F32)


def backward_own(wide, pad, rolled, grid, coeff, row_energy, column_energy):
    smem = pl.BlockSpec(memory_space=pltpu.SMEM)
    rows, columns = coeff.shape
    return call(
        functools.partial(own_kernel, wide),
        "backward_own",
        array(coeff.shape, F32),
        [smem] + [VMEM] * 5,
        VMEM,
        flops=2 * rows * columns * rolled.shape[1] // wide,
        moved=4 * MIB,
    )(pad, rolled, grid, coeff, row_energy[:, None], column_energy[None, :])


def rest_kernel(wide, pad_ref, total_ref, rolled_ref, *refs):
    grids, (out_hbm, out_ref, sems) = refs[: wide - 1], refs[wide - 1 :]
    slots = pad_ref.shape[0]
    width = rolled_ref.shape[0] // slots
    me = lax.axis_index("wide")
    own = rolled_ref.shape[1] // wide
    starts = [pl.multiple_of((me ^ k) * own, own) for k in range(wide)]
    steps = sems.shape[0]
    rows = rolled_ref.shape[0] // steps
    row = lax.broadcasted_iota(jnp.int32, (width, out_ref.shape[1]), 0)
    copies = []
    for i in range(steps):
        span = pl.ds(i * rows, rows)
        total = total_ref[span, :]
        for k in range(1, wide):
            total = total + dot(rolled_ref[span, pl.ds(starts[k], own)], grids[k - 1][...])
        for s in range(rows // width):
            slot = i * (rows // width) + s
            value = total[s * width : (s + 1) * width, :]
            out_ref[pl.ds(slot * width, width), :] = jnp.where(
                row < width - pad_ref[slot], value, 0.0
            )
        copies.append(pltpu.make_async_copy(out_ref.at[span, :], out_hbm.at[span, :], sems.at[i]))
        copies[-1].start()
    for copy in copies:
        copy.wait()


def backward_rest(wide, pad, total, rolled, grids):
    smem = pl.BlockSpec(memory_space=pltpu.SMEM)
    rows, columns = total.shape
    return call(
        functools.partial(rest_kernel, wide),
        "backward_rest",
        array(total.shape, F32),
        [smem] + [VMEM] * (wide + 1),
        HBM,
        [pltpu.VMEM(total.shape, F32), pltpu.SemaphoreType.DMA((4,))],
        flops=2 * rows * columns * rolled.shape[1],
        moved=4 * MIB,
    )(pad, total, rolled, *grids)


def exchange(value, step, size, axis):
    return lax.ppermute(value, axis, [(i, i ^ step) for i in range(size)])


def along_z(value, narrow):
    groups = [list(range(core, narrow, 2)) for core in range(2)]
    return lax.all_to_all(
        value, "narrow", split_axis=0, concat_axis=0, axis_index_groups=groups, tiled=True
    )


def body(
    wide,
    narrow,
    coeff,
    groupb_row_energy,
    groupa_energy,
    groupb_basis_values,
    basis_a,
    potential,
    slot_sparse_level,
    block_pad,
    slot_grid_offset,
):
    chips = narrow // 2
    tables = jnp.swapaxes(groupb_basis_values, 1, 2)
    parts, rolled, basis, pot = first(
        wide,
        chips,
        slot_sparse_level,
        block_pad,
        slot_grid_offset,
        coeff,
        tables,
        basis_a,
        potential,
    )
    columns = coeff.shape[1]
    arrived = lax.all_to_all(parts, "wide", split_axis=0, concat_axis=0, tiled=True)
    summed = jnp.sum(arrived.astype(F32), axis=0).astype(BF16)
    x = along_z(summed.reshape(chips, summed.shape[0] // chips, columns), narrow)
    mine, theirs = to_points(x, basis)
    acted = act(mine, exchange(theirs, 1, narrow, "narrow"), pot)
    other = exchange(acted, 1, narrow, "narrow")
    blocks = along_z(to_functions(acted, other, basis), narrow)
    grid = blocks.reshape(summed.shape)
    grids = [exchange(grid, k, wide, "wide") for k in range(1, wide)]
    start = backward_own(
        wide, block_pad, rolled, grid, coeff, groupb_row_energy, groupa_energy
    )
    return backward_rest(wide, block_pad, start, rolled, grids)


def solution(mesh):
    return jax.shard_map(
        functools.partial(body, mesh.shape["wide"], mesh.shape["narrow"]),
        mesh=mesh,
        in_specs=(
            P("wide", "narrow"),
            P("wide"),
            P("narrow"),
            P(),
            P(),
            P(("wide", "narrow"), None),
            P("wide"),
            P("wide"),
            P("wide"),
        ),
        out_specs=P("wide", "narrow"),
        check_vma=False,
    )
```

```python
import functools

import jax
import jax.numpy as jnp
from jax import lax
from jax.experimental import pallas as pl
from jax.experimental.pallas import tpu as pltpu
from jax.sharding import PartitionSpec as P

MIB = 1024 * 1024
HBM = pl.BlockSpec(memory_space=pltpu.HBM)
VMEM = pl.BlockSpec(memory_space=pltpu.VMEM)
BF16 = jnp.bfloat16
F32 = jnp.float32
LONG = 8


def call(kernel, name, out_shape, in_specs, out_specs, scratch=(), flops=0, moved=0, mib=16):
    return pl.pallas_call(
        kernel,
        out_shape=out_shape,
        in_specs=in_specs,
        out_specs=out_specs,
        scratch_shapes=scratch,
        compiler_params=pltpu.CompilerParams(vmem_limit_bytes=mib * MIB),
        cost_estimate=pl.CostEstimate(flops=flops, bytes_accessed=moved, transcendentals=0),
        name=name,
    )


def in_hbm(value):
    return pltpu.with_memory_space_constraint(value, pltpu.HBM)


def array(shape, dtype):
    return jax.ShapeDtypeStruct(shape, dtype)


def dot(left, right):
    return jnp.dot(left, right, preferred_element_type=F32)


def dot_turned(left, right):
    return lax.dot_general(left, right, (((1,), (1,)), ((), ())), preferred_element_type=F32)


def chunk_of(turned_ref, rolled_ref, wide, k):
    own = rolled_ref.shape[1] // wide
    start = pl.multiple_of((lax.axis_index("wide") ^ k) * own, own)
    return dot(turned_ref[...], rolled_ref[:, pl.ds(start, own)])


def first_kernel(
    wide,
    level_hbm,
    pad_hbm,
    shift_hbm,
    coeff_hbm,
    table_hbm,
    out_ref,
    turned_ref,
    rolled_ref,
    level_ref,
    pad_ref,
    shift_ref,
    coeff_ref,
    table_ref,
    sems,
):
    pairs = [
        (level_hbm, level_ref),
        (shift_hbm, shift_ref),
        (pad_hbm, pad_ref),
        (table_hbm, table_ref),
        (coeff_hbm, coeff_ref),
    ]
    copies = [
        pltpu.make_async_copy(source, target, sems.at[i])
        for i, (source, target) in enumerate(pairs)
    ]
    for copy in copies:
        copy.start()
    for copy in copies[:4]:
        copy.wait()
    slots = pad_ref.shape[0]
    width = table_ref.shape[1]
    for s in range(slots):
        rows = slice(s * width, (s + 1) * width)
        rolled_ref[rows, :] = pltpu.roll(table_ref[level_ref[s]], shift_ref[s], 1)
    copies[4].wait()
    row = lax.broadcasted_iota(jnp.int32, (width, coeff_ref.shape[1]), 0)
    pieces = []
    for s in range(slots):
        rows = slice(s * width, (s + 1) * width)
        piece = coeff_ref[rows, :].astype(F32)
        pieces.append(jnp.where(row < width - pad_ref[s], piece, 0.0).astype(BF16))
    turned_ref[...] = jnp.concatenate(pieces, axis=0).T
    out_ref[...] = chunk_of(turned_ref, rolled_ref, wide, wide - 1).astype(BF16).T


def first(wide, level, pad, shift, coeff, tables):
    rows, columns = coeff.shape
    points = tables.shape[2]
    slots = pad.shape[0]
    inputs = (level, pad, shift, coeff, tables)
    return call(
        functools.partial(first_kernel, wide),
        "forward_first",
        (
            array((points // wide, columns), BF16),
            array((columns, rows), BF16),
            array((rows, points), BF16),
        ),
        [HBM] * 5,
        (VMEM,) * 3,
        [
            pltpu.SMEM((slots,), jnp.int32),
            pltpu.SMEM((slots,), jnp.int32),
            pltpu.SMEM((slots,), jnp.int32),
            pltpu.VMEM(coeff.shape, coeff.dtype),
            pltpu.VMEM(tables.shape, tables.dtype),
            pltpu.SemaphoreType.DMA((5,)),
        ],
        flops=2 * rows * points // wide * columns,
        moved=4 * MIB,
    )(*(in_hbm(value) for value in inputs))


def chunk_kernel(wide, k, turned_ref, rolled_ref, out_ref):
    out_ref[...] = chunk_of(turned_ref, rolled_ref, wide, k).astype(BF16).T


def chunk(wide, k, turned, rolled):
    columns, rows = turned.shape
    own = rolled.shape[1] // wide
    return call(
        functools.partial(chunk_kernel, wide, k),
        "forward_chunk",
        array((own, columns), BF16),
        [VMEM] * 2,
        VMEM,
        flops=2 * rows * own * columns * LONG,
        moved=MIB * LONG,
    )(turned, rolled)


def last_kernel(
    wide,
    chips,
    turned_ref,
    rolled_ref,
    basis_hbm,
    potential_hbm,
    out_ref,
    basis_ref,
    potential_ref,
    sems,
):
    place = lax.axis_index("narrow")
    core, chip = place % 2, place // 2
    columns = turned_ref.shape[0]
    pairs = []
    for j in range(chips):
        start = pl.multiple_of(((chip ^ j) * 2 + core) * columns, columns)
        pairs.append((basis_hbm.at[pl.ds(start, columns), :], basis_ref.at[j]))
    pairs.append((potential_hbm, potential_ref))
    copies = [
        pltpu.make_async_copy(source, target, sems.at[i])
        for i, (source, target) in enumerate(pairs)
    ]
    for copy in copies:
        copy.start()
    out_ref[...] = chunk_of(turned_ref, rolled_ref, wide, 0).T
    for copy in copies:
        copy.wait()


def last(wide, chips, turned, rolled, basis, potential):
    columns, rows = turned.shape
    own = rolled.shape[1] // wide
    return call(
        functools.partial(last_kernel, wide, chips),
        "forward_own",
        (
            array((own, columns), F32),
            array((chips, columns, basis.shape[1]), BF16),
            array(potential.shape, F32),
        ),
        [VMEM, VMEM, HBM, HBM],
        (VMEM,) * 3,
        [pltpu.SemaphoreType.DMA((chips + 1,))],
        flops=2 * rows * own * columns,
        moved=10 * MIB,
    )(turned, rolled, in_hbm(basis), in_hbm(potential))


def combine_kernel(wide, chips, *refs):
    parts, outs = refs[:wide], refs[wide:]
    chip = lax.axis_index("narrow") // 2
    rows = outs[0].shape[0]
    for j in range(chips):
        start = pl.multiple_of((chip ^ j) * rows, rows)
        total = parts[0][pl.ds(start, rows), :]
        for part in parts[1:]:
            total = total + part[pl.ds(start, rows), :].astype(F32)
        outs[j][...] = total.astype(BF16)


def combine(chips, parts):
    rows, columns = parts[0].shape
    wide = len(parts)
    return call(
        functools.partial(combine_kernel, wide, chips),
        "wide_sum",
        tuple(array((rows // chips, columns), BF16) for _ in range(chips)),
        [VMEM] * wide,
        (VMEM,) * chips,
        moved=MIB,
    )(*parts)


def own_points_kernel(x_ref, basis_ref, out_ref):
    out_ref[...] = dot(x_ref[...], basis_ref[0])


def own_points(x, basis):
    rows = x.shape[0]
    points = basis.shape[2]
    return call(
        own_points_kernel,
        "points_own",
        array((rows, points), F32),
        [VMEM] * 2,
        VMEM,
        flops=2 * rows * points * x.shape[1],
        moved=2 * MIB,
    )(x, basis)


def more_points_kernel(j, total_ref, x_ref, basis_ref, out_ref):
    out_ref[...] = total_ref[...] + dot(x_ref[...], basis_ref[j])


def more_points(j, total, x, basis):
    rows, points = total.shape
    return call(
        functools.partial(more_points_kernel, j),
        "points_more",
        array((rows, points), F32),
        [VMEM] * 3,
        VMEM,
        flops=2 * rows * points * x.shape[1],
        moved=2 * MIB,
    )(total, x, basis)


def last_points_kernel(j, total_ref, x_ref, basis_ref, mine_ref, theirs_ref):
    core = lax.axis_index("narrow") % 2
    rows = mine_ref.shape[0]
    total = total_ref[...] + dot(x_ref[...], basis_ref[j])
    low, high = total[:rows], total[rows:]
    mine_ref[...] = jnp.where(core == 0, low, high)
    theirs_ref[...] = jnp.where(core == 0, high, low)


def last_points(j, total, x, basis):
    rows, points = total.shape
    half = array((rows // 2, points), F32)
    return call(
        functools.partial(last_points_kernel, j),
        "points_last",
        (half, half),
        [VMEM] * 3,
        (VMEM, VMEM),
        flops=2 * rows * points * x.shape[1],
        moved=2 * MIB,
    )(total, x, basis)


def act_kernel(mine_ref, other_ref, potential_ref, out_ref):
    on_grid = mine_ref[...] + other_ref[...]
    out_ref[...] = (potential_ref[...] * on_grid).astype(BF16)


def act(mine, other, potential):
    return call(
        act_kernel, "act", array(mine.shape, BF16), [VMEM] * 3, VMEM, moved=MIB
    )(mine, other, potential)


def first_functions_kernel(j, mine_ref, other_ref, basis_ref, out_ref, both_ref):
    core = lax.axis_index("narrow") % 2
    rows = mine_ref.shape[0]
    mine, other = mine_ref[...].astype(F32), other_ref[...].astype(F32)
    both_ref[:rows] = jnp.where(core == 0, mine, other).astype(BF16)
    both_ref[rows:] = jnp.where(core == 0, other, mine).astype(BF16)
    out_ref[...] = dot_turned(both_ref[...], basis_ref[j]).astype(BF16)


def first_functions(j, mine, other, basis):
    rows, points = mine.shape
    columns = basis.shape[1]
    return call(
        functools.partial(first_functions_kernel, j),
        "functions_first",
        (array((2 * rows, columns), BF16), array((2 * rows, points), BF16)),
        [VMEM] * 3,
        (VMEM, VMEM),
        flops=4 * rows * points * columns,
        moved=2 * MIB,
    )(mine, other, basis)


def functions_kernel(j, both_ref, basis_ref, out_ref):
    out_ref[...] = dot_turned(both_ref[...], basis_ref[j]).astype(BF16)


def functions(j, both, basis):
    rows, points = both.shape
    columns = basis.shape[1]
    long = LONG if j else 1
    return call(
        functools.partial(functions_kernel, j),
        "functions_more",
        array((rows, columns), BF16),
        [VMEM] * 2,
        VMEM,
        flops=2 * rows * points * columns * long,
        moved=2 * MIB * long,
    )(both, basis)


def assemble_kernel(*refs):
    parts, out_ref = refs[:-1], refs[-1]
    chip = lax.axis_index("narrow") // 2
    rows = parts[0].shape[0]
    for j, part in enumerate(parts):
        start = pl.multiple_of((chip ^ j) * rows, rows)
        out_ref[pl.ds(start, rows), :] = part[...]


def assemble(parts):
    rows, columns = parts[0].shape
    chips = len(parts)
    return call(
        assemble_kernel,
        "assemble",
        array((rows * chips, columns), BF16),
        [VMEM] * chips,
        VMEM,
        moved=MIB // 4,
    )(*parts)


def own_kernel(wide, pad_ref, rolled_ref, grid_ref, coeff_ref, row_ref, column_ref, out_ref):
    slots = pad_ref.shape[0]
    width = rolled_ref.shape[0] // slots
    me = lax.axis_index("wide")
    own = rolled_ref.shape[1] // wide
    start = pl.multiple_of(me * own, own)
    out_ref[...] = dot(rolled_ref[:, pl.ds(start, own)], grid_ref[...])
    for s in range(slots):
        rows = slice(s * width, (s + 1) * width)
        energy = row_ref[rows, :] + column_ref[...]
        out_ref[rows, :] += energy * coeff_ref[rows, :].astype(F32)


def backward_own(wide, pad, rolled, grid, coeff, row_energy, column_energy):
    smem = pl.BlockSpec(memory_space=pltpu.SMEM)
    rows, columns = coeff.shape
    return call(
        functools.partial(own_kernel, wide),
        "backward_own",
        array(coeff.shape, F32),
        [smem] + [VMEM] * 5,
        VMEM,
        flops=2 * rows * columns * rolled.shape[1] // wide,
        moved=4 * MIB,
    )(pad, rolled, grid, coeff, row_energy[:, None], column_energy[None, :])


def more_kernel(wide, k, total_ref, rolled_ref, grid_ref, out_ref):
    own = rolled_ref.shape[1] // wide
    start = pl.multiple_of((lax.axis_index("wide") ^ k) * own, own)
    out_ref[...] = total_ref[...] + dot(rolled_ref[:, pl.ds(start, own)], grid_ref[...])


def backward_more(wide, k, total, rolled, grid):
    rows, columns = total.shape
    return call(
        functools.partial(more_kernel, wide, k),
        "backward_more",
        array(total.shape, F32),
        [VMEM] * 3,
        VMEM,
        flops=2 * rows * columns * rolled.shape[1] // wide,
        moved=3 * MIB,
    )(total, rolled, grid)


def end_kernel(wide, k, pad_ref, total_ref, rolled_ref, grid_ref, out_hbm, out_ref, sems):
    slots = pad_ref.shape[0]
    width = rolled_ref.shape[0] // slots
    own = rolled_ref.shape[1] // wide
    start = pl.multiple_of((lax.axis_index("wide") ^ k) * own, own)
    steps = sems.shape[0]
    rows = rolled_ref.shape[0] // steps
    row = lax.broadcasted_iota(jnp.int32, (width, out_ref.shape[1]), 0)
    copies = []
    for i in range(steps):
        span = pl.ds(i * rows, rows)
        total = total_ref[span, :] + dot(rolled_ref[span, pl.ds(start, own)], grid_ref[...])
        for s in range(rows // width):
            slot = i * (rows // width) + s
            value = total[s * width : (s + 1) * width, :]
            out_ref[pl.ds(slot * width, width), :] = jnp.where(
                row < width - pad_ref[slot], value, 0.0
            )
        copies.append(pltpu.make_async_copy(out_ref.at[span, :], out_hbm.at[span, :], sems.at[i]))
        copies[-1].start()
    for copy in copies:
        copy.wait()


def backward_end(wide, k, pad, total, rolled, grid):
    smem = pl.BlockSpec(memory_space=pltpu.SMEM)
    rows, columns = total.shape
    return call(
        functools.partial(end_kernel, wide, k),
        "backward_end",
        array(total.shape, F32),
        [smem] + [VMEM] * 3,
        HBM,
        [pltpu.VMEM(total.shape, F32), pltpu.SemaphoreType.DMA((4,))],
        flops=2 * rows * columns * rolled.shape[1] // wide,
        moved=4 * MIB,
    )(pad, total, rolled, grid)


def exchange(value, step, size, axis):
    return lax.ppermute(value, axis, [(i, i ^ step) for i in range(size)])


def body(
    wide,
    narrow,
    coeff,
    groupb_row_energy,
    groupa_energy,
    groupb_basis_values,
    basis_a,
    potential,
    slot_sparse_level,
    block_pad,
    slot_grid_offset,
):
    chips = narrow // 2
    tables = jnp.swapaxes(groupb_basis_values, 1, 2)
    far, turned, rolled = first(
        wide, slot_sparse_level, block_pad, slot_grid_offset, coeff, tables
    )
    arrived = {wide - 1: exchange(far, wide - 1, wide, "wide")}
    for k in range(1, wide - 1):
        arrived[k] = exchange(chunk(wide, k, turned, rolled), k, wide, "wide")
    mine, basis, pot = last(wide, chips, turned, rolled, basis_a, potential)
    pieces = combine(chips, [mine] + [arrived[k] for k in range(1, wide)])
    xs = [exchange(pieces[j], 2 * j, narrow, "narrow") for j in range(1, chips)]
    total = own_points(pieces[0], basis)
    for j in range(1, chips - 1):
        total = more_points(j, total, xs[j - 1], basis)
    mine, theirs = last_points(chips - 1, total, xs[-1], basis)
    acted = act(mine, exchange(theirs, 1, narrow, "narrow"), pot)
    other = exchange(acted, 1, narrow, "narrow")
    block, both = first_functions(chips - 1, acted, other, basis)
    sent = {chips - 1: exchange(block, 2 * (chips - 1), narrow, "narrow")}
    for j in reversed(range(1, chips - 1)):
        sent[j] = exchange(functions(j, both, basis), 2 * j, narrow, "narrow")
    grid = assemble([functions(0, both, basis)] + [sent[j] for j in range(1, chips)])
    grids = [exchange(grid, k, wide, "wide") for k in range(1, wide)]
    total = backward_own(
        wide, block_pad, rolled, grid, coeff, groupb_row_energy, groupa_energy
    )
    for k in range(1, wide - 1):
        total = backward_more(wide, k, total, rolled, grids[k - 1])
    return backward_end(wide, wide - 1, block_pad, total, rolled, grids[-1])


def solution(mesh):
    return jax.shard_map(
        functools.partial(body, mesh.shape["wide"], mesh.shape["narrow"]),
        mesh=mesh,
        in_specs=(
            P("wide", "narrow"),
            P("wide"),
            P("narrow"),
            P(),
            P(),
            P(("wide", "narrow"), None),
            P("wide"),
            P("wide"),
            P("wide"),
        ),
        out_specs=P("wide", "narrow"),
        check_vma=False,
    )
```

```python
import functools

import jax
import jax.numpy as jnp
from jax import lax
from jax.experimental import pallas as pl
from jax.experimental.pallas import tpu as pltpu
from jax.sharding import PartitionSpec as P

MIB = 1024 * 1024
HBM = pl.BlockSpec(memory_space=pltpu.HBM)
VMEM = pl.BlockSpec(memory_space=pltpu.VMEM)
BF16 = jnp.bfloat16
F32 = jnp.float32
LONG = 8


def call(kernel, name, out_shape, in_specs, out_specs, scratch=(), flops=0, moved=0, mib=16):
    return pl.pallas_call(
        kernel,
        out_shape=out_shape,
        in_specs=in_specs,
        out_specs=out_specs,
        scratch_shapes=scratch,
        compiler_params=pltpu.CompilerParams(vmem_limit_bytes=mib * MIB),
        cost_estimate=pl.CostEstimate(flops=flops, bytes_accessed=moved, transcendentals=0),
        name=name,
    )


def in_hbm(value):
    return pltpu.with_memory_space_constraint(value, pltpu.HBM)


def array(shape, dtype):
    return jax.ShapeDtypeStruct(shape, dtype)


def dot(left, right):
    return jnp.dot(left, right, preferred_element_type=F32)


def dot_turned(left, right):
    return lax.dot_general(left, right, (((1,), (1,)), ((), ())), preferred_element_type=F32)


def chunk_of(turned_ref, rolled_ref, wide, k):
    own = rolled_ref.shape[1] // wide
    start = pl.multiple_of((lax.axis_index("wide") ^ k) * own, own)
    return dot(turned_ref[...], rolled_ref[:, pl.ds(start, own)])


def store_halves(chips, total, far_ref, near_ref):
    upper = lax.axis_index("narrow") // 2 >= chips // 2
    rows = far_ref.shape[0]
    turned = total.astype(BF16).T.astype(F32)
    low, high = turned[:rows], turned[rows:]
    far_ref[...] = jnp.where(upper, low, high).astype(BF16)
    near_ref[...] = jnp.where(upper, high, low).astype(BF16)


def halves(rows, columns):
    return (array((rows // 2, columns), BF16),) * 2


def first_kernel(
    wide,
    chips,
    level_hbm,
    pad_hbm,
    shift_hbm,
    coeff_hbm,
    table_hbm,
    far_ref,
    near_ref,
    turned_ref,
    rolled_ref,
    level_ref,
    pad_ref,
    shift_ref,
    coeff_ref,
    table_ref,
    sems,
):
    pairs = [
        (level_hbm, level_ref),
        (shift_hbm, shift_ref),
        (pad_hbm, pad_ref),
        (table_hbm, table_ref),
        (coeff_hbm, coeff_ref),
    ]
    copies = [
        pltpu.make_async_copy(source, target, sems.at[i])
        for i, (source, target) in enumerate(pairs)
    ]
    for copy in copies:
        copy.start()
    for copy in copies[:4]:
        copy.wait()
    slots = pad_ref.shape[0]
    width, points = table_ref.shape[1:]
    row = lax.broadcasted_iota(jnp.int32, (width, 128), 0)
    for s in range(slots):
        rows = slice(s * width, (s + 1) * width)
        live = jnp.where(row < width - pad_ref[s], 1.0, 0.0).astype(BF16)
        rolled = pltpu.roll(table_ref[level_ref[s]], shift_ref[s], 1)
        for p in range(0, points, 128):
            rolled_ref[rows, p : p + 128] = rolled[:, p : p + 128] * live
    copies[4].wait()
    turned_ref[...] = coeff_ref[...].T
    store_halves(chips, chunk_of(turned_ref, rolled_ref, wide, wide - 1), far_ref, near_ref)


def first(wide, chips, level, pad, shift, coeff, tables):
    rows, columns = coeff.shape
    points = tables.shape[2]
    slots = pad.shape[0]
    inputs = (level, pad, shift, coeff, tables)
    return call(
        functools.partial(first_kernel, wide, chips),
        "forward_first",
        (
            *halves(points // wide, columns),
            array((columns, rows), BF16),
            array((rows, points), BF16),
        ),
        [HBM] * 5,
        (VMEM,) * 4,
        [
            pltpu.SMEM((slots,), jnp.int32),
            pltpu.SMEM((slots,), jnp.int32),
            pltpu.SMEM((slots,), jnp.int32),
            pltpu.VMEM(coeff.shape, coeff.dtype),
            pltpu.VMEM(tables.shape, tables.dtype),
            pltpu.SemaphoreType.DMA((5,)),
        ],
        flops=2 * rows * points // wide * columns,
        moved=4 * MIB,
    )(*(in_hbm(value) for value in inputs))


def chunk_kernel(wide, chips, k, turned_ref, rolled_ref, far_ref, near_ref):
    store_halves(chips, chunk_of(turned_ref, rolled_ref, wide, k), far_ref, near_ref)


def chunk(wide, chips, k, turned, rolled):
    columns, rows = turned.shape
    own = rolled.shape[1] // wide
    return call(
        functools.partial(chunk_kernel, wide, chips, k),
        "forward_chunk",
        halves(own, columns),
        [VMEM] * 2,
        (VMEM,) * 2,
        flops=2 * rows * own * columns * LONG,
        moved=MIB * LONG,
    )(turned, rolled)


def last_kernel(
    wide,
    chips,
    turned_ref,
    rolled_ref,
    basis_hbm,
    potential_hbm,
    out_ref,
    basis_ref,
    potential_ref,
    sems,
):
    place = lax.axis_index("narrow")
    core, chip = place % 2, place // 2
    columns = turned_ref.shape[0]
    pairs = []
    for j in range(chips):
        start = pl.multiple_of(((chip ^ j) * 2 + core) * columns, columns)
        pairs.append((basis_hbm.at[pl.ds(start, columns), :], basis_ref.at[j]))
    pairs.append((potential_hbm, potential_ref))
    copies = [
        pltpu.make_async_copy(source, target, sems.at[i])
        for i, (source, target) in enumerate(pairs)
    ]
    for copy in copies:
        copy.start()
    out_ref[...] = chunk_of(turned_ref, rolled_ref, wide, 0).T
    for copy in copies:
        copy.wait()


def last(wide, chips, turned, rolled, basis, potential):
    columns, rows = turned.shape
    own = rolled.shape[1] // wide
    return call(
        functools.partial(last_kernel, wide, chips),
        "forward_own",
        (
            array((own, columns), F32),
            array((chips, columns, basis.shape[1]), BF16),
            array(potential.shape, F32),
        ),
        [VMEM, VMEM, HBM, HBM],
        (VMEM,) * 3,
        [pltpu.SemaphoreType.DMA((chips + 1,))],
        flops=2 * rows * own * columns,
        moved=10 * MIB,
    )(turned, rolled, in_hbm(basis), in_hbm(potential))


def combine_kernel(chips, first, mine_ref, *refs):
    count = chips // 2
    parts, outs = refs[:-count], refs[-count:]
    chip = lax.axis_index("narrow") // 2
    rows = outs[0].shape[0]
    for i in range(count):
        target = chip ^ (first + i)
        total = mine_ref[pl.ds(pl.multiple_of(target * rows, rows), rows), :]
        start = pl.multiple_of((target % count) * rows, rows)
        for part in parts:
            total = total + part[pl.ds(start, rows), :].astype(F32)
        outs[i][...] = total.astype(BF16)


def combine(chips, first, mine, parts):
    rows, columns = mine.shape
    count = chips // 2
    return call(
        functools.partial(combine_kernel, chips, first),
        "wide_sum",
        (array((rows // chips, columns), BF16),) * count,
        [VMEM] * (len(parts) + 1),
        (VMEM,) * count,
        moved=MIB,
    )(mine, *parts)


def own_points_kernel(x_ref, basis_ref, out_ref):
    out_ref[...] = dot(x_ref[...], basis_ref[0])


def own_points(x, basis):
    rows = x.shape[0]
    points = basis.shape[2]
    return call(
        own_points_kernel,
        "points_own",
        array((rows, points), F32),
        [VMEM] * 2,
        VMEM,
        flops=2 * rows * points * x.shape[1],
        moved=2 * MIB,
    )(x, basis)


def more_points_kernel(j, total_ref, x_ref, basis_ref, out_ref):
    out_ref[...] = total_ref[...] + dot(x_ref[...], basis_ref[j])


def more_points(j, total, x, basis):
    rows, points = total.shape
    return call(
        functools.partial(more_points_kernel, j),
        "points_more",
        array((rows, points), F32),
        [VMEM] * 3,
        VMEM,
        flops=2 * rows * points * x.shape[1],
        moved=2 * MIB,
    )(total, x, basis)


def last_points_kernel(j, total_ref, x_ref, basis_ref, mine_ref, theirs_ref):
    core = lax.axis_index("narrow") % 2
    rows = mine_ref.shape[0]
    total = total_ref[...] + dot(x_ref[...], basis_ref[j])
    low, high = total[:rows], total[rows:]
    mine_ref[...] = jnp.where(core == 0, low, high)
    theirs_ref[...] = jnp.where(core == 0, high, low)


def last_points(j, total, x, basis):
    rows, points = total.shape
    half = array((rows // 2, points), F32)
    return call(
        functools.partial(last_points_kernel, j),
        "points_last",
        (half, half),
        [VMEM] * 3,
        (VMEM, VMEM),
        flops=2 * rows * points * x.shape[1],
        moved=2 * MIB,
    )(total, x, basis)


def act_kernel(mine_ref, other_ref, potential_ref, out_ref):
    on_grid = mine_ref[...] + other_ref[...]
    out_ref[...] = (potential_ref[...] * on_grid).astype(BF16)


def act(mine, other, potential):
    return call(
        act_kernel, "act", array(mine.shape, BF16), [VMEM] * 3, VMEM, moved=MIB
    )(mine, other, potential)


def first_functions_kernel(j, mine_ref, other_ref, basis_ref, out_ref, both_ref):
    core = lax.axis_index("narrow") % 2
    rows = mine_ref.shape[0]
    mine, other = mine_ref[...].astype(F32), other_ref[...].astype(F32)
    both_ref[:rows] = jnp.where(core == 0, mine, other).astype(BF16)
    both_ref[rows:] = jnp.where(core == 0, other, mine).astype(BF16)
    out_ref[...] = dot_turned(both_ref[...], basis_ref[j]).astype(BF16)


def first_functions(j, mine, other, basis):
    rows, points = mine.shape
    columns = basis.shape[1]
    return call(
        functools.partial(first_functions_kernel, j),
        "functions_first",
        (array((2 * rows, columns), BF16), array((2 * rows, points), BF16)),
        [VMEM] * 3,
        (VMEM, VMEM),
        flops=4 * rows * points * columns,
        moved=2 * MIB,
    )(mine, other, basis)


def functions_kernel(j, both_ref, basis_ref, out_ref):
    out_ref[...] = dot_turned(both_ref[...], basis_ref[j]).astype(BF16)


def functions(j, both, basis):
    rows, points = both.shape
    columns = basis.shape[1]
    long = LONG if j else 1
    return call(
        functools.partial(functions_kernel, j),
        "functions_more",
        array((rows, columns), BF16),
        [VMEM] * 2,
        VMEM,
        flops=2 * rows * points * columns * long,
        moved=2 * MIB * long,
    )(both, basis)


def assemble_kernel(first, *refs):
    parts, out_ref = refs[:-1], refs[-1]
    chip = lax.axis_index("narrow") // 2
    rows = parts[0].shape[0]
    for i, part in enumerate(parts):
        place = (chip ^ (first + i)) % len(parts)
        out_ref[pl.ds(pl.multiple_of(place * rows, rows), rows), :] = part[...]


def assemble(first, parts):
    rows, columns = parts[0].shape
    count = len(parts)
    return call(
        functools.partial(assemble_kernel, first),
        "assemble",
        array((rows * count, columns), BF16),
        [VMEM] * count,
        VMEM,
        moved=MIB // 4,
    )(*parts)


def columns_of(chips, wide, k, far, half):
    upper = lax.axis_index("narrow") // 2 // (chips // 2)
    place = (lax.axis_index("wide") ^ k) * 2 + (upper ^ far)
    return pl.ds(pl.multiple_of(place * half, half), half)


def own_kernel(wide, chips, pad_ref, rolled_ref, near_ref, coeff_ref, row_ref, column_ref, out_ref):
    slots = pad_ref.shape[0]
    width = rolled_ref.shape[0] // slots
    half = near_ref.shape[0]
    mine = columns_of(chips, wide, 0, 0, half)
    row = lax.broadcasted_iota(jnp.int32, (width, out_ref.shape[1]), 0)

    def one(s, _):
        rows = pl.ds(pl.multiple_of(s * width, width), width)
        energy = row_ref[rows, :] + column_ref[...]
        diagonal = energy * coeff_ref[rows, :].astype(F32)
        diagonal = jnp.where(row < width - pad_ref[s], diagonal, 0.0)
        out_ref[rows, :] = diagonal + dot(rolled_ref[rows, mine], near_ref[...])
        return 0

    lax.fori_loop(0, slots, one, 0, unroll=4)


def backward_own(wide, chips, pad, rolled, near, coeff, row_energy, column_energy):
    smem = pl.BlockSpec(memory_space=pltpu.SMEM)
    rows, columns = coeff.shape
    return call(
        functools.partial(own_kernel, wide, chips),
        "backward_own",
        array(coeff.shape, F32),
        [smem] + [VMEM] * 5,
        VMEM,
        flops=2 * rows * columns * near.shape[0],
        moved=4 * MIB,
    )(pad, rolled, near, coeff, row_energy[:, None], column_energy[None, :])


def more_kernel(wide, chips, pieces, total_ref, rolled_ref, *refs):
    grids, out_ref = refs[:-1], refs[-1]
    half = grids[0].shape[0]
    steps = 4
    count = rolled_ref.shape[0] // steps

    def one(i, _):
        rows = pl.ds(pl.multiple_of(i * count, count), count)
        total = total_ref[rows, :]
        for (k, far), grid in zip(pieces, grids):
            place = columns_of(chips, wide, k, far, half)
            total = total + dot(rolled_ref[rows, place], grid[...])
        out_ref[rows, :] = total
        return 0

    lax.fori_loop(0, steps, one, 0)


def backward_more(wide, chips, pieces, total, rolled, grids):
    rows, columns = total.shape
    return call(
        functools.partial(more_kernel, wide, chips, pieces),
        "backward_more",
        array(total.shape, F32),
        [VMEM] * (2 + len(grids)),
        VMEM,
        flops=2 * rows * columns * grids[0].shape[0] * len(grids),
        moved=3 * MIB,
    )(total, rolled, *grids)


def end_kernel(wide, chips, k, far, total_ref, rolled_ref, grid_ref, out_hbm, out_ref, sems):
    place = columns_of(chips, wide, k, far, grid_ref.shape[0])
    steps = sems.shape[0]
    rows = rolled_ref.shape[0] // steps
    copies = []
    for i in range(steps):
        span = pl.ds(i * rows, rows)
        out_ref[span, :] = total_ref[span, :] + dot(rolled_ref[span, place], grid_ref[...])
        copies.append(pltpu.make_async_copy(out_ref.at[span, :], out_hbm.at[span, :], sems.at[i]))
        copies[-1].start()
    for copy in copies:
        copy.wait()


def backward_end(wide, chips, k, far, total, rolled, grid):
    rows, columns = total.shape
    return call(
        functools.partial(end_kernel, wide, chips, k, far),
        "backward_end",
        array(total.shape, F32),
        [VMEM] * 3,
        HBM,
        [pltpu.VMEM(total.shape, F32), pltpu.SemaphoreType.DMA((4,))],
        flops=2 * rows * columns * grid.shape[0],
        moved=4 * MIB,
    )(total, rolled, grid)


def exchange(value, step, size, axis):
    return lax.ppermute(value, axis, [(i, i ^ step) for i in range(size)])


def body(
    wide,
    narrow,
    coeff,
    groupb_row_energy,
    groupa_energy,
    groupb_basis_values,
    basis_a,
    potential,
    slot_sparse_level,
    block_pad,
    slot_grid_offset,
):
    chips = narrow // 2
    tables = jnp.swapaxes(groupb_basis_values, 1, 2)
    half = chips // 2
    order = [wide - 1] + list(range(1, wide - 1))
    far, near, turned, rolled = first(
        wide, chips, slot_sparse_level, block_pad, slot_grid_offset, coeff, tables
    )
    sent = {wide - 1: (far, near)}
    for k in order[1:]:
        sent[k] = chunk(wide, chips, k, turned, rolled)
    far_parts = [exchange(sent[k][0], k, wide, "wide") for k in order]
    near_parts = [exchange(sent[k][1], k, wide, "wide") for k in order]
    mine, basis, pot = last(wide, chips, turned, rolled, basis_a, potential)
    pieces = combine(chips, half, mine, far_parts)
    xs = {j: exchange(pieces[j - half], 2 * j, narrow, "narrow") for j in range(half, chips)}
    pieces = combine(chips, 0, mine, near_parts)
    for j in range(1, half):
        xs[j] = exchange(pieces[j], 2 * j, narrow, "narrow")
    total = own_points(pieces[0], basis)
    visits = list(range(half, chips)) + list(range(1, half))
    for j in visits[:-1]:
        total = more_points(j, total, xs[j], basis)
    mine, theirs = last_points(visits[-1], total, xs[visits[-1]], basis)
    acted = act(mine, exchange(theirs, 1, narrow, "narrow"), pot)
    other = exchange(acted, 1, narrow, "narrow")
    blocks = {}
    block, both = first_functions(1, acted, other, basis)
    blocks[1] = exchange(block, 2, narrow, "narrow")
    for j in range(2, chips):
        blocks[j] = exchange(functions(j, both, basis), 2 * j, narrow, "narrow")
    near = assemble(0, [functions(0, both, basis)] + [blocks[j] for j in range(1, half)])
    nears = [exchange(near, k, wide, "wide") for k in order]
    far = assemble(half, [blocks[j] for j in range(half, chips)])
    fars = [exchange(far, k, wide, "wide") for k in order]
    total = backward_own(
        wide, chips, block_pad, rolled, near, coeff, groupb_row_energy, groupa_energy
    )
    total = backward_more(
        wide, chips, [(0, 1)] + [(k, 0) for k in order], total, rolled, [far] + nears
    )
    total = backward_more(
        wide, chips, [(k, 1) for k in order[:-1]], total, rolled, fars[:-1]
    )
    return backward_end(wide, chips, order[-1], 1, total, rolled, fars[-1])


def solution(mesh):
    return jax.shard_map(
        functools.partial(body, mesh.shape["wide"], mesh.shape["narrow"]),
        mesh=mesh,
        in_specs=(
            P("wide", "narrow"),
            P("wide"),
            P("narrow"),
            P(),
            P(),
            P(("wide", "narrow"), None),
            P("wide"),
            P("wide"),
            P("wide"),
        ),
        out_specs=P("wide", "narrow"),
        check_vma=False,
    )
```

```python
import functools

import jax
import jax.numpy as jnp
from jax import lax
from jax.experimental import pallas as pl
from jax.experimental.pallas import tpu as pltpu
from jax.sharding import PartitionSpec as P

MIB = 1024 * 1024
HBM = pl.BlockSpec(memory_space=pltpu.HBM)
VMEM = pl.BlockSpec(memory_space=pltpu.VMEM)
BF16 = jnp.bfloat16
F32 = jnp.float32
LONG = 8


def call(kernel, name, out_shape, in_specs, out_specs, scratch=(), flops=0, moved=0, mib=16):
    return pl.pallas_call(
        kernel,
        out_shape=out_shape,
        in_specs=in_specs,
        out_specs=out_specs,
        scratch_shapes=scratch,
        compiler_params=pltpu.CompilerParams(vmem_limit_bytes=mib * MIB),
        cost_estimate=pl.CostEstimate(flops=flops, bytes_accessed=moved, transcendentals=0),
        name=name,
    )


def in_hbm(value):
    return pltpu.with_memory_space_constraint(value, pltpu.HBM)


def array(shape, dtype):
    return jax.ShapeDtypeStruct(shape, dtype)


def dot(left, right):
    return jnp.dot(left, right, preferred_element_type=F32)


def dot_turned(left, right):
    return lax.dot_general(left, right, (((1,), (1,)), ((), ())), preferred_element_type=F32)


def chunk_of(turned_ref, rolled_ref, wide, k):
    own = rolled_ref.shape[1] // wide
    start = pl.multiple_of((lax.axis_index("wide") ^ k) * own, own)
    return dot(turned_ref[...], rolled_ref[:, pl.ds(start, own)])


def store_halves(chips, total, far_ref, near_ref):
    upper = lax.axis_index("narrow") // 2 >= chips // 2
    rows = far_ref.shape[0]
    turned = total.astype(BF16).T.astype(F32)
    low, high = turned[:rows], turned[rows:]
    far_ref[...] = jnp.where(upper, low, high).astype(BF16)
    near_ref[...] = jnp.where(upper, high, low).astype(BF16)


def fetch_basis(basis_hbm, basis_ref, sems, first):
    count, columns, _ = basis_ref.shape
    place = lax.axis_index("narrow")
    core, chip = place % 2, place // 2
    copies = []
    for i in range(count):
        start = pl.multiple_of(((chip ^ (first + i)) * 2 + core) * columns, columns)
        copies.append(
            pltpu.make_async_copy(
                basis_hbm.at[pl.ds(start, columns), :], basis_ref.at[i], sems.at[i]
            )
        )
        copies[-1].start()
    return copies


def halves(rows, columns):
    return (array((rows // 2, columns), BF16),) * 2


def first_kernel(
    wide,
    chips,
    level_hbm,
    pad_hbm,
    shift_hbm,
    coeff_hbm,
    table_hbm,
    basis_hbm,
    far_ref,
    near_ref,
    turned_ref,
    rolled_ref,
    basis_ref,
    level_ref,
    pad_ref,
    shift_ref,
    coeff_ref,
    table_ref,
    sems,
    basis_sems,
):
    pairs = [
        (level_hbm, level_ref),
        (shift_hbm, shift_ref),
        (pad_hbm, pad_ref),
        (table_hbm, table_ref),
        (coeff_hbm, coeff_ref),
    ]
    copies = [
        pltpu.make_async_copy(source, target, sems.at[i])
        for i, (source, target) in enumerate(pairs)
    ]
    for copy in copies:
        copy.start()
    for copy in copies[:4]:
        copy.wait()
    fetches = fetch_basis(basis_hbm, basis_ref, basis_sems, 0)
    slots = pad_ref.shape[0]
    width, points = table_ref.shape[1:]
    row = lax.broadcasted_iota(jnp.int32, (width, 128), 0)
    for s in range(slots):
        rows = slice(s * width, (s + 1) * width)
        live = jnp.where(row < width - pad_ref[s], 1.0, 0.0).astype(BF16)
        rolled = pltpu.roll(table_ref[level_ref[s]], shift_ref[s], 1)
        for p in range(0, points, 128):
            rolled_ref[rows, p : p + 128] = rolled[:, p : p + 128] * live
    copies[4].wait()
    turned_ref[...] = coeff_ref[...].T
    store_halves(chips, chunk_of(turned_ref, rolled_ref, wide, wide - 1), far_ref, near_ref)
    for fetch in fetches:
        fetch.wait()


def first(wide, chips, level, pad, shift, coeff, tables, basis):
    rows, columns = coeff.shape
    points = tables.shape[2]
    slots = pad.shape[0]
    inputs = (level, pad, shift, coeff, tables, basis)
    return call(
        functools.partial(first_kernel, wide, chips),
        "forward_first",
        (
            *halves(points // wide, columns),
            array((columns, rows), BF16),
            array((rows, points), BF16),
            array((chips // 2, columns, basis.shape[1]), BF16),
        ),
        [HBM] * 6,
        (VMEM,) * 5,
        [
            pltpu.SMEM((slots,), jnp.int32),
            pltpu.SMEM((slots,), jnp.int32),
            pltpu.SMEM((slots,), jnp.int32),
            pltpu.VMEM(coeff.shape, coeff.dtype),
            pltpu.VMEM(tables.shape, tables.dtype),
            pltpu.SemaphoreType.DMA((5,)),
            pltpu.SemaphoreType.DMA((chips // 2,)),
        ],
        flops=2 * rows * points // wide * columns,
        moved=4 * MIB,
    )(*(in_hbm(value) for value in inputs))


def chunk_kernel(
    wide, chips, k, part, turned_ref, rolled_ref, basis_hbm, far_ref, near_ref, basis_ref, sems
):
    fetches = fetch_basis(basis_hbm, basis_ref, sems, part)
    store_halves(chips, chunk_of(turned_ref, rolled_ref, wide, k), far_ref, near_ref)
    for fetch in fetches:
        fetch.wait()


def chunk_only_kernel(wide, chips, k, turned_ref, rolled_ref, far_ref, near_ref):
    store_halves(chips, chunk_of(turned_ref, rolled_ref, wide, k), far_ref, near_ref)


def chunk(wide, chips, k, part, count, turned, rolled, basis):
    columns, rows = turned.shape
    own = rolled.shape[1] // wide
    cost = dict(flops=2 * rows * own * columns * LONG, moved=MIB * LONG)
    if not count:
        return call(
            functools.partial(chunk_only_kernel, wide, chips, k),
            "forward_chunk",
            halves(own, columns),
            [VMEM] * 2,
            (VMEM,) * 2,
            **cost,
        )(turned, rolled)
    return call(
        functools.partial(chunk_kernel, wide, chips, k, part),
        "forward_chunk",
        (*halves(own, columns), array((count, columns, basis.shape[1]), BF16)),
        [VMEM, VMEM, HBM],
        (VMEM,) * 3,
        [pltpu.SemaphoreType.DMA((count,))],
        **cost,
    )(turned, rolled, in_hbm(basis))


def last_kernel(wide, turned_ref, rolled_ref, potential_hbm, out_ref, potential_ref, sem):
    copy = pltpu.make_async_copy(potential_hbm, potential_ref, sem)
    copy.start()
    out_ref[...] = chunk_of(turned_ref, rolled_ref, wide, 0).T
    copy.wait()


def last(wide, turned, rolled, potential):
    columns, rows = turned.shape
    own = rolled.shape[1] // wide
    return call(
        functools.partial(last_kernel, wide),
        "forward_own",
        (array((own, columns), F32), array(potential.shape, F32)),
        [VMEM, VMEM, HBM],
        (VMEM,) * 2,
        [pltpu.SemaphoreType.DMA],
        flops=2 * rows * own * columns,
        moved=MIB,
    )(turned, rolled, in_hbm(potential))


def combine_kernel(chips, first, mine_ref, *refs):
    count = chips // 2
    parts, outs = refs[:-count], refs[-count:]
    chip = lax.axis_index("narrow") // 2
    rows = outs[0].shape[0]
    for i in range(count):
        target = chip ^ (first + i)
        total = mine_ref[pl.ds(pl.multiple_of(target * rows, rows), rows), :]
        start = pl.multiple_of((target % count) * rows, rows)
        for part in parts:
            total = total + part[pl.ds(start, rows), :].astype(F32)
        outs[i][...] = total.astype(BF16)


def combine(chips, first, mine, parts):
    rows, columns = mine.shape
    count = chips // 2
    return call(
        functools.partial(combine_kernel, chips, first),
        "wide_sum",
        (array((rows // chips, columns), BF16),) * count,
        [VMEM] * (len(parts) + 1),
        (VMEM,) * count,
        moved=MIB,
    )(mine, *parts)


def own_points_kernel(x_ref, basis_ref, out_ref):
    out_ref[...] = dot(x_ref[...], basis_ref[0])


def own_points(x, where):
    basis, _ = where
    rows = x.shape[0]
    points = basis.shape[2]
    return call(
        own_points_kernel,
        "points_own",
        array((rows, points), F32),
        [VMEM] * 2,
        VMEM,
        flops=2 * rows * points * x.shape[1],
        moved=2 * MIB,
    )(x, basis)


def more_points_kernel(j, total_ref, x_ref, basis_ref, out_ref):
    out_ref[...] = total_ref[...] + dot(x_ref[...], basis_ref[j])


def more_points(total, x, where):
    basis, j = where
    rows, points = total.shape
    return call(
        functools.partial(more_points_kernel, j),
        "points_more",
        array((rows, points), F32),
        [VMEM] * 3,
        VMEM,
        flops=2 * rows * points * x.shape[1],
        moved=2 * MIB,
    )(total, x, basis)


def last_points_kernel(j, total_ref, x_ref, basis_ref, mine_ref, theirs_ref):
    core = lax.axis_index("narrow") % 2
    rows = mine_ref.shape[0]
    total = total_ref[...] + dot(x_ref[...], basis_ref[j])
    low, high = total[:rows], total[rows:]
    mine_ref[...] = jnp.where(core == 0, low, high)
    theirs_ref[...] = jnp.where(core == 0, high, low)


def last_points(total, x, where):
    basis, j = where
    rows, points = total.shape
    half = array((rows // 2, points), F32)
    return call(
        functools.partial(last_points_kernel, j),
        "points_last",
        (half, half),
        [VMEM] * 3,
        (VMEM, VMEM),
        flops=2 * rows * points * x.shape[1],
        moved=2 * MIB,
    )(total, x, basis)


def act_kernel(mine_ref, other_ref, potential_ref, out_ref):
    on_grid = mine_ref[...] + other_ref[...]
    out_ref[...] = (potential_ref[...] * on_grid).astype(BF16)


def act(mine, other, potential):
    return call(
        act_kernel, "act", array(mine.shape, BF16), [VMEM] * 3, VMEM, moved=MIB
    )(mine, other, potential)


def first_functions_kernel(j, mine_ref, other_ref, basis_ref, out_ref, both_ref):
    core = lax.axis_index("narrow") % 2
    rows = mine_ref.shape[0]
    mine, other = mine_ref[...].astype(F32), other_ref[...].astype(F32)
    both_ref[:rows] = jnp.where(core == 0, mine, other).astype(BF16)
    both_ref[rows:] = jnp.where(core == 0, other, mine).astype(BF16)
    out_ref[...] = dot_turned(both_ref[...], basis_ref[j]).astype(BF16)


def first_functions(mine, other, where):
    basis, j = where
    rows, points = mine.shape
    columns = basis.shape[1]
    return call(
        functools.partial(first_functions_kernel, j),
        "functions_first",
        (array((2 * rows, columns), BF16), array((2 * rows, points), BF16)),
        [VMEM] * 3,
        (VMEM, VMEM),
        flops=4 * rows * points * columns,
        moved=2 * MIB,
    )(mine, other, basis)


def functions_kernel(j, both_ref, basis_ref, out_ref):
    out_ref[...] = dot_turned(both_ref[...], basis_ref[j]).astype(BF16)


def functions(both, where):
    basis, j = where
    rows, points = both.shape
    columns = basis.shape[1]
    return call(
        functools.partial(functions_kernel, j),
        "functions_more",
        array((rows, columns), BF16),
        [VMEM] * 2,
        VMEM,
        flops=2 * rows * points * columns,
        moved=2 * MIB,
    )(both, basis)


def assemble_kernel(*refs):
    parts, out_ref = refs[:-1], refs[-1]
    chip = lax.axis_index("narrow") // 2
    rows = parts[0].shape[0]
    for j, part in enumerate(parts):
        start = pl.multiple_of((chip ^ j) * rows, rows)
        out_ref[pl.ds(start, rows), :] = part[...]


def assemble(parts):
    rows, columns = parts[0].shape
    chips = len(parts)
    return call(
        assemble_kernel,
        "assemble",
        array((rows * chips, columns), BF16),
        [VMEM] * chips,
        VMEM,
        moved=MIB // 4,
    )(*parts)


def own_kernel(wide, pad_ref, rolled_ref, grid_ref, coeff_ref, row_ref, column_ref, out_ref):
    slots = pad_ref.shape[0]
    width = rolled_ref.shape[0] // slots
    me = lax.axis_index("wide")
    own = rolled_ref.shape[1] // wide
    start = pl.multiple_of(me * own, own)
    out_ref[...] = dot(rolled_ref[:, pl.ds(start, own)], grid_ref[...])
    row = lax.broadcasted_iota(jnp.int32, (width, out_ref.shape[1]), 0)
    for s in range(slots):
        rows = slice(s * width, (s + 1) * width)
        energy = row_ref[rows, :] + column_ref[...]
        diagonal = energy * coeff_ref[rows, :].astype(F32)
        out_ref[rows, :] += jnp.where(row < width - pad_ref[s], diagonal, 0.0)


def backward_own(wide, pad, rolled, grid, coeff, row_energy, column_energy):
    smem = pl.BlockSpec(memory_space=pltpu.SMEM)
    rows, columns = coeff.shape
    return call(
        functools.partial(own_kernel, wide),
        "backward_own",
        array(coeff.shape, F32),
        [smem] + [VMEM] * 5,
        VMEM,
        flops=2 * rows * columns * rolled.shape[1] // wide,
        moved=4 * MIB,
    )(pad, rolled, grid, coeff, row_energy[:, None], column_energy[None, :])


def more_kernel(wide, k, total_ref, rolled_ref, grid_ref, out_ref):
    own = rolled_ref.shape[1] // wide
    start = pl.multiple_of((lax.axis_index("wide") ^ k) * own, own)
    out_ref[...] = total_ref[...] + dot(rolled_ref[:, pl.ds(start, own)], grid_ref[...])


def backward_more(wide, k, total, rolled, grid):
    rows, columns = total.shape
    return call(
        functools.partial(more_kernel, wide, k),
        "backward_more",
        array(total.shape, F32),
        [VMEM] * 3,
        VMEM,
        flops=2 * rows * columns * rolled.shape[1] // wide,
        moved=3 * MIB,
    )(total, rolled, grid)


def end_kernel(wide, k, total_ref, rolled_ref, grid_ref, out_hbm, out_ref, sems):
    own = rolled_ref.shape[1] // wide
    start = pl.multiple_of((lax.axis_index("wide") ^ k) * own, own)
    steps = sems.shape[0]
    rows = rolled_ref.shape[0] // steps
    copies = []
    for i in range(steps):
        span = pl.ds(i * rows, rows)
        part = dot(rolled_ref[span, pl.ds(start, own)], grid_ref[...])
        out_ref[span, :] = total_ref[span, :] + part
        copies.append(pltpu.make_async_copy(out_ref.at[span, :], out_hbm.at[span, :], sems.at[i]))
        copies[-1].start()
    for copy in copies:
        copy.wait()


def backward_end(wide, k, total, rolled, grid):
    rows, columns = total.shape
    return call(
        functools.partial(end_kernel, wide, k),
        "backward_end",
        array(total.shape, F32),
        [VMEM] * 3,
        HBM,
        [pltpu.VMEM(total.shape, F32), pltpu.SemaphoreType.DMA((8,))],
        flops=2 * rows * columns * rolled.shape[1] // wide,
        moved=4 * MIB,
    )(total, rolled, grid)


def exchange(value, step, size, axis):
    return lax.ppermute(value, axis, [(i, i ^ step) for i in range(size)])


def body(
    wide,
    narrow,
    coeff,
    groupb_row_energy,
    groupa_energy,
    groupb_basis_values,
    basis_a,
    potential,
    slot_sparse_level,
    block_pad,
    slot_grid_offset,
):
    chips = narrow // 2
    tables = jnp.swapaxes(groupb_basis_values, 1, 2)
    half = chips // 2
    order = [wide - 1] + list(range(1, wide - 1))
    far, near, turned, rolled, basis = first(
        wide, chips, slot_sparse_level, block_pad, slot_grid_offset, coeff, tables, basis_a
    )
    where = {j: (basis, j) for j in range(half)}
    sent = {wide - 1: (far, near)}
    taken = half
    for n, k in enumerate(order[1:]):
        count = max(0, min(chips - taken, -(-(chips - taken) // (len(order) - 1 - n))))
        far, near, *more = chunk(wide, chips, k, taken, count, turned, rolled, basis_a)
        sent[k] = far, near
        for i in range(count):
            where[taken + i] = more[0], i
        taken += count
    far_parts = [exchange(sent[k][0], k, wide, "wide") for k in order]
    near_parts = [exchange(sent[k][1], k, wide, "wide") for k in order]
    mine, pot = last(wide, turned, rolled, potential)
    pieces = combine(chips, half, mine, far_parts)
    xs = {j: exchange(pieces[j - half], 2 * j, narrow, "narrow") for j in range(half, chips)}
    pieces = combine(chips, 0, mine, near_parts)
    for j in range(1, half):
        xs[j] = exchange(pieces[j], 2 * j, narrow, "narrow")
    total = own_points(pieces[0], where[0])
    visits = list(range(half, chips)) + list(range(1, half))
    for j in visits[:-1]:
        total = more_points(total, xs[j], where[j])
    mine, theirs = last_points(total, xs[visits[-1]], where[visits[-1]])
    acted = act(mine, exchange(theirs, 1, narrow, "narrow"), pot)
    other = exchange(acted, 1, narrow, "narrow")
    block, both = first_functions(acted, other, where[chips - 1])
    blocks = {chips - 1: exchange(block, 2 * (chips - 1), narrow, "narrow")}
    for j in reversed(range(1, chips - 1)):
        blocks[j] = exchange(functions(both, where[j]), 2 * j, narrow, "narrow")
    grid = assemble([functions(both, where[0])] + [blocks[j] for j in range(1, chips)])
    grids = [exchange(grid, k, wide, "wide") for k in range(1, wide)]
    total = backward_own(
        wide, block_pad, rolled, grid, coeff, groupb_row_energy, groupa_energy
    )
    for k in range(1, wide - 1):
        total = backward_more(wide, k, total, rolled, grids[k - 1])
    return backward_end(wide, wide - 1, total, rolled, grids[-1])


def solution(mesh):
    return jax.shard_map(
        functools.partial(body, mesh.shape["wide"], mesh.shape["narrow"]),
        mesh=mesh,
        in_specs=(
            P("wide", "narrow"),
            P("wide"),
            P("narrow"),
            P(),
            P(),
            P(("wide", "narrow"), None),
            P("wide"),
            P("wide"),
            P("wide"),
        ),
        out_specs=P("wide", "narrow"),
        check_vma=False,
    )
```

```python
import functools

import jax
import jax.numpy as jnp
from jax import lax
from jax.experimental import pallas as pl
from jax.experimental.pallas import tpu as pltpu
from jax.sharding import PartitionSpec as P

MIB = 1024 * 1024
HBM = pl.BlockSpec(memory_space=pltpu.HBM)
VMEM = pl.BlockSpec(memory_space=pltpu.VMEM)
BF16 = jnp.bfloat16
F32 = jnp.float32
LONG = 8


def call(kernel, name, out_shape, in_specs, out_specs, scratch=(), flops=0, moved=0, mib=16):
    return pl.pallas_call(
        kernel,
        out_shape=out_shape,
        in_specs=in_specs,
        out_specs=out_specs,
        scratch_shapes=scratch,
        compiler_params=pltpu.CompilerParams(vmem_limit_bytes=mib * MIB),
        cost_estimate=pl.CostEstimate(flops=flops, bytes_accessed=moved, transcendentals=0),
        name=name,
    )


def in_hbm(value):
    return pltpu.with_memory_space_constraint(value, pltpu.HBM)


def array(shape, dtype):
    return jax.ShapeDtypeStruct(shape, dtype)


def dot(left, right):
    return jnp.dot(left, right, preferred_element_type=F32)


def dot_turned(left, right):
    return lax.dot_general(left, right, (((1,), (1,)), ((), ())), preferred_element_type=F32)


def chunk_of(turned_ref, rolled_ref, wide, k):
    own = rolled_ref.shape[1] // wide
    start = pl.multiple_of((lax.axis_index("wide") ^ k) * own, own)
    return dot(turned_ref[...], rolled_ref[:, pl.ds(start, own)])


def store_halves(chips, total, far_ref, near_ref):
    upper = lax.axis_index("narrow") // 2 >= chips // 2
    rows = far_ref.shape[0]
    turned = total.astype(BF16).T.astype(F32)
    low, high = turned[:rows], turned[rows:]
    far_ref[...] = jnp.where(upper, low, high).astype(BF16)
    near_ref[...] = jnp.where(upper, high, low).astype(BF16)


def start_pieces(source, target, rows, sem):
    for r in range(0, source.shape[0], rows):
        span = pl.ds(r, rows)
        pltpu.make_async_copy(source.at[span], target.at[span], sem).start()


def wait_all(source, target, sem):
    pltpu.make_async_copy(source, target, sem).wait()


def basis_pieces(basis_hbm, basis_ref):
    chips, columns, _ = basis_ref.shape
    place = lax.axis_index("narrow")
    core, chip = place % 2, place // 2
    pairs = []
    for j in range(chips):
        start = pl.multiple_of(((chip ^ j) * 2 + core) * columns, columns)
        pairs.append((basis_hbm.at[pl.ds(start, columns)], basis_ref.at[j]))
    return pairs


def halves(rows, columns):
    return (array((rows // 2, columns), BF16),) * 2


def first_kernel(
    wide,
    chips,
    level_hbm,
    pad_hbm,
    shift_hbm,
    coeff_hbm,
    table_hbm,
    basis_hbm,
    potential_hbm,
    far_ref,
    near_ref,
    turned_ref,
    rolled_ref,
    basis_ref,
    potential_ref,
    level_ref,
    pad_ref,
    shift_ref,
    coeff_ref,
    table_ref,
    sems,
):
    slots = pad_ref.shape[0]
    levels, width, points = table_ref.shape
    small = [
        pltpu.make_async_copy(source, target, sems.at[i])
        for i, (source, target) in enumerate(
            ((level_hbm, level_ref), (shift_hbm, shift_ref), (pad_hbm, pad_ref))
        )
    ]
    for copy in small:
        copy.start()
    for n in range(levels):
        start_pieces(table_hbm.at[n], table_ref.at[n], 32, sems.at[3])
    start_pieces(coeff_hbm, coeff_ref, 128, sems.at[4])
    pairs = basis_pieces(basis_hbm, basis_ref)
    for j, (source, target) in enumerate(pairs):
        start_pieces(source, target, 64, sems.at[6 + j])
    start_pieces(potential_hbm, potential_ref, 8, sems.at[5])
    for copy in small:
        copy.wait()
    wait_all(table_hbm, table_ref, sems.at[3])
    row = lax.broadcasted_iota(jnp.int32, (width, 128), 0)
    for s in range(slots):
        rows = slice(s * width, (s + 1) * width)
        live = jnp.where(row < width - pad_ref[s], 1.0, 0.0).astype(BF16)
        rolled = pltpu.roll(table_ref[level_ref[s]], shift_ref[s], 1)
        for p in range(0, points, 128):
            rolled_ref[rows, p : p + 128] = rolled[:, p : p + 128] * live
    wait_all(coeff_hbm, coeff_ref, sems.at[4])
    turned_ref[...] = coeff_ref[...].T
    store_halves(chips, chunk_of(turned_ref, rolled_ref, wide, wide - 1), far_ref, near_ref)
    for j, (source, target) in enumerate(pairs):
        wait_all(source, target, sems.at[6 + j])
    wait_all(potential_hbm, potential_ref, sems.at[5])


def first(wide, chips, level, pad, shift, coeff, tables, basis, potential):
    rows, columns = coeff.shape
    points = tables.shape[2]
    slots = pad.shape[0]
    inputs = (level, pad, shift, coeff, tables, basis, potential)
    return call(
        functools.partial(first_kernel, wide, chips),
        "forward_first",
        (
            *halves(points // wide, columns),
            array((columns, rows), BF16),
            array((rows, points), BF16),
            array((chips, columns, basis.shape[1]), BF16),
            array(potential.shape, F32),
        ),
        [HBM] * 7,
        (VMEM,) * 6,
        [
            pltpu.SMEM((slots,), jnp.int32),
            pltpu.SMEM((slots,), jnp.int32),
            pltpu.SMEM((slots,), jnp.int32),
            pltpu.VMEM(coeff.shape, coeff.dtype),
            pltpu.VMEM(tables.shape, tables.dtype),
            pltpu.SemaphoreType.DMA((6 + chips,)),
        ],
        flops=2 * rows * points // wide * columns,
        moved=4 * MIB,
    )(*(in_hbm(value) for value in inputs))


def chunk_kernel(wide, chips, k, turned_ref, rolled_ref, far_ref, near_ref):
    store_halves(chips, chunk_of(turned_ref, rolled_ref, wide, k), far_ref, near_ref)


def chunk(wide, chips, k, turned, rolled):
    columns, rows = turned.shape
    own = rolled.shape[1] // wide
    return call(
        functools.partial(chunk_kernel, wide, chips, k),
        "forward_chunk",
        halves(own, columns),
        [VMEM] * 2,
        (VMEM,) * 2,
        flops=2 * rows * own * columns * LONG,
        moved=MIB * LONG,
    )(turned, rolled)


def last_kernel(wide, turned_ref, rolled_ref, out_ref):
    out_ref[...] = chunk_of(turned_ref, rolled_ref, wide, 0).T


def last(wide, turned, rolled):
    columns, rows = turned.shape
    own = rolled.shape[1] // wide
    return call(
        functools.partial(last_kernel, wide),
        "forward_own",
        array((own, columns), F32),
        [VMEM] * 2,
        VMEM,
        flops=2 * rows * own * columns,
        moved=MIB,
    )(turned, rolled)


def combine_kernel(chips, first, mine_ref, *refs):
    count = chips // 2
    parts, outs = refs[:-count], refs[-count:]
    chip = lax.axis_index("narrow") // 2
    rows = outs[0].shape[0]
    for i in range(count):
        target = chip ^ (first + i)
        total = mine_ref[pl.ds(pl.multiple_of(target * rows, rows), rows), :]
        start = pl.multiple_of((target % count) * rows, rows)
        for part in parts:
            total = total + part[pl.ds(start, rows), :].astype(F32)
        outs[i][...] = total.astype(BF16)


def combine(chips, first, mine, parts):
    rows, columns = mine.shape
    count = chips // 2
    return call(
        functools.partial(combine_kernel, chips, first),
        "wide_sum",
        (array((rows // chips, columns), BF16),) * count,
        [VMEM] * (len(parts) + 1),
        (VMEM,) * count,
        moved=MIB,
    )(mine, *parts)


def own_points_kernel(x_ref, basis_ref, out_ref):
    out_ref[...] = dot(x_ref[...], basis_ref[0])


def own_points(x, where):
    basis, _ = where
    rows = x.shape[0]
    points = basis.shape[2]
    return call(
        own_points_kernel,
        "points_own",
        array((rows, points), F32),
        [VMEM] * 2,
        VMEM,
        flops=2 * rows * points * x.shape[1],
        moved=2 * MIB,
    )(x, basis)


def more_points_kernel(j, total_ref, x_ref, basis_ref, out_ref):
    out_ref[...] = total_ref[...] + dot(x_ref[...], basis_ref[j])


def more_points(total, x, where):
    basis, j = where
    rows, points = total.shape
    return call(
        functools.partial(more_points_kernel, j),
        "points_more",
        array((rows, points), F32),
        [VMEM] * 3,
        VMEM,
        flops=2 * rows * points * x.shape[1],
        moved=2 * MIB,
    )(total, x, basis)


def last_points_kernel(j, total_ref, x_ref, basis_ref, mine_ref, theirs_ref):
    core = lax.axis_index("narrow") % 2
    rows = mine_ref.shape[0]
    total = total_ref[...] + dot(x_ref[...], basis_ref[j])
    low, high = total[:rows], total[rows:]
    mine_ref[...] = jnp.where(core == 0, low, high)
    theirs_ref[...] = jnp.where(core == 0, high, low)


def last_points(total, x, where):
    basis, j = where
    rows, points = total.shape
    half = array((rows // 2, points), F32)
    return call(
        functools.partial(last_points_kernel, j),
        "points_last",
        (half, half),
        [VMEM] * 3,
        (VMEM, VMEM),
        flops=2 * rows * points * x.shape[1],
        moved=2 * MIB,
    )(total, x, basis)


def act_kernel(mine_ref, other_ref, potential_ref, out_ref):
    on_grid = mine_ref[...] + other_ref[...]
    out_ref[...] = (potential_ref[...] * on_grid).astype(BF16)


def act(mine, other, potential):
    return call(
        act_kernel, "act", array(mine.shape, BF16), [VMEM] * 3, VMEM, moved=MIB
    )(mine, other, potential)


def first_functions_kernel(j, mine_ref, other_ref, basis_ref, out_ref, both_ref):
    core = lax.axis_index("narrow") % 2
    rows = mine_ref.shape[0]
    mine, other = mine_ref[...].astype(F32), other_ref[...].astype(F32)
    both_ref[:rows] = jnp.where(core == 0, mine, other).astype(BF16)
    both_ref[rows:] = jnp.where(core == 0, other, mine).astype(BF16)
    out_ref[...] = dot_turned(both_ref[...], basis_ref[j]).astype(BF16)


def first_functions(mine, other, where):
    basis, j = where
    rows, points = mine.shape
    columns = basis.shape[1]
    return call(
        functools.partial(first_functions_kernel, j),
        "functions_first",
        (array((2 * rows, columns), BF16), array((2 * rows, points), BF16)),
        [VMEM] * 3,
        (VMEM, VMEM),
        flops=4 * rows * points * columns,
        moved=2 * MIB,
    )(mine, other, basis)


def functions_kernel(j, both_ref, basis_ref, out_ref):
    out_ref[...] = dot_turned(both_ref[...], basis_ref[j]).astype(BF16)


def functions(both, where):
    basis, j = where
    rows, points = both.shape
    columns = basis.shape[1]
    return call(
        functools.partial(functions_kernel, j),
        "functions_more",
        array((rows, columns), BF16),
        [VMEM] * 2,
        VMEM,
        flops=2 * rows * points * columns,
        moved=2 * MIB,
    )(both, basis)


def assemble_kernel(*refs):
    parts, out_ref = refs[:-1], refs[-1]
    chip = lax.axis_index("narrow") // 2
    rows = parts[0].shape[0]
    for j, part in enumerate(parts):
        start = pl.multiple_of((chip ^ j) * rows, rows)
        out_ref[pl.ds(start, rows), :] = part[...]


def assemble(parts):
    rows, columns = parts[0].shape
    chips = len(parts)
    return call(
        assemble_kernel,
        "assemble",
        array((rows * chips, columns), BF16),
        [VMEM] * chips,
        VMEM,
        moved=MIB // 4,
    )(*parts)


def own_kernel(wide, pad_ref, rolled_ref, grid_ref, coeff_ref, row_ref, column_ref, out_ref):
    slots = pad_ref.shape[0]
    width = rolled_ref.shape[0] // slots
    me = lax.axis_index("wide")
    own = rolled_ref.shape[1] // wide
    start = pl.multiple_of(me * own, own)
    out_ref[...] = dot(rolled_ref[:, pl.ds(start, own)], grid_ref[...])
    row = lax.broadcasted_iota(jnp.int32, (width, out_ref.shape[1]), 0)
    for s in range(slots):
        rows = slice(s * width, (s + 1) * width)
        energy = row_ref[rows, :] + column_ref[...]
        diagonal = energy * coeff_ref[rows, :].astype(F32)
        out_ref[rows, :] += jnp.where(row < width - pad_ref[s], diagonal, 0.0)


def backward_own(wide, pad, rolled, grid, coeff, row_energy, column_energy):
    smem = pl.BlockSpec(memory_space=pltpu.SMEM)
    rows, columns = coeff.shape
    return call(
        functools.partial(own_kernel, wide),
        "backward_own",
        array(coeff.shape, F32),
        [smem] + [VMEM] * 5,
        VMEM,
        flops=2 * rows * columns * rolled.shape[1] // wide,
        moved=4 * MIB,
    )(pad, rolled, grid, coeff, row_energy[:, None], column_energy[None, :])


def more_kernel(wide, k, total_ref, rolled_ref, grid_ref, out_ref):
    own = rolled_ref.shape[1] // wide
    start = pl.multiple_of((lax.axis_index("wide") ^ k) * own, own)
    out_ref[...] = total_ref[...] + dot(rolled_ref[:, pl.ds(start, own)], grid_ref[...])


def backward_more(wide, k, total, rolled, grid):
    rows, columns = total.shape
    return call(
        functools.partial(more_kernel, wide, k),
        "backward_more",
        array(total.shape, F32),
        [VMEM] * 3,
        VMEM,
        flops=2 * rows * columns * rolled.shape[1] // wide,
        moved=3 * MIB,
    )(total, rolled, grid)


def end_kernel(wide, k, total_ref, rolled_ref, grid_ref, out_hbm, out_ref, sems):
    own = rolled_ref.shape[1] // wide
    start = pl.multiple_of((lax.axis_index("wide") ^ k) * own, own)
    steps = sems.shape[0]
    rows = rolled_ref.shape[0] // steps
    copies = []
    for i in range(steps):
        span = pl.ds(i * rows, rows)
        part = dot(rolled_ref[span, pl.ds(start, own)], grid_ref[...])
        out_ref[span, :] = total_ref[span, :] + part
        copies.append(pltpu.make_async_copy(out_ref.at[span, :], out_hbm.at[span, :], sems.at[i]))
        copies[-1].start()
    for copy in copies:
        copy.wait()


def backward_end(wide, k, total, rolled, grid):
    rows, columns = total.shape
    return call(
        functools.partial(end_kernel, wide, k),
        "backward_end",
        array(total.shape, F32),
        [VMEM] * 3,
        HBM,
        [pltpu.VMEM(total.shape, F32), pltpu.SemaphoreType.DMA((16,))],
        flops=2 * rows * columns * rolled.shape[1] // wide,
        moved=4 * MIB,
    )(total, rolled, grid)


def exchange(value, step, size, axis):
    return lax.ppermute(value, axis, [(i, i ^ step) for i in range(size)])


def body(
    wide,
    narrow,
    coeff,
    groupb_row_energy,
    groupa_energy,
    groupb_basis_values,
    basis_a,
    potential,
    slot_sparse_level,
    block_pad,
    slot_grid_offset,
):
    chips = narrow // 2
    tables = jnp.swapaxes(groupb_basis_values, 1, 2)
    half = chips // 2
    order = [wide - 1] + list(range(1, wide - 1))
    far, near, turned, rolled, basis, pot = first(
        wide,
        chips,
        slot_sparse_level,
        block_pad,
        slot_grid_offset,
        coeff,
        tables,
        basis_a,
        potential,
    )
    where = {j: (basis, j) for j in range(chips)}
    sent = {wide - 1: (far, near)}
    for k in order[1:]:
        sent[k] = chunk(wide, chips, k, turned, rolled)
    far_parts = [exchange(sent[k][0], k, wide, "wide") for k in order]
    near_parts = [exchange(sent[k][1], k, wide, "wide") for k in order]
    mine = last(wide, turned, rolled)
    pieces = combine(chips, half, mine, far_parts)
    xs = {j: exchange(pieces[j - half], 2 * j, narrow, "narrow") for j in range(half, chips)}
    pieces = combine(chips, 0, mine, near_parts)
    for j in range(1, half):
        xs[j] = exchange(pieces[j], 2 * j, narrow, "narrow")
    total = own_points(pieces[0], where[0])
    visits = list(range(half, chips)) + list(range(1, half))
    for j in visits[:-1]:
        total = more_points(total, xs[j], where[j])
    mine, theirs = last_points(total, xs[visits[-1]], where[visits[-1]])
    acted = act(mine, exchange(theirs, 1, narrow, "narrow"), pot)
    other = exchange(acted, 1, narrow, "narrow")
    block, both = first_functions(acted, other, where[chips - 1])
    blocks = {chips - 1: exchange(block, 2 * (chips - 1), narrow, "narrow")}
    for j in reversed(range(1, chips - 1)):
        blocks[j] = exchange(functions(both, where[j]), 2 * j, narrow, "narrow")
    grid = assemble([functions(both, where[0])] + [blocks[j] for j in range(1, chips)])
    grids = [exchange(grid, k, wide, "wide") for k in range(1, wide)]
    total = backward_own(
        wide, block_pad, rolled, grid, coeff, groupb_row_energy, groupa_energy
    )
    for k in range(1, wide - 1):
        total = backward_more(wide, k, total, rolled, grids[k - 1])
    return backward_end(wide, wide - 1, total, rolled, grids[-1])


def solution(mesh):
    return jax.shard_map(
        functools.partial(body, mesh.shape["wide"], mesh.shape["narrow"]),
        mesh=mesh,
        in_specs=(
            P("wide", "narrow"),
            P("wide"),
            P("narrow"),
            P(),
            P(),
            P(("wide", "narrow"), None),
            P("wide"),
            P("wide"),
            P("wide"),
        ),
        out_specs=P("wide", "narrow"),
        check_vma=False,
    )
```

```python
import functools

import jax
import jax.numpy as jnp
from jax import lax
from jax.experimental import pallas as pl
from jax.experimental.pallas import tpu as pltpu
from jax.sharding import PartitionSpec as P

MIB = 1024 * 1024
HBM = pl.BlockSpec(memory_space=pltpu.HBM)
VMEM = pl.BlockSpec(memory_space=pltpu.VMEM)
BF16 = jnp.bfloat16
F32 = jnp.float32


def call(kernel, name, out_shape, in_specs, out_specs, scratch=(), flops=0, moved=0, mib=16):
    return pl.pallas_call(
        kernel,
        out_shape=out_shape,
        in_specs=in_specs,
        out_specs=out_specs,
        scratch_shapes=scratch,
        compiler_params=pltpu.CompilerParams(vmem_limit_bytes=mib * MIB),
        cost_estimate=pl.CostEstimate(flops=flops, bytes_accessed=moved, transcendentals=0),
        name=name,
    )


def in_hbm(value):
    return pltpu.with_memory_space_constraint(value, pltpu.HBM)


def array(shape, dtype):
    return jax.ShapeDtypeStruct(shape, dtype)


def dot(left, right):
    return jnp.dot(left, right, preferred_element_type=F32)


def dot_turned(left, right):
    return lax.dot_general(left, right, (((1,), (1,)), ((), ())), preferred_element_type=F32)


def chunks_of(chips, turned_ref, rolled_ref, wide, targets, far):
    half = rolled_ref.shape[1] // wide // 2
    upper = lax.axis_index("narrow") // 2 // (chips // 2)
    me = lax.axis_index("wide")
    parts = []
    for k in targets:
        start = pl.multiple_of(((me ^ k) * 2 + (upper ^ far)) * half, half)
        parts.append(rolled_ref[:, pl.ds(start, half)])
    return dot(turned_ref[...], jnp.concatenate(parts, axis=1))


def start_pieces(source, target, rows, sem):
    for r in range(0, source.shape[0], rows):
        span = pl.ds(r, rows)
        pltpu.make_async_copy(source.at[span], target.at[span], sem).start()


def wait_all(source, target, sem):
    pltpu.make_async_copy(source, target, sem).wait()


def basis_pieces(basis_hbm, basis_ref):
    chips, columns, _ = basis_ref.shape
    place = lax.axis_index("narrow")
    core, chip = place % 2, place // 2
    pairs = []
    for j in range(chips):
        start = pl.multiple_of(((chip ^ j) * 2 + core) * columns, columns)
        pairs.append((basis_hbm.at[pl.ds(start, columns)], basis_ref.at[j]))
    return pairs


def first_kernel(
    wide,
    chips,
    messages,
    level_hbm,
    pad_hbm,
    shift_hbm,
    coeff_hbm,
    table_hbm,
    *refs,
):
    outs = refs[: len(messages)]
    turned_ref, rolled_ref = refs[len(messages) : len(messages) + 2]
    level_ref, pad_ref, shift_ref, coeff_ref, table_ref, sems = refs[len(messages) + 2 :]
    slots = pad_ref.shape[0]
    levels, width, points = table_ref.shape
    small = [
        pltpu.make_async_copy(source, target, sems.at[i])
        for i, (source, target) in enumerate(
            ((level_hbm, level_ref), (shift_hbm, shift_ref), (pad_hbm, pad_ref))
        )
    ]
    for copy in small:
        copy.start()
    for n in range(levels):
        start_pieces(table_hbm.at[n], table_ref.at[n], 32, sems.at[3])
    start_pieces(coeff_hbm, coeff_ref, 128, sems.at[4])
    for copy in small:
        copy.wait()
    wait_all(table_hbm, table_ref, sems.at[3])
    row = lax.broadcasted_iota(jnp.int32, (width, 128), 0)
    for s in range(slots):
        rows = slice(s * width, (s + 1) * width)
        live = jnp.where(row < width - pad_ref[s], 1.0, 0.0).astype(BF16)
        rolled = pltpu.roll(table_ref[level_ref[s]], shift_ref[s], 1)
        for p in range(0, points, 128):
            rolled_ref[rows, p : p + 128] = rolled[:, p : p + 128] * live
    wait_all(coeff_hbm, coeff_ref, sems.at[4])
    turned_ref[...] = coeff_ref[...].T
    for targets, out in zip(messages, outs):
        total = chunks_of(chips, turned_ref, rolled_ref, wide, targets, 1)
        out[...] = total.astype(BF16).T


def first(wide, chips, messages, level, pad, shift, coeff, tables):
    rows, columns = coeff.shape
    points = tables.shape[2]
    slots = pad.shape[0]
    half = points // wide // 2
    inputs = (level, pad, shift, coeff, tables)
    return call(
        functools.partial(first_kernel, wide, chips, messages),
        "forward_first",
        (
            *(array((len(targets) * half, columns), BF16) for targets in messages),
            array((columns, rows), BF16),
            array((rows, points), BF16),
        ),
        [HBM] * 5,
        (VMEM,) * (len(messages) + 2),
        [
            pltpu.SMEM((slots,), jnp.int32),
            pltpu.SMEM((slots,), jnp.int32),
            pltpu.SMEM((slots,), jnp.int32),
            pltpu.VMEM(coeff.shape, coeff.dtype),
            pltpu.VMEM(tables.shape, tables.dtype),
            pltpu.SemaphoreType.DMA((5,)),
        ],
    )(*(in_hbm(value) for value in inputs))


def chunk_kernel(wide, chips, messages, turned_ref, rolled_ref, *outs):
    for targets, out in zip(messages, outs):
        total = chunks_of(chips, turned_ref, rolled_ref, wide, targets, 0)
        out[...] = total.astype(BF16).T


def chunk(wide, chips, messages, turned, rolled):
    half = rolled.shape[1] // wide // 2
    return call(
        functools.partial(chunk_kernel, wide, chips, messages),
        "forward_near",
        tuple(array((len(targets) * half, turned.shape[0]), BF16) for targets in messages),
        [VMEM] * 2,
        (VMEM,) * len(messages),
    )(turned, rolled)


def last_kernel(
    wide,
    chips,
    far_targets,
    near_targets,
    turned_ref,
    rolled_ref,
    basis_hbm,
    potential_hbm,
    far_ref,
    near_ref,
    basis_ref,
    potential_ref,
    sems,
):
    pairs = basis_pieces(basis_hbm, basis_ref)
    for j, (source, target) in enumerate(pairs):
        start_pieces(source, target, 64, sems.at[1 + j])
    start_pieces(potential_hbm, potential_ref, 8, sems.at[0])
    far_ref[...] = chunks_of(chips, turned_ref, rolled_ref, wide, far_targets, 1).T
    near_ref[...] = chunks_of(chips, turned_ref, rolled_ref, wide, near_targets, 0).T
    for j, (source, target) in enumerate(pairs):
        wait_all(source, target, sems.at[1 + j])
    wait_all(potential_hbm, potential_ref, sems.at[0])


def last(wide, chips, far_targets, near_targets, turned, rolled, basis, potential):
    columns, rows = turned.shape
    half = rolled.shape[1] // wide // 2
    return call(
        functools.partial(last_kernel, wide, chips, far_targets, near_targets),
        "forward_own",
        (
            array((len(far_targets) * half, columns), F32),
            array((len(near_targets) * half, columns), F32),
            array((chips, columns, basis.shape[1]), BF16),
            array(potential.shape, F32),
        ),
        [VMEM, VMEM, HBM, HBM],
        (VMEM,) * 4,
        [pltpu.SemaphoreType.DMA((1 + chips,))],
    )(turned, rolled, in_hbm(basis), in_hbm(potential))


def halfway_kernel(count, mine_ref, *refs):
    parts, outs = refs[:-count], refs[-count:]
    rows = outs[0].shape[0]
    for h in range(count):
        span = slice(h * rows, (h + 1) * rows)
        total = mine_ref[span, :]
        for part in parts:
            total = total + part[span, :].astype(F32)
        outs[h][...] = total.astype(outs[h].dtype)


def halfway(count, mine, parts):
    rows, columns = mine.shape
    return call(
        functools.partial(halfway_kernel, count),
        "wide_half",
        tuple(array((rows // count, columns), BF16 if h else F32) for h in range(count)),
        [VMEM] * (1 + len(parts)),
        (VMEM,) * count,
    )(mine, *parts)


def combine_kernel(chips, first, mine_ref, *refs):
    count = chips // 2
    parts, outs = refs[:-count], refs[-count:]
    chip = lax.axis_index("narrow") // 2
    rows = outs[0].shape[0]
    for i in range(count):
        start = pl.multiple_of((chip ^ (first + i)) % count * rows, rows)
        total = mine_ref[pl.ds(start, rows), :]
        for part in parts:
            total = total + part[pl.ds(start, rows), :].astype(F32)
        outs[i][...] = total.astype(BF16)


def combine(chips, first, mine, parts):
    rows, columns = mine.shape
    count = chips // 2
    return call(
        functools.partial(combine_kernel, chips, first),
        "wide_sum",
        (array((rows // count, columns), BF16),) * count,
        [VMEM] * (len(parts) + 1),
        (VMEM,) * count,
    )(mine, *parts)


def own_points_kernel(x_ref, basis_ref, out_ref):
    out_ref[...] = dot(x_ref[...], basis_ref[0])


def own_points(x, where):
    basis, _ = where
    rows = x.shape[0]
    points = basis.shape[2]
    return call(
        own_points_kernel,
        "points_own",
        array((rows, points), F32),
        [VMEM] * 2,
        VMEM,
        flops=2 * rows * points * x.shape[1],
        moved=2 * MIB,
    )(x, basis)


def more_points_kernel(j, total_ref, x_ref, basis_ref, out_ref):
    out_ref[...] = total_ref[...] + dot(x_ref[...], basis_ref[j])


def more_points(total, x, where):
    basis, j = where
    rows, points = total.shape
    return call(
        functools.partial(more_points_kernel, j),
        "points_more",
        array((rows, points), F32),
        [VMEM] * 3,
        VMEM,
        flops=2 * rows * points * x.shape[1],
        moved=2 * MIB,
    )(total, x, basis)


def last_points_kernel(j, total_ref, x_ref, basis_ref, mine_ref, theirs_ref):
    core = lax.axis_index("narrow") % 2
    rows = mine_ref.shape[0]
    total = total_ref[...] + dot(x_ref[...], basis_ref[j])
    low, high = total[:rows], total[rows:]
    mine_ref[...] = jnp.where(core == 0, low, high)
    theirs_ref[...] = jnp.where(core == 0, high, low)


def last_points(total, x, where):
    basis, j = where
    rows, points = total.shape
    half = array((rows // 2, points), F32)
    return call(
        functools.partial(last_points_kernel, j),
        "points_last",
        (half, half),
        [VMEM] * 3,
        (VMEM, VMEM),
        flops=2 * rows * points * x.shape[1],
        moved=2 * MIB,
    )(total, x, basis)


def act_kernel(mine_ref, other_ref, potential_ref, out_ref):
    on_grid = mine_ref[...] + other_ref[...]
    out_ref[...] = (potential_ref[...] * on_grid).astype(BF16)


def act(mine, other, potential):
    return call(
        act_kernel, "act", array(mine.shape, BF16), [VMEM] * 3, VMEM, moved=MIB
    )(mine, other, potential)


def first_functions_kernel(j, mine_ref, other_ref, basis_ref, out_ref, both_ref):
    core = lax.axis_index("narrow") % 2
    rows = mine_ref.shape[0]
    mine, other = mine_ref[...].astype(F32), other_ref[...].astype(F32)
    both_ref[:rows] = jnp.where(core == 0, mine, other).astype(BF16)
    both_ref[rows:] = jnp.where(core == 0, other, mine).astype(BF16)
    out_ref[...] = dot_turned(both_ref[...], basis_ref[j]).astype(BF16)


def first_functions(mine, other, where):
    basis, j = where
    rows, points = mine.shape
    columns = basis.shape[1]
    return call(
        functools.partial(first_functions_kernel, j),
        "functions_first",
        (array((2 * rows, columns), BF16), array((2 * rows, points), BF16)),
        [VMEM] * 3,
        (VMEM, VMEM),
        flops=4 * rows * points * columns,
        moved=2 * MIB,
    )(mine, other, basis)


def functions_kernel(j, both_ref, basis_ref, out_ref):
    out_ref[...] = dot_turned(both_ref[...], basis_ref[j]).astype(BF16)


def functions(both, where):
    basis, j = where
    rows, points = both.shape
    columns = basis.shape[1]
    return call(
        functools.partial(functions_kernel, j),
        "functions_more",
        array((rows, columns), BF16),
        [VMEM] * 2,
        VMEM,
        flops=2 * rows * points * columns,
        moved=2 * MIB,
    )(both, basis)


def assemble_kernel(*refs):
    parts, out_ref = refs[:-1], refs[-1]
    chip = lax.axis_index("narrow") // 2
    rows = parts[0].shape[0]
    for j, part in enumerate(parts):
        start = pl.multiple_of((chip ^ j) * rows, rows)
        out_ref[pl.ds(start, rows), :] = part[...]


def assemble(parts):
    rows, columns = parts[0].shape
    chips = len(parts)
    return call(
        assemble_kernel,
        "assemble",
        array((rows * chips, columns), BF16),
        [VMEM] * chips,
        VMEM,
        moved=MIB // 4,
    )(*parts)


def own_kernel(wide, pad_ref, rolled_ref, grid_ref, coeff_ref, row_ref, column_ref, out_ref):
    slots = pad_ref.shape[0]
    width = rolled_ref.shape[0] // slots
    me = lax.axis_index("wide")
    own = rolled_ref.shape[1] // wide
    start = pl.multiple_of(me * own, own)
    out_ref[...] = dot(rolled_ref[:, pl.ds(start, own)], grid_ref[...])
    row = lax.broadcasted_iota(jnp.int32, (width, out_ref.shape[1]), 0)
    for s in range(slots):
        rows = slice(s * width, (s + 1) * width)
        energy = row_ref[rows, :] + column_ref[...]
        diagonal = energy * coeff_ref[rows, :].astype(F32)
        out_ref[rows, :] += jnp.where(row < width - pad_ref[s], diagonal, 0.0)


def backward_own(wide, pad, rolled, grid, coeff, row_energy, column_energy):
    smem = pl.BlockSpec(memory_space=pltpu.SMEM)
    rows, columns = coeff.shape
    return call(
        functools.partial(own_kernel, wide),
        "backward_own",
        array(coeff.shape, F32),
        [smem] + [VMEM] * 5,
        VMEM,
        flops=2 * rows * columns * rolled.shape[1] // wide,
        moved=4 * MIB,
    )(pad, rolled, grid, coeff, row_energy[:, None], column_energy[None, :])


def more_kernel(wide, k, total_ref, rolled_ref, grid_ref, out_ref):
    own = rolled_ref.shape[1] // wide
    start = pl.multiple_of((lax.axis_index("wide") ^ k) * own, own)
    out_ref[...] = total_ref[...] + dot(rolled_ref[:, pl.ds(start, own)], grid_ref[...])


def backward_more(wide, k, total, rolled, grid):
    rows, columns = total.shape
    return call(
        functools.partial(more_kernel, wide, k),
        "backward_more",
        array(total.shape, F32),
        [VMEM] * 3,
        VMEM,
        flops=2 * rows * columns * rolled.shape[1] // wide,
        moved=3 * MIB,
    )(total, rolled, grid)


def end_kernel(wide, k, total_ref, rolled_ref, grid_ref, out_hbm, out_ref, sems):
    own = rolled_ref.shape[1] // wide
    start = pl.multiple_of((lax.axis_index("wide") ^ k) * own, own)
    steps = sems.shape[0]
    rows = rolled_ref.shape[0] // steps
    copies = []
    for i in range(steps):
        span = pl.ds(i * rows, rows)
        part = dot(rolled_ref[span, pl.ds(start, own)], grid_ref[...])
        out_ref[span, :] = total_ref[span, :] + part
        copies.append(pltpu.make_async_copy(out_ref.at[span, :], out_hbm.at[span, :], sems.at[i]))
        copies[-1].start()
    for copy in copies:
        copy.wait()


def backward_end(wide, k, total, rolled, grid):
    rows, columns = total.shape
    return call(
        functools.partial(end_kernel, wide, k),
        "backward_end",
        array(total.shape, F32),
        [VMEM] * 3,
        HBM,
        [pltpu.VMEM(total.shape, F32), pltpu.SemaphoreType.DMA((16,))],
        flops=2 * rows * columns * rolled.shape[1] // wide,
        moved=4 * MIB,
    )(total, rolled, grid)


def exchange(value, step, size, axis):
    return lax.ppermute(value, axis, [(i, i ^ step) for i in range(size)])


def body(
    wide,
    narrow,
    coeff,
    groupb_row_energy,
    groupa_energy,
    groupb_basis_values,
    basis_a,
    potential,
    slot_sparse_level,
    block_pad,
    slot_grid_offset,
):
    chips = narrow // 2
    tables = jnp.swapaxes(groupb_basis_values, 1, 2)
    half = chips // 2
    low = 1 << ((wide.bit_length() - 1) // 2)
    lows = list(range(low))
    highs = list(range(0, wide, low))
    far_messages = [[m ^ h for h in highs] for m in lows[1:]]
    near_messages = [[h ^ m for m in lows] for h in highs[1:]]
    *far_out, turned, rolled = first(
        wide, chips, far_messages, slot_sparse_level, block_pad, slot_grid_offset, coeff, tables
    )
    far_in = [exchange(v, m, wide, "wide") for v, m in zip(far_out, lows[1:])]
    near_out = chunk(wide, chips, near_messages, turned, rolled)
    near_in = [exchange(v, h, wide, "wide") for v, h in zip(near_out, highs[1:])]
    far, near, basis, pot = last(wide, chips, highs, lows, turned, rolled, basis_a, potential)
    where = {j: (basis, j) for j in range(chips)}
    far, *far_out = halfway(len(highs), far, far_in)
    far_in = [exchange(v, h, wide, "wide") for v, h in zip(far_out, highs[1:])]
    near, *near_out = halfway(len(lows), near, near_in)
    near_in = [exchange(v, m, wide, "wide") for v, m in zip(near_out, lows[1:])]
    pieces = combine(chips, half, far, far_in)
    xs = {j: exchange(pieces[j - half], 2 * j, narrow, "narrow") for j in range(half, chips)}
    pieces = combine(chips, 0, near, near_in)
    for j in range(1, half):
        xs[j] = exchange(pieces[j], 2 * j, narrow, "narrow")
    visits = list(range(half, chips)) + list(range(1, half))
    total = own_points(pieces[0], where[0])
    for j in visits[:-1]:
        total = more_points(total, xs[j], where[j])
    mine, theirs = last_points(total, xs[visits[-1]], where[visits[-1]])
    acted = act(mine, exchange(theirs, 1, narrow, "narrow"), pot)
    other = exchange(acted, 1, narrow, "narrow")
    block, both = first_functions(acted, other, where[chips - 1])
    blocks = {chips - 1: exchange(block, 2 * (chips - 1), narrow, "narrow")}
    for j in reversed(range(1, chips - 1)):
        blocks[j] = exchange(functions(both, where[j]), 2 * j, narrow, "narrow")
    grid = assemble([functions(both, where[0])] + [blocks[j] for j in range(1, chips)])
    grids = [exchange(grid, k, wide, "wide") for k in range(1, wide)]
    total = backward_own(
        wide, block_pad, rolled, grid, coeff, groupb_row_energy, groupa_energy
    )
    for k in range(1, wide - 1):
        total = backward_more(wide, k, total, rolled, grids[k - 1])
    return backward_end(wide, wide - 1, total, rolled, grids[-1])


def solution(mesh):
    return jax.shard_map(
        functools.partial(body, mesh.shape["wide"], mesh.shape["narrow"]),
        mesh=mesh,
        in_specs=(
            P("wide", "narrow"),
            P("wide"),
            P("narrow"),
            P(),
            P(),
            P(("wide", "narrow"), None),
            P("wide"),
            P("wide"),
            P("wide"),
        ),
        out_specs=P("wide", "narrow"),
        check_vma=False,
    )
```

```python
import functools

import jax
import jax.numpy as jnp
from jax import lax
from jax.experimental import pallas as pl
from jax.experimental.pallas import tpu as pltpu
from jax.sharding import PartitionSpec as P

MIB = 1024 * 1024
HBM = pl.BlockSpec(memory_space=pltpu.HBM)
VMEM = pl.BlockSpec(memory_space=pltpu.VMEM)
BF16 = jnp.bfloat16
F32 = jnp.float32
LONG = 8


def call(kernel, name, out_shape, in_specs, out_specs, scratch=(), flops=0, moved=0, mib=16):
    return pl.pallas_call(
        kernel,
        out_shape=out_shape,
        in_specs=in_specs,
        out_specs=out_specs,
        scratch_shapes=scratch,
        compiler_params=pltpu.CompilerParams(vmem_limit_bytes=mib * MIB),
        cost_estimate=pl.CostEstimate(flops=flops, bytes_accessed=moved, transcendentals=0),
        name=name,
    )


def in_hbm(value):
    return pltpu.with_memory_space_constraint(value, pltpu.HBM)


def array(shape, dtype):
    return jax.ShapeDtypeStruct(shape, dtype)


def dot(left, right):
    return jnp.dot(left, right, preferred_element_type=F32)


def dot_turned(left, right):
    return lax.dot_general(left, right, (((1,), (1,)), ((), ())), preferred_element_type=F32)


def chunk_of(turned_ref, rolled_ref, wide, k):
    own = rolled_ref.shape[1] // wide
    start = pl.multiple_of((lax.axis_index("wide") ^ k) * own, own)
    return dot(turned_ref[...], rolled_ref[:, pl.ds(start, own)])


def store_halves(chips, total, far_ref, near_ref):
    upper = lax.axis_index("narrow") // 2 >= chips // 2
    rows = far_ref.shape[0]
    turned = total.astype(BF16).T.astype(F32)
    low, high = turned[:rows], turned[rows:]
    far_ref[...] = jnp.where(upper, low, high).astype(BF16)
    near_ref[...] = jnp.where(upper, high, low).astype(BF16)


def start_pieces(source, target, rows, sem):
    for r in range(0, source.shape[0], rows):
        span = pl.ds(r, rows)
        pltpu.make_async_copy(source.at[span], target.at[span], sem).start()


def wait_all(source, target, sem):
    pltpu.make_async_copy(source, target, sem).wait()


def basis_pieces(basis_hbm, basis_ref):
    chips, columns, _ = basis_ref.shape
    place = lax.axis_index("narrow")
    core, chip = place % 2, place // 2
    pairs = []
    for j in range(chips):
        start = pl.multiple_of(((chip ^ j) * 2 + core) * columns, columns)
        pairs.append((basis_hbm.at[pl.ds(start, columns)], basis_ref.at[j]))
    return pairs


def halves(rows, columns):
    return (array((rows // 2, columns), BF16),) * 2


def first_kernel(
    wide,
    chips,
    level_hbm,
    pad_hbm,
    shift_hbm,
    coeff_hbm,
    table_hbm,
    basis_hbm,
    potential_hbm,
    out_ref,
    turned_ref,
    rolled_ref,
    basis_ref,
    potential_ref,
    level_ref,
    pad_ref,
    shift_ref,
    coeff_ref,
    table_ref,
    sems,
):
    slots = pad_ref.shape[0]
    levels, width, points = table_ref.shape
    small = [
        pltpu.make_async_copy(source, target, sems.at[i])
        for i, (source, target) in enumerate(
            ((level_hbm, level_ref), (shift_hbm, shift_ref), (pad_hbm, pad_ref))
        )
    ]
    for copy in small:
        copy.start()
    for n in range(levels):
        start_pieces(table_hbm.at[n], table_ref.at[n], 32, sems.at[3])
    start_pieces(coeff_hbm, coeff_ref, 128, sems.at[4])
    pairs = basis_pieces(basis_hbm, basis_ref)
    for j, (source, target) in enumerate(pairs):
        start_pieces(source, target, 64, sems.at[6 + j])
    start_pieces(potential_hbm, potential_ref, 8, sems.at[5])
    for copy in small:
        copy.wait()
    wait_all(table_hbm, table_ref, sems.at[3])
    row = lax.broadcasted_iota(jnp.int32, (width, 128), 0)
    for s in range(slots):
        rows = slice(s * width, (s + 1) * width)
        live = jnp.where(row < width - pad_ref[s], 1.0, 0.0).astype(BF16)
        rolled = pltpu.roll(table_ref[level_ref[s]], shift_ref[s], 1)
        for p in range(0, points, 128):
            rolled_ref[rows, p : p + 128] = rolled[:, p : p + 128] * live
    wait_all(coeff_hbm, coeff_ref, sems.at[4])
    turned_ref[...] = coeff_ref[...].T
    out_ref[...] = chunk_of(turned_ref, rolled_ref, wide, wide - 1).astype(BF16).T
    for j, (source, target) in enumerate(pairs):
        wait_all(source, target, sems.at[6 + j])
    wait_all(potential_hbm, potential_ref, sems.at[5])


def first(wide, chips, level, pad, shift, coeff, tables, basis, potential):
    rows, columns = coeff.shape
    points = tables.shape[2]
    slots = pad.shape[0]
    inputs = (level, pad, shift, coeff, tables, basis, potential)
    return call(
        functools.partial(first_kernel, wide, chips),
        "forward_first",
        (
            array((points // wide, columns), BF16),
            array((columns, rows), BF16),
            array((rows, points), BF16),
            array((chips, columns, basis.shape[1]), BF16),
            array(potential.shape, F32),
        ),
        [HBM] * 7,
        (VMEM,) * 5,
        [
            pltpu.SMEM((slots,), jnp.int32),
            pltpu.SMEM((slots,), jnp.int32),
            pltpu.SMEM((slots,), jnp.int32),
            pltpu.VMEM(coeff.shape, coeff.dtype),
            pltpu.VMEM(tables.shape, tables.dtype),
            pltpu.SemaphoreType.DMA((6 + chips,)),
        ],
        flops=2 * rows * points // wide * columns,
        moved=4 * MIB,
    )(*(in_hbm(value) for value in inputs))


def chunk_kernel(wide, chips, k, turned_ref, rolled_ref, far_ref, near_ref):
    store_halves(chips, chunk_of(turned_ref, rolled_ref, wide, k), far_ref, near_ref)


def chunk(wide, chips, k, turned, rolled):
    columns, rows = turned.shape
    own = rolled.shape[1] // wide
    return call(
        functools.partial(chunk_kernel, wide, chips, k),
        "forward_chunk",
        halves(own, columns),
        [VMEM] * 2,
        (VMEM,) * 2,
        flops=2 * rows * own * columns * LONG,
        moved=MIB * LONG,
    )(turned, rolled)


def last_kernel(wide, turned_ref, rolled_ref, out_ref):
    out_ref[...] = chunk_of(turned_ref, rolled_ref, wide, 0).T


def last(wide, turned, rolled):
    columns, rows = turned.shape
    own = rolled.shape[1] // wide
    return call(
        functools.partial(last_kernel, wide),
        "forward_own",
        array((own, columns), F32),
        [VMEM] * 2,
        VMEM,
        flops=2 * rows * own * columns,
        moved=MIB,
    )(turned, rolled)


def combine_kernel(chips, first, mine_ref, whole_ref, *refs):
    count = chips // 2
    parts, outs = refs[:-count], refs[-count:]
    chip = lax.axis_index("narrow") // 2
    rows = outs[0].shape[0]
    for i in range(count):
        target = chip ^ (first + i)
        span = pl.ds(pl.multiple_of(target * rows, rows), rows)
        total = mine_ref[span, :] + whole_ref[span, :].astype(F32)
        start = pl.multiple_of((target % count) * rows, rows)
        for part in parts:
            total = total + part[pl.ds(start, rows), :].astype(F32)
        outs[i][...] = total.astype(BF16)


def combine(chips, first, mine, whole, parts):
    rows, columns = mine.shape
    count = chips // 2
    return call(
        functools.partial(combine_kernel, chips, first),
        "wide_sum",
        (array((rows // chips, columns), BF16),) * count,
        [VMEM] * (len(parts) + 2),
        (VMEM,) * count,
        moved=MIB,
    )(mine, whole, *parts)


def own_points_kernel(x_ref, basis_ref, out_ref):
    out_ref[...] = dot(x_ref[...], basis_ref[0])


def own_points(x, where):
    basis, _ = where
    rows = x.shape[0]
    points = basis.shape[2]
    return call(
        own_points_kernel,
        "points_own",
        array((rows, points), F32),
        [VMEM] * 2,
        VMEM,
        flops=2 * rows * points * x.shape[1],
        moved=2 * MIB,
    )(x, basis)


def more_points_kernel(j, total_ref, x_ref, basis_ref, out_ref):
    out_ref[...] = total_ref[...] + dot(x_ref[...], basis_ref[j])


def more_points(total, x, where):
    basis, j = where
    rows, points = total.shape
    return call(
        functools.partial(more_points_kernel, j),
        "points_more",
        array((rows, points), F32),
        [VMEM] * 3,
        VMEM,
        flops=2 * rows * points * x.shape[1],
        moved=2 * MIB,
    )(total, x, basis)


def last_points_kernel(j, total_ref, x_ref, basis_ref, mine_ref, theirs_ref):
    core = lax.axis_index("narrow") % 2
    rows = mine_ref.shape[0]
    total = total_ref[...] + dot(x_ref[...], basis_ref[j])
    low, high = total[:rows], total[rows:]
    mine_ref[...] = jnp.where(core == 0, low, high)
    theirs_ref[...] = jnp.where(core == 0, high, low)


def last_points(total, x, where):
    basis, j = where
    rows, points = total.shape
    half = array((rows // 2, points), F32)
    return call(
        functools.partial(last_points_kernel, j),
        "points_last",
        (half, half),
        [VMEM] * 3,
        (VMEM, VMEM),
        flops=2 * rows * points * x.shape[1],
        moved=2 * MIB,
    )(total, x, basis)


def act_kernel(mine_ref, other_ref, potential_ref, out_ref):
    on_grid = mine_ref[...] + other_ref[...]
    out_ref[...] = (potential_ref[...] * on_grid).astype(BF16)


def act(mine, other, potential):
    return call(
        act_kernel, "act", array(mine.shape, BF16), [VMEM] * 3, VMEM, moved=MIB
    )(mine, other, potential)


def first_functions_kernel(j, mine_ref, other_ref, basis_ref, out_ref, both_ref):
    core = lax.axis_index("narrow") % 2
    rows = mine_ref.shape[0]
    mine, other = mine_ref[...].astype(F32), other_ref[...].astype(F32)
    both_ref[:rows] = jnp.where(core == 0, mine, other).astype(BF16)
    both_ref[rows:] = jnp.where(core == 0, other, mine).astype(BF16)
    out_ref[...] = dot_turned(both_ref[...], basis_ref[j]).astype(BF16)


def first_functions(mine, other, where):
    basis, j = where
    rows, points = mine.shape
    columns = basis.shape[1]
    return call(
        functools.partial(first_functions_kernel, j),
        "functions_first",
        (array((2 * rows, columns), BF16), array((2 * rows, points), BF16)),
        [VMEM] * 3,
        (VMEM, VMEM),
        flops=4 * rows * points * columns,
        moved=2 * MIB,
    )(mine, other, basis)


def functions_kernel(j, both_ref, basis_ref, out_ref):
    out_ref[...] = dot_turned(both_ref[...], basis_ref[j]).astype(BF16)


def functions(both, where):
    basis, j = where
    rows, points = both.shape
    columns = basis.shape[1]
    return call(
        functools.partial(functions_kernel, j),
        "functions_more",
        array((rows, columns), BF16),
        [VMEM] * 2,
        VMEM,
        flops=2 * rows * points * columns,
        moved=2 * MIB,
    )(both, basis)


def assemble_kernel(*refs):
    parts, out_ref = refs[:-1], refs[-1]
    chip = lax.axis_index("narrow") // 2
    rows = parts[0].shape[0]
    for j, part in enumerate(parts):
        start = pl.multiple_of((chip ^ j) * rows, rows)
        out_ref[pl.ds(start, rows), :] = part[...]


def assemble(parts):
    rows, columns = parts[0].shape
    chips = len(parts)
    return call(
        assemble_kernel,
        "assemble",
        array((rows * chips, columns), BF16),
        [VMEM] * chips,
        VMEM,
        moved=MIB // 4,
    )(*parts)


def own_kernel(wide, pad_ref, rolled_ref, grid_ref, coeff_ref, row_ref, column_ref, out_ref):
    slots = pad_ref.shape[0]
    width = rolled_ref.shape[0] // slots
    me = lax.axis_index("wide")
    own = rolled_ref.shape[1] // wide
    start = pl.multiple_of(me * own, own)
    out_ref[...] = dot(rolled_ref[:, pl.ds(start, own)], grid_ref[...])
    row = lax.broadcasted_iota(jnp.int32, (width, out_ref.shape[1]), 0)
    for s in range(slots):
        rows = slice(s * width, (s + 1) * width)
        energy = row_ref[rows, :] + column_ref[...]
        diagonal = energy * coeff_ref[rows, :].astype(F32)
        out_ref[rows, :] += jnp.where(row < width - pad_ref[s], diagonal, 0.0)


def backward_own(wide, pad, rolled, grid, coeff, row_energy, column_energy):
    smem = pl.BlockSpec(memory_space=pltpu.SMEM)
    rows, columns = coeff.shape
    return call(
        functools.partial(own_kernel, wide),
        "backward_own",
        array(coeff.shape, F32),
        [smem] + [VMEM] * 5,
        VMEM,
        flops=2 * rows * columns * rolled.shape[1] // wide,
        moved=4 * MIB,
    )(pad, rolled, grid, coeff, row_energy[:, None], column_energy[None, :])


def more_kernel(wide, k, total_ref, rolled_ref, grid_ref, out_ref):
    own = rolled_ref.shape[1] // wide
    start = pl.multiple_of((lax.axis_index("wide") ^ k) * own, own)
    out_ref[...] = total_ref[...] + dot(rolled_ref[:, pl.ds(start, own)], grid_ref[...])


def backward_more(wide, k, total, rolled, grid):
    rows, columns = total.shape
    return call(
        functools.partial(more_kernel, wide, k),
        "backward_more",
        array(total.shape, F32),
        [VMEM] * 3,
        VMEM,
        flops=2 * rows * columns * rolled.shape[1] // wide,
        moved=3 * MIB,
    )(total, rolled, grid)


def end_kernel(wide, k, total_ref, rolled_ref, grid_ref, out_hbm, out_ref, sems):
    own = rolled_ref.shape[1] // wide
    start = pl.multiple_of((lax.axis_index("wide") ^ k) * own, own)
    steps = sems.shape[0]
    rows = rolled_ref.shape[0] // steps
    copies = []
    for i in range(steps):
        span = pl.ds(i * rows, rows)
        part = dot(rolled_ref[span, pl.ds(start, own)], grid_ref[...])
        out_ref[span, :] = total_ref[span, :] + part
        copies.append(pltpu.make_async_copy(out_ref.at[span, :], out_hbm.at[span, :], sems.at[i]))
        copies[-1].start()
    for copy in copies:
        copy.wait()


def backward_end(wide, k, total, rolled, grid):
    rows, columns = total.shape
    return call(
        functools.partial(end_kernel, wide, k),
        "backward_end",
        array(total.shape, F32),
        [VMEM] * 3,
        HBM,
        [pltpu.VMEM(total.shape, F32), pltpu.SemaphoreType.DMA((16,))],
        flops=2 * rows * columns * rolled.shape[1] // wide,
        moved=4 * MIB,
    )(total, rolled, grid)


def exchange(value, step, size, axis):
    return lax.ppermute(value, axis, [(i, i ^ step) for i in range(size)])


def body(
    wide,
    narrow,
    coeff,
    groupb_row_energy,
    groupa_energy,
    groupb_basis_values,
    basis_a,
    potential,
    slot_sparse_level,
    block_pad,
    slot_grid_offset,
):
    chips = narrow // 2
    tables = jnp.swapaxes(groupb_basis_values, 1, 2)
    half = chips // 2
    order = list(range(1, wide - 1))
    whole, turned, rolled, basis, pot = first(
        wide,
        chips,
        slot_sparse_level,
        block_pad,
        slot_grid_offset,
        coeff,
        tables,
        basis_a,
        potential,
    )
    whole = exchange(whole, wide - 1, wide, "wide")
    where = {j: (basis, j) for j in range(chips)}
    sent = {k: chunk(wide, chips, k, turned, rolled) for k in order}
    far_parts = [exchange(sent[k][0], k, wide, "wide") for k in order]
    near_parts = [exchange(sent[k][1], k, wide, "wide") for k in order]
    mine = last(wide, turned, rolled)
    pieces = combine(chips, half, mine, whole, far_parts)
    xs = {j: exchange(pieces[j - half], 2 * j, narrow, "narrow") for j in range(half, chips)}
    pieces = combine(chips, 0, mine, whole, near_parts)
    for j in range(1, half):
        xs[j] = exchange(pieces[j], 2 * j, narrow, "narrow")
    total = own_points(pieces[0], where[0])
    visits = list(range(half, chips)) + list(range(1, half))
    for j in visits[:-1]:
        total = more_points(total, xs[j], where[j])
    mine, theirs = last_points(total, xs[visits[-1]], where[visits[-1]])
    acted = act(mine, exchange(theirs, 1, narrow, "narrow"), pot)
    other = exchange(acted, 1, narrow, "narrow")
    leave = list(range(1, chips))
    block, both = first_functions(acted, other, where[leave[0]])
    blocks = {leave[0]: exchange(block, 2 * leave[0], narrow, "narrow")}
    for j in leave[1:]:
        blocks[j] = exchange(functions(both, where[j]), 2 * j, narrow, "narrow")
    grid = assemble([functions(both, where[0])] + [blocks[j] for j in range(1, chips)])
    steps = [wide - 1] + order
    grids = {k: exchange(grid, k, wide, "wide") for k in steps}
    total = backward_own(
        wide, block_pad, rolled, grid, coeff, groupb_row_energy, groupa_energy
    )
    for k in steps[:-1]:
        total = backward_more(wide, k, total, rolled, grids[k])
    return backward_end(wide, steps[-1], total, rolled, grids[steps[-1]])


def solution(mesh):
    return jax.shard_map(
        functools.partial(body, mesh.shape["wide"], mesh.shape["narrow"]),
        mesh=mesh,
        in_specs=(
            P("wide", "narrow"),
            P("wide"),
            P("narrow"),
            P(),
            P(),
            P(("wide", "narrow"), None),
            P("wide"),
            P("wide"),
            P("wide"),
        ),
        out_specs=P("wide", "narrow"),
        check_vma=False,
    )
```

```python
import functools

import jax
import jax.numpy as jnp
from jax import lax
from jax.experimental import pallas as pl
from jax.experimental.pallas import tpu as pltpu
from jax.sharding import PartitionSpec as P

MIB = 1024 * 1024
HBM = pl.BlockSpec(memory_space=pltpu.HBM)
VMEM = pl.BlockSpec(memory_space=pltpu.VMEM)
BF16 = jnp.bfloat16
F32 = jnp.float32
LONG = 8


def call(kernel, name, out_shape, in_specs, out_specs, scratch=(), flops=0, moved=0, mib=16):
    return pl.pallas_call(
        kernel,
        out_shape=out_shape,
        in_specs=in_specs,
        out_specs=out_specs,
        scratch_shapes=scratch,
        compiler_params=pltpu.CompilerParams(vmem_limit_bytes=mib * MIB),
        cost_estimate=pl.CostEstimate(flops=flops, bytes_accessed=moved, transcendentals=0),
        name=name,
    )


def in_hbm(value):
    return pltpu.with_memory_space_constraint(value, pltpu.HBM)


def array(shape, dtype):
    return jax.ShapeDtypeStruct(shape, dtype)


def dot(left, right):
    return jnp.dot(left, right, preferred_element_type=F32)


def dot_turned(left, right):
    return lax.dot_general(left, right, (((1,), (1,)), ((), ())), preferred_element_type=F32)


def chunk_of(turned_ref, rolled_ref, wide, k):
    own = rolled_ref.shape[1] // wide
    start = pl.multiple_of((lax.axis_index("wide") ^ k) * own, own)
    return dot(turned_ref[...], rolled_ref[:, pl.ds(start, own)])


def store_halves(chips, total, far_ref, near_ref):
    upper = lax.axis_index("narrow") // 2 >= chips // 2
    rows = far_ref.shape[0]
    turned = total.astype(BF16).T.astype(F32)
    low, high = turned[:rows], turned[rows:]
    far_ref[...] = jnp.where(upper, low, high).astype(BF16)
    near_ref[...] = jnp.where(upper, high, low).astype(BF16)


def start_pieces(source, target, rows, sem):
    for r in range(0, source.shape[0], rows):
        span = pl.ds(r, rows)
        pltpu.make_async_copy(source.at[span], target.at[span], sem).start()


def wait_all(source, target, sem):
    pltpu.make_async_copy(source, target, sem).wait()


def basis_pieces(basis_hbm, basis_ref):
    chips, columns, _ = basis_ref.shape
    place = lax.axis_index("narrow")
    core, chip = place % 2, place // 2
    pairs = []
    for j in range(chips):
        start = pl.multiple_of(((chip ^ j) * 2 + core) * columns, columns)
        pairs.append((basis_hbm.at[pl.ds(start, columns)], basis_ref.at[j]))
    return pairs


def halves(rows, columns):
    return (array((rows // 2, columns), BF16),) * 2


def first_kernel(
    wide,
    chips,
    level_hbm,
    pad_hbm,
    shift_hbm,
    coeff_hbm,
    table_hbm,
    basis_hbm,
    potential_hbm,
    out_ref,
    turned_ref,
    rolled_ref,
    basis_ref,
    potential_ref,
    level_ref,
    pad_ref,
    shift_ref,
    coeff_ref,
    table_ref,
    sems,
):
    slots = pad_ref.shape[0]
    levels, width, points = table_ref.shape
    small = [
        pltpu.make_async_copy(source, target, sems.at[i])
        for i, (source, target) in enumerate(
            ((level_hbm, level_ref), (shift_hbm, shift_ref), (pad_hbm, pad_ref))
        )
    ]
    for copy in small:
        copy.start()
    for n in range(levels):
        start_pieces(table_hbm.at[n], table_ref.at[n], 32, sems.at[3])
    start_pieces(coeff_hbm, coeff_ref, 128, sems.at[4])
    pairs = basis_pieces(basis_hbm, basis_ref)
    for j, (source, target) in enumerate(pairs):
        start_pieces(source, target, 64, sems.at[6 + j])
    start_pieces(potential_hbm, potential_ref, 8, sems.at[5])
    for copy in small:
        copy.wait()
    wait_all(table_hbm, table_ref, sems.at[3])
    row = lax.broadcasted_iota(jnp.int32, (width, 128), 0)

    def roll_slot(s, _):
        rows = pl.ds(pl.multiple_of(s * width, width), width)
        live = jnp.where(row < width - pad_ref[s], 1.0, 0.0).astype(BF16)
        rolled = pltpu.roll(table_ref[level_ref[s]], shift_ref[s], 1)
        for p in range(0, points, 128):
            rolled_ref[rows, p : p + 128] = rolled[:, p : p + 128] * live
        return 0

    lax.fori_loop(0, slots, roll_slot, 0, unroll=2)
    wait_all(coeff_hbm, coeff_ref, sems.at[4])
    turned_ref[...] = coeff_ref[...].T
    out_ref[...] = chunk_of(turned_ref, rolled_ref, wide, wide - 1).astype(BF16).T
    for j, (source, target) in enumerate(pairs):
        wait_all(source, target, sems.at[6 + j])
    wait_all(potential_hbm, potential_ref, sems.at[5])


def first(wide, chips, level, pad, shift, coeff, tables, basis, potential):
    rows, columns = coeff.shape
    points = tables.shape[2]
    slots = pad.shape[0]
    inputs = (level, pad, shift, coeff, tables, basis, potential)
    return call(
        functools.partial(first_kernel, wide, chips),
        "forward_first",
        (
            array((points // wide, columns), BF16),
            array((columns, rows), BF16),
            array((rows, points), BF16),
            array((chips, columns, basis.shape[1]), BF16),
            array(potential.shape, F32),
        ),
        [HBM] * 7,
        (VMEM,) * 5,
        [
            pltpu.SMEM((slots,), jnp.int32),
            pltpu.SMEM((slots,), jnp.int32),
            pltpu.SMEM((slots,), jnp.int32),
            pltpu.VMEM(coeff.shape, coeff.dtype),
            pltpu.VMEM(tables.shape, tables.dtype),
            pltpu.SemaphoreType.DMA((6 + chips,)),
        ],
        flops=2 * rows * points // wide * columns,
        moved=4 * MIB,
    )(*(in_hbm(value) for value in inputs))


def chunk_kernel(wide, chips, k, turned_ref, rolled_ref, far_ref, near_ref):
    store_halves(chips, chunk_of(turned_ref, rolled_ref, wide, k), far_ref, near_ref)


def chunk(wide, chips, k, turned, rolled):
    columns, rows = turned.shape
    own = rolled.shape[1] // wide
    return call(
        functools.partial(chunk_kernel, wide, chips, k),
        "forward_chunk",
        halves(own, columns),
        [VMEM] * 2,
        (VMEM,) * 2,
        flops=2 * rows * own * columns * LONG,
        moved=MIB * LONG,
    )(turned, rolled)


def last_kernel(wide, turned_ref, rolled_ref, out_ref):
    out_ref[...] = chunk_of(turned_ref, rolled_ref, wide, 0).T


def last(wide, turned, rolled):
    columns, rows = turned.shape
    own = rolled.shape[1] // wide
    return call(
        functools.partial(last_kernel, wide),
        "forward_own",
        array((own, columns), F32),
        [VMEM] * 2,
        VMEM,
        flops=2 * rows * own * columns,
        moved=MIB,
    )(turned, rolled)


def combine_kernel(chips, first, mine_ref, whole_ref, *refs):
    count = chips // 2
    parts, outs = refs[:-count], refs[-count:]
    chip = lax.axis_index("narrow") // 2
    rows = outs[0].shape[0]
    for i in range(count):
        target = chip ^ (first + i)
        span = pl.ds(pl.multiple_of(target * rows, rows), rows)
        total = mine_ref[span, :] + whole_ref[span, :].astype(F32)
        start = pl.multiple_of((target % count) * rows, rows)
        for part in parts:
            total = total + part[pl.ds(start, rows), :].astype(F32)
        outs[i][...] = total.astype(BF16)


def combine(chips, first, mine, whole, parts):
    rows, columns = mine.shape
    count = chips // 2
    return call(
        functools.partial(combine_kernel, chips, first),
        "wide_sum",
        (array((rows // chips, columns), BF16),) * count,
        [VMEM] * (len(parts) + 2),
        (VMEM,) * count,
        moved=MIB,
    )(mine, whole, *parts)


def own_points_kernel(x_ref, basis_ref, out_ref):
    out_ref[...] = dot(x_ref[...], basis_ref[0])


def own_points(x, where):
    basis, _ = where
    rows = x.shape[0]
    points = basis.shape[2]
    return call(
        own_points_kernel,
        "points_own",
        array((rows, points), F32),
        [VMEM] * 2,
        VMEM,
        flops=2 * rows * points * x.shape[1],
        moved=2 * MIB,
    )(x, basis)


def more_points_kernel(j, total_ref, x_ref, basis_ref, out_ref):
    out_ref[...] = total_ref[...] + dot(x_ref[...], basis_ref[j])


def more_points(total, x, where):
    basis, j = where
    rows, points = total.shape
    return call(
        functools.partial(more_points_kernel, j),
        "points_more",
        array((rows, points), F32),
        [VMEM] * 3,
        VMEM,
        flops=2 * rows * points * x.shape[1],
        moved=2 * MIB,
    )(total, x, basis)


def last_points_kernel(j, total_ref, x_ref, basis_ref, mine_ref, theirs_ref):
    core = lax.axis_index("narrow") % 2
    rows = mine_ref.shape[0]
    total = total_ref[...] + dot(x_ref[...], basis_ref[j])
    low, high = total[:rows], total[rows:]
    mine_ref[...] = jnp.where(core == 0, low, high)
    theirs_ref[...] = jnp.where(core == 0, high, low)


def last_points(total, x, where):
    basis, j = where
    rows, points = total.shape
    half = array((rows // 2, points), F32)
    return call(
        functools.partial(last_points_kernel, j),
        "points_last",
        (half, half),
        [VMEM] * 3,
        (VMEM, VMEM),
        flops=2 * rows * points * x.shape[1],
        moved=2 * MIB,
    )(total, x, basis)


def act_kernel(mine_ref, other_ref, potential_ref, out_ref):
    on_grid = mine_ref[...] + other_ref[...]
    out_ref[...] = (potential_ref[...] * on_grid).astype(BF16)


def act(mine, other, potential):
    return call(
        act_kernel, "act", array(mine.shape, BF16), [VMEM] * 3, VMEM, moved=MIB
    )(mine, other, potential)


def first_functions_kernel(leave, mine_ref, other_ref, basis_ref, *refs):
    outs, both_ref = refs[:-1], refs[-1]
    core = lax.axis_index("narrow") % 2
    rows = mine_ref.shape[0]
    mine, other = mine_ref[...].astype(F32), other_ref[...].astype(F32)
    both_ref[:rows] = jnp.where(core == 0, mine, other).astype(BF16)
    both_ref[rows:] = jnp.where(core == 0, other, mine).astype(BF16)
    for j, out in zip(leave, outs):
        out[...] = dot_turned(both_ref[...], basis_ref[j]).astype(BF16)


def first_functions(leave, mine, other, basis):
    rows, points = mine.shape
    columns = basis.shape[1]
    return call(
        functools.partial(first_functions_kernel, leave),
        "functions_first",
        (array((2 * rows, columns), BF16),) * len(leave) + (array((2 * rows, points), BF16),),
        [VMEM] * 3,
        (VMEM,) * (len(leave) + 1),
    )(mine, other, basis)


def functions_kernel(j, both_ref, basis_ref, out_ref):
    out_ref[...] = dot_turned(both_ref[...], basis_ref[j]).astype(BF16)


def functions(both, where):
    basis, j = where
    rows, points = both.shape
    columns = basis.shape[1]
    return call(
        functools.partial(functions_kernel, j),
        "functions_more",
        array((rows, columns), BF16),
        [VMEM] * 2,
        VMEM,
        flops=2 * rows * points * columns,
        moved=2 * MIB,
    )(both, basis)


def assemble_kernel(*refs):
    parts, out_ref = refs[:-1], refs[-1]
    chip = lax.axis_index("narrow") // 2
    rows = parts[0].shape[0]
    for j, part in enumerate(parts):
        start = pl.multiple_of((chip ^ j) * rows, rows)
        out_ref[pl.ds(start, rows), :] = part[...]


def assemble(parts):
    rows, columns = parts[0].shape
    chips = len(parts)
    return call(
        assemble_kernel,
        "assemble",
        array((rows * chips, columns), BF16),
        [VMEM] * chips,
        VMEM,
        moved=MIB // 4,
    )(*parts)


def own_kernel(wide, pad_ref, rolled_ref, grid_ref, coeff_ref, row_ref, column_ref, out_ref):
    slots = pad_ref.shape[0]
    width = rolled_ref.shape[0] // slots
    me = lax.axis_index("wide")
    own = rolled_ref.shape[1] // wide
    start = pl.multiple_of(me * own, own)
    row = lax.broadcasted_iota(jnp.int32, (width, out_ref.shape[1]), 0)
    group = 4

    def block(i, _):
        base = pl.multiple_of(i * group * width, group * width)
        part = dot(rolled_ref[pl.ds(base, group * width), pl.ds(start, own)], grid_ref[...])
        for s in range(group):
            rows = pl.ds(base + s * width, width)
            energy = row_ref[rows, :] + column_ref[...]
            diagonal = energy * coeff_ref[rows, :].astype(F32)
            live = row < width - pad_ref[i * group + s]
            out_ref[rows, :] = part[s * width : (s + 1) * width] + jnp.where(live, diagonal, 0.0)
        return 0

    lax.fori_loop(0, slots // group, block, 0)


def backward_own(wide, pad, rolled, grid, coeff, row_energy, column_energy):
    smem = pl.BlockSpec(memory_space=pltpu.SMEM)
    rows, columns = coeff.shape
    return call(
        functools.partial(own_kernel, wide),
        "backward_own",
        array(coeff.shape, F32),
        [smem] + [VMEM] * 5,
        VMEM,
        flops=2 * rows * columns * rolled.shape[1] // wide,
        moved=4 * MIB,
    )(pad, rolled, grid, coeff, row_energy[:, None], column_energy[None, :])


def more_kernel(wide, k, total_ref, rolled_ref, grid_ref, out_ref):
    own = rolled_ref.shape[1] // wide
    start = pl.multiple_of((lax.axis_index("wide") ^ k) * own, own)
    count = 256

    def block(i, _):
        rows = pl.ds(pl.multiple_of(i * count, count), count)
        part = dot(rolled_ref[rows, pl.ds(start, own)], grid_ref[...])
        out_ref[rows, :] = total_ref[rows, :] + part
        return 0

    lax.fori_loop(0, rolled_ref.shape[0] // count, block, 0)


def backward_more(wide, k, total, rolled, grid):
    rows, columns = total.shape
    return call(
        functools.partial(more_kernel, wide, k),
        "backward_more",
        array(total.shape, F32),
        [VMEM] * 3,
        VMEM,
        flops=2 * rows * columns * rolled.shape[1] // wide,
        moved=3 * MIB,
    )(total, rolled, grid)


def end_kernel(wide, k, total_ref, rolled_ref, grid_ref, out_hbm, out_ref, sems):
    own = rolled_ref.shape[1] // wide
    start = pl.multiple_of((lax.axis_index("wide") ^ k) * own, own)
    steps = sems.shape[0]
    rows = rolled_ref.shape[0] // steps

    def block(i, _):
        span = pl.ds(pl.multiple_of(i * rows, rows), rows)
        part = dot(rolled_ref[span, pl.ds(start, own)], grid_ref[...])
        out_ref[span, :] = total_ref[span, :] + part
        pltpu.make_async_copy(out_ref.at[span, :], out_hbm.at[span, :], sems.at[i]).start()
        return 0

    lax.fori_loop(0, steps, block, 0)

    def finish(i, _):
        span = pl.ds(pl.multiple_of(i * rows, rows), rows)
        pltpu.make_async_copy(out_ref.at[span, :], out_hbm.at[span, :], sems.at[i]).wait()
        return 0

    lax.fori_loop(0, steps, finish, 0)


def backward_end(wide, k, total, rolled, grid):
    rows, columns = total.shape
    return call(
        functools.partial(end_kernel, wide, k),
        "backward_end",
        array(total.shape, F32),
        [VMEM] * 3,
        HBM,
        [pltpu.VMEM(total.shape, F32), pltpu.SemaphoreType.DMA((8,))],
        flops=2 * rows * columns * rolled.shape[1] // wide,
        moved=4 * MIB,
    )(total, rolled, grid)


def exchange(value, step, size, axis):
    return lax.ppermute(value, axis, [(i, i ^ step) for i in range(size)])


def body(
    wide,
    narrow,
    coeff,
    groupb_row_energy,
    groupa_energy,
    groupb_basis_values,
    basis_a,
    potential,
    slot_sparse_level,
    block_pad,
    slot_grid_offset,
):
    chips = narrow // 2
    tables = jnp.swapaxes(groupb_basis_values, 1, 2)
    half = chips // 2
    order = list(range(1, wide - 1))
    whole, turned, rolled, basis, pot = first(
        wide,
        chips,
        slot_sparse_level,
        block_pad,
        slot_grid_offset,
        coeff,
        tables,
        basis_a,
        potential,
    )
    whole = exchange(whole, wide - 1, wide, "wide")
    where = {j: (basis, j) for j in range(chips)}
    sent = {k: chunk(wide, chips, k, turned, rolled) for k in order}
    far_parts = [exchange(sent[k][0], k, wide, "wide") for k in order]
    near_parts = [exchange(sent[k][1], k, wide, "wide") for k in order]
    mine = last(wide, turned, rolled)
    pieces = combine(chips, half, mine, whole, far_parts)
    xs = {j: exchange(pieces[j - half], 2 * j, narrow, "narrow") for j in range(half, chips)}
    pieces = combine(chips, 0, mine, whole, near_parts)
    for j in range(1, half):
        xs[j] = exchange(pieces[j], 2 * j, narrow, "narrow")
    total = own_points(pieces[0], where[0])
    visits = list(range(half, chips)) + list(range(1, half))
    for j in visits[:-1]:
        total = more_points(total, xs[j], where[j])
    mine, theirs = last_points(total, xs[visits[-1]], where[visits[-1]])
    acted = act(mine, exchange(theirs, 1, narrow, "narrow"), pot)
    other = exchange(acted, 1, narrow, "narrow")
    leave = list(reversed(range(1, chips)))
    *out, both = first_functions(leave, acted, other, basis)
    blocks = {j: exchange(out[i], 2 * j, narrow, "narrow") for i, j in enumerate(leave)}
    grid = assemble([functions(both, where[0])] + [blocks[j] for j in range(1, chips)])
    steps = [wide - 1] + order
    grids = {k: exchange(grid, k, wide, "wide") for k in steps}
    total = backward_own(
        wide, block_pad, rolled, grid, coeff, groupb_row_energy, groupa_energy
    )
    for k in steps[:-1]:
        total = backward_more(wide, k, total, rolled, grids[k])
    return backward_end(wide, steps[-1], total, rolled, grids[steps[-1]])


def solution(mesh):
    return jax.shard_map(
        functools.partial(body, mesh.shape["wide"], mesh.shape["narrow"]),
        mesh=mesh,
        in_specs=(
            P("wide", "narrow"),
            P("wide"),
            P("narrow"),
            P(),
            P(),
            P(("wide", "narrow"), None),
            P("wide"),
            P("wide"),
            P("wide"),
        ),
        out_specs=P("wide", "narrow"),
        check_vma=False,
    )
```

```python
import functools

import jax
import jax.numpy as jnp
from jax import lax
from jax.experimental import pallas as pl
from jax.experimental.pallas import tpu as pltpu
from jax.sharding import PartitionSpec as P

MIB = 1024 * 1024
HBM = pl.BlockSpec(memory_space=pltpu.HBM)
VMEM = pl.BlockSpec(memory_space=pltpu.VMEM)
BF16 = jnp.bfloat16
F32 = jnp.float32
LONG = 8


def call(kernel, name, out_shape, in_specs, out_specs, scratch=(), flops=0, moved=0, mib=16):
    return pl.pallas_call(
        kernel,
        out_shape=out_shape,
        in_specs=in_specs,
        out_specs=out_specs,
        scratch_shapes=scratch,
        compiler_params=pltpu.CompilerParams(vmem_limit_bytes=mib * MIB),
        cost_estimate=pl.CostEstimate(flops=flops, bytes_accessed=moved, transcendentals=0),
        name=name,
    )


def in_hbm(value):
    return pltpu.with_memory_space_constraint(value, pltpu.HBM)


def array(shape, dtype):
    return jax.ShapeDtypeStruct(shape, dtype)


def dot(left, right):
    return jnp.dot(left, right, preferred_element_type=F32)


def dot_turned(left, right):
    return lax.dot_general(left, right, (((1,), (1,)), ((), ())), preferred_element_type=F32)


def chunk_of(turned_ref, rolled_ref, wide, k):
    own = rolled_ref.shape[1] // wide
    start = pl.multiple_of((lax.axis_index("wide") ^ k) * own, own)
    return dot(turned_ref[...], rolled_ref[:, pl.ds(start, own)])


def store_halves(chips, total, far_ref, near_ref):
    upper = lax.axis_index("narrow") // 2 >= chips // 2
    rows = far_ref.shape[0]
    turned = total.astype(BF16).T.astype(F32)
    low, high = turned[:rows], turned[rows:]
    far_ref[...] = jnp.where(upper, low, high).astype(BF16)
    near_ref[...] = jnp.where(upper, high, low).astype(BF16)


def start_pieces(source, target, rows, sem):
    for r in range(0, source.shape[0], rows):
        span = pl.ds(r, rows)
        pltpu.make_async_copy(source.at[span], target.at[span], sem).start()


def wait_all(source, target, sem):
    pltpu.make_async_copy(source, target, sem).wait()


def basis_pieces(basis_hbm, basis_ref):
    chips, columns, _ = basis_ref.shape
    place = lax.axis_index("narrow")
    core, chip = place % 2, place // 2
    pairs = []
    for j in range(chips):
        start = pl.multiple_of(((chip ^ j) * 2 + core) * columns, columns)
        pairs.append((basis_hbm.at[pl.ds(start, columns)], basis_ref.at[j]))
    return pairs


def halves(rows, columns):
    return (array((rows // 2, columns), BF16),) * 2


def first_kernel(
    wide,
    chips,
    level_hbm,
    pad_hbm,
    shift_hbm,
    coeff_hbm,
    table_hbm,
    basis_hbm,
    potential_hbm,
    out_ref,
    turned_ref,
    rolled_ref,
    basis_ref,
    potential_ref,
    level_ref,
    pad_ref,
    shift_ref,
    coeff_ref,
    table_ref,
    sems,
):
    slots = pad_ref.shape[0]
    levels, width, points = table_ref.shape
    small = [
        pltpu.make_async_copy(source, target, sems.at[i])
        for i, (source, target) in enumerate(
            ((level_hbm, level_ref), (shift_hbm, shift_ref), (pad_hbm, pad_ref))
        )
    ]
    for copy in small:
        copy.start()
    for n in range(levels):
        start_pieces(table_hbm.at[n], table_ref.at[n], 32, sems.at[3])
    start_pieces(coeff_hbm, coeff_ref, 128, sems.at[4])
    pairs = basis_pieces(basis_hbm, basis_ref)
    for j, (source, target) in enumerate(pairs):
        start_pieces(source, target, 64, sems.at[6 + j])
    start_pieces(potential_hbm, potential_ref, 8, sems.at[5])
    for copy in small:
        copy.wait()
    wait_all(table_hbm, table_ref, sems.at[3])
    row = lax.broadcasted_iota(jnp.int32, (width, 128), 0)
    for s in range(slots):
        rows = slice(s * width, (s + 1) * width)
        live = jnp.where(row < width - pad_ref[s], 1.0, 0.0).astype(BF16)
        rolled = pltpu.roll(table_ref[level_ref[s]], shift_ref[s], 1)
        for p in range(0, points, 128):
            rolled_ref[rows, p : p + 128] = rolled[:, p : p + 128] * live
    wait_all(coeff_hbm, coeff_ref, sems.at[4])
    turned_ref[...] = coeff_ref[...].T
    out_ref[...] = chunk_of(turned_ref, rolled_ref, wide, wide - 1).astype(BF16).T
    for j, (source, target) in enumerate(pairs):
        wait_all(source, target, sems.at[6 + j])
    wait_all(potential_hbm, potential_ref, sems.at[5])


def first(wide, chips, level, pad, shift, coeff, tables, basis, potential):
    rows, columns = coeff.shape
    points = tables.shape[2]
    slots = pad.shape[0]
    inputs = (level, pad, shift, coeff, tables, basis, potential)
    return call(
        functools.partial(first_kernel, wide, chips),
        "forward_first",
        (
            array((points // wide, columns), BF16),
            array((columns, rows), BF16),
            array((rows, points), BF16),
            array((chips, columns, basis.shape[1]), BF16),
            array(potential.shape, F32),
        ),
        [HBM] * 7,
        (VMEM,) * 5,
        [
            pltpu.SMEM((slots,), jnp.int32),
            pltpu.SMEM((slots,), jnp.int32),
            pltpu.SMEM((slots,), jnp.int32),
            pltpu.VMEM(coeff.shape, coeff.dtype),
            pltpu.VMEM(tables.shape, tables.dtype),
            pltpu.SemaphoreType.DMA((6 + chips,)),
        ],
        flops=2 * rows * points // wide * columns,
        moved=4 * MIB,
    )(*(in_hbm(value) for value in inputs))


def chunk_kernel(wide, chips, k, turned_ref, rolled_ref, far_ref, near_ref):
    store_halves(chips, chunk_of(turned_ref, rolled_ref, wide, k), far_ref, near_ref)


def chunk(wide, chips, k, turned, rolled):
    columns, rows = turned.shape
    own = rolled.shape[1] // wide
    return call(
        functools.partial(chunk_kernel, wide, chips, k),
        "forward_chunk",
        halves(own, columns),
        [VMEM] * 2,
        (VMEM,) * 2,
        flops=2 * rows * own * columns * LONG,
        moved=MIB * LONG,
    )(turned, rolled)


def last_kernel(wide, turned_ref, rolled_ref, out_ref):
    out_ref[...] = chunk_of(turned_ref, rolled_ref, wide, 0).T


def last(wide, turned, rolled):
    columns, rows = turned.shape
    own = rolled.shape[1] // wide
    return call(
        functools.partial(last_kernel, wide),
        "forward_own",
        array((own, columns), F32),
        [VMEM] * 2,
        VMEM,
        flops=2 * rows * own * columns,
        moved=MIB,
    )(turned, rolled)


def combine_kernel(chips, first, mine_ref, whole_ref, *refs):
    count = chips // 2
    parts, outs = refs[:-count], refs[-count:]
    chip = lax.axis_index("narrow") // 2
    rows = outs[0].shape[0]
    for i in range(count):
        target = chip ^ (first + i)
        span = pl.ds(pl.multiple_of(target * rows, rows), rows)
        total = mine_ref[span, :] + whole_ref[span, :].astype(F32)
        start = pl.multiple_of((target % count) * rows, rows)
        for part in parts:
            total = total + part[pl.ds(start, rows), :].astype(F32)
        outs[i][...] = total.astype(BF16)


def combine(chips, first, mine, whole, parts):
    rows, columns = mine.shape
    count = chips // 2
    return call(
        functools.partial(combine_kernel, chips, first),
        "wide_sum",
        (array((rows // chips, columns), BF16),) * count,
        [VMEM] * (len(parts) + 2),
        (VMEM,) * count,
        moved=MIB,
    )(mine, whole, *parts)


def own_points_kernel(x_ref, basis_ref, out_ref):
    out_ref[...] = dot(x_ref[...], basis_ref[0])


def own_points(x, where):
    basis, _ = where
    rows = x.shape[0]
    points = basis.shape[2]
    return call(
        own_points_kernel,
        "points_own",
        array((rows, points), F32),
        [VMEM] * 2,
        VMEM,
        flops=2 * rows * points * x.shape[1],
        moved=2 * MIB,
    )(x, basis)


def more_points_kernel(j, total_ref, x_ref, basis_ref, out_ref):
    out_ref[...] = total_ref[...] + dot(x_ref[...], basis_ref[j])


def more_points(total, x, where):
    basis, j = where
    rows, points = total.shape
    return call(
        functools.partial(more_points_kernel, j),
        "points_more",
        array((rows, points), F32),
        [VMEM] * 3,
        VMEM,
        flops=2 * rows * points * x.shape[1],
        moved=2 * MIB,
    )(total, x, basis)


def last_points_kernel(j, total_ref, x_ref, basis_ref, mine_ref, theirs_ref):
    core = lax.axis_index("narrow") % 2
    rows = mine_ref.shape[0]
    total = total_ref[...] + dot(x_ref[...], basis_ref[j])
    low, high = total[:rows], total[rows:]
    mine_ref[...] = jnp.where(core == 0, low, high)
    theirs_ref[...] = jnp.where(core == 0, high, low)


def last_points(total, x, where):
    basis, j = where
    rows, points = total.shape
    half = array((rows // 2, points), F32)
    return call(
        functools.partial(last_points_kernel, j),
        "points_last",
        (half, half),
        [VMEM] * 3,
        (VMEM, VMEM),
        flops=2 * rows * points * x.shape[1],
        moved=2 * MIB,
    )(total, x, basis)


def act_kernel(mine_ref, other_ref, potential_ref, out_ref):
    on_grid = mine_ref[...] + other_ref[...]
    out_ref[...] = (potential_ref[...] * on_grid).astype(BF16)


def act(mine, other, potential):
    return call(
        act_kernel, "act", array(mine.shape, BF16), [VMEM] * 3, VMEM, moved=MIB
    )(mine, other, potential)


def first_functions_kernel(leave, mine_ref, other_ref, basis_ref, *refs):
    outs, both_ref = refs[:-1], refs[-1]
    core = lax.axis_index("narrow") % 2
    rows = mine_ref.shape[0]
    mine, other = mine_ref[...].astype(F32), other_ref[...].astype(F32)
    both_ref[:rows] = jnp.where(core == 0, mine, other).astype(BF16)
    both_ref[rows:] = jnp.where(core == 0, other, mine).astype(BF16)
    for j, out in zip(leave, outs):
        out[...] = dot_turned(both_ref[...], basis_ref[j]).astype(BF16)


def first_functions(leave, mine, other, basis):
    rows, points = mine.shape
    columns = basis.shape[1]
    return call(
        functools.partial(first_functions_kernel, leave),
        "functions_first",
        (array((2 * rows, columns), BF16),) * len(leave) + (array((2 * rows, points), BF16),),
        [VMEM] * 3,
        (VMEM,) * (len(leave) + 1),
    )(mine, other, basis)


def functions_kernel(j, both_ref, basis_ref, out_ref):
    out_ref[...] = dot_turned(both_ref[...], basis_ref[j]).astype(BF16)


def functions(both, where):
    basis, j = where
    rows, points = both.shape
    columns = basis.shape[1]
    return call(
        functools.partial(functions_kernel, j),
        "functions_more",
        array((rows, columns), BF16),
        [VMEM] * 2,
        VMEM,
        flops=2 * rows * points * columns,
        moved=2 * MIB,
    )(both, basis)


def assemble_kernel(*refs):
    parts, out_ref = refs[:-1], refs[-1]
    chip = lax.axis_index("narrow") // 2
    rows = parts[0].shape[0]
    for j, part in enumerate(parts):
        start = pl.multiple_of((chip ^ j) * rows, rows)
        out_ref[pl.ds(start, rows), :] = part[...]


def assemble(parts):
    rows, columns = parts[0].shape
    chips = len(parts)
    return call(
        assemble_kernel,
        "assemble",
        array((rows * chips, columns), BF16),
        [VMEM] * chips,
        VMEM,
        moved=MIB // 4,
    )(*parts)


def diagonal_kernel(pad_ref, coeff_ref, row_ref, column_ref, out_ref):
    slots = pad_ref.shape[0]
    width = coeff_ref.shape[0] // slots
    row = lax.broadcasted_iota(jnp.int32, (width, out_ref.shape[1]), 0)
    for s in range(slots):
        rows = slice(s * width, (s + 1) * width)
        energy = row_ref[rows, :] + column_ref[...]
        diagonal = energy * coeff_ref[rows, :].astype(F32)
        out_ref[rows, :] = jnp.where(row < width - pad_ref[s], diagonal, 0.0)


def diagonal(pad, coeff, row_energy, column_energy):
    smem = pl.BlockSpec(memory_space=pltpu.SMEM)
    return call(
        diagonal_kernel,
        "diagonal",
        array(coeff.shape, F32),
        [smem] + [VMEM] * 3,
        VMEM,
    )(pad, coeff, row_energy[:, None], column_energy[None, :])


def more_kernel(wide, k, total_ref, rolled_ref, grid_ref, out_ref):
    own = rolled_ref.shape[1] // wide
    start = pl.multiple_of((lax.axis_index("wide") ^ k) * own, own)
    out_ref[...] = total_ref[...] + dot(rolled_ref[:, pl.ds(start, own)], grid_ref[...])


def backward_more(wide, k, total, rolled, grid):
    rows, columns = total.shape
    return call(
        functools.partial(more_kernel, wide, k),
        "backward_more",
        array(total.shape, F32),
        [VMEM] * 3,
        VMEM,
        flops=2 * rows * columns * rolled.shape[1] // wide,
        moved=3 * MIB,
    )(total, rolled, grid)


def end_kernel(wide, k, total_ref, rolled_ref, grid_ref, out_hbm, out_ref, sems):
    own = rolled_ref.shape[1] // wide
    start = pl.multiple_of((lax.axis_index("wide") ^ k) * own, own)
    steps = sems.shape[0]
    rows = rolled_ref.shape[0] // steps
    copies = []
    for i in range(steps):
        span = pl.ds(i * rows, rows)
        part = dot(rolled_ref[span, pl.ds(start, own)], grid_ref[...])
        out_ref[span, :] = total_ref[span, :] + part
        copies.append(pltpu.make_async_copy(out_ref.at[span, :], out_hbm.at[span, :], sems.at[i]))
        copies[-1].start()
    for copy in copies:
        copy.wait()


def backward_end(wide, k, total, rolled, grid):
    rows, columns = total.shape
    return call(
        functools.partial(end_kernel, wide, k),
        "backward_end",
        array(total.shape, F32),
        [VMEM] * 3,
        HBM,
        [pltpu.VMEM(total.shape, F32), pltpu.SemaphoreType.DMA((16,))],
        flops=2 * rows * columns * rolled.shape[1] // wide,
        moved=4 * MIB,
    )(total, rolled, grid)


def exchange(value, step, size, axis):
    return lax.ppermute(value, axis, [(i, i ^ step) for i in range(size)])


def body(
    wide,
    narrow,
    coeff,
    groupb_row_energy,
    groupa_energy,
    groupb_basis_values,
    basis_a,
    potential,
    slot_sparse_level,
    block_pad,
    slot_grid_offset,
):
    chips = narrow // 2
    tables = jnp.swapaxes(groupb_basis_values, 1, 2)
    half = chips // 2
    order = list(range(1, wide - 1))
    whole, turned, rolled, basis, pot = first(
        wide,
        chips,
        slot_sparse_level,
        block_pad,
        slot_grid_offset,
        coeff,
        tables,
        basis_a,
        potential,
    )
    whole = exchange(whole, wide - 1, wide, "wide")
    where = {j: (basis, j) for j in range(chips)}
    sent = {k: chunk(wide, chips, k, turned, rolled) for k in order}
    far_parts = [exchange(sent[k][0], k, wide, "wide") for k in order]
    near_parts = [exchange(sent[k][1], k, wide, "wide") for k in order]
    mine = last(wide, turned, rolled)
    pieces = combine(chips, half, mine, whole, far_parts)
    xs = {j: exchange(pieces[j - half], 2 * j, narrow, "narrow") for j in range(half, chips)}
    pieces = combine(chips, 0, mine, whole, near_parts)
    for j in range(1, half):
        xs[j] = exchange(pieces[j], 2 * j, narrow, "narrow")
    total = own_points(pieces[0], where[0])
    visits = list(range(half, chips)) + list(range(1, half))
    for j in visits[:-1]:
        total = more_points(total, xs[j], where[j])
    mine, theirs = last_points(total, xs[visits[-1]], where[visits[-1]])
    acted = act(mine, exchange(theirs, 1, narrow, "narrow"), pot)
    other = exchange(acted, 1, narrow, "narrow")
    leave = list(reversed(range(1, chips)))
    *out, both = first_functions(leave, acted, other, basis)
    blocks = {j: exchange(out[i], 2 * j, narrow, "narrow") for i, j in enumerate(leave)}
    grid = assemble([functions(both, where[0])] + [blocks[j] for j in range(1, chips)])
    steps = [wide - 1] + order
    grids = {k: exchange(grid, k, wide, "wide") for k in steps}
    total = diagonal(block_pad, coeff, groupb_row_energy, groupa_energy)
    total = backward_more(wide, 0, total, rolled, grid)
    for k in steps[:-1]:
        total = backward_more(wide, k, total, rolled, grids[k])
    return backward_end(wide, steps[-1], total, rolled, grids[steps[-1]])


def solution(mesh):
    return jax.shard_map(
        functools.partial(body, mesh.shape["wide"], mesh.shape["narrow"]),
        mesh=mesh,
        in_specs=(
            P("wide", "narrow"),
            P("wide"),
            P("narrow"),
            P(),
            P(),
            P(("wide", "narrow"), None),
            P("wide"),
            P("wide"),
            P("wide"),
        ),
        out_specs=P("wide", "narrow"),
        check_vma=False,
    )
```

```python
import functools

import jax
import jax.numpy as jnp
from jax import lax
from jax.experimental import pallas as pl
from jax.experimental.pallas import tpu as pltpu
from jax.sharding import PartitionSpec as P

MIB = 1024 * 1024
HBM = pl.BlockSpec(memory_space=pltpu.HBM)
VMEM = pl.BlockSpec(memory_space=pltpu.VMEM)
BF16 = jnp.bfloat16
F32 = jnp.float32
LONG = 8


def call(kernel, name, out_shape, in_specs, out_specs, scratch=(), flops=0, moved=0, mib=16):
    return pl.pallas_call(
        kernel,
        out_shape=out_shape,
        in_specs=in_specs,
        out_specs=out_specs,
        scratch_shapes=scratch,
        compiler_params=pltpu.CompilerParams(vmem_limit_bytes=mib * MIB),
        cost_estimate=pl.CostEstimate(flops=flops, bytes_accessed=moved, transcendentals=0),
        name=name,
    )


def in_hbm(value):
    return pltpu.with_memory_space_constraint(value, pltpu.HBM)


def array(shape, dtype):
    return jax.ShapeDtypeStruct(shape, dtype)


def dot(left, right):
    return jnp.dot(left, right, preferred_element_type=F32)


def dot_turned(left, right):
    return lax.dot_general(left, right, (((1,), (1,)), ((), ())), preferred_element_type=F32)


def chunk_of(turned_ref, rolled_ref, wide, k):
    own = rolled_ref.shape[1] // wide
    start = pl.multiple_of((lax.axis_index("wide") ^ k) * own, own)
    return dot(turned_ref[...], rolled_ref[:, pl.ds(start, own)])


def store_halves(chips, total, far_ref, near_ref):
    upper = lax.axis_index("narrow") // 2 >= chips // 2
    rows = far_ref.shape[0]
    turned = total.astype(BF16).T.astype(F32)
    low, high = turned[:rows], turned[rows:]
    far_ref[...] = jnp.where(upper, low, high).astype(BF16)
    near_ref[...] = jnp.where(upper, high, low).astype(BF16)


def start_pieces(source, target, rows, sem):
    for r in range(0, source.shape[0], rows):
        span = pl.ds(r, rows)
        pltpu.make_async_copy(source.at[span], target.at[span], sem).start()


def wait_all(source, target, sem):
    pltpu.make_async_copy(source, target, sem).wait()


def basis_pieces(first, basis_hbm, basis_ref):
    count, columns, _ = basis_ref.shape
    place = lax.axis_index("narrow")
    core, chip = place % 2, place // 2
    pairs = []
    for j in range(count):
        start = pl.multiple_of(((chip ^ (first + j)) * 2 + core) * columns, columns)
        pairs.append((basis_hbm.at[pl.ds(start, columns)], basis_ref.at[j]))
    return pairs


def halves(rows, columns):
    return (array((rows // 2, columns), BF16),) * 2


def first_kernel(
    wide,
    chips,
    level_hbm,
    pad_hbm,
    shift_hbm,
    coeff_hbm,
    table_hbm,
    basis_hbm,
    potential_hbm,
    out_ref,
    turned_ref,
    rolled_ref,
    basis_ref,
    potential_ref,
    level_ref,
    pad_ref,
    shift_ref,
    coeff_ref,
    table_ref,
    sems,
):
    slots = pad_ref.shape[0]
    levels, width, points = table_ref.shape
    small = [
        pltpu.make_async_copy(source, target, sems.at[i])
        for i, (source, target) in enumerate(
            ((level_hbm, level_ref), (shift_hbm, shift_ref), (pad_hbm, pad_ref))
        )
    ]
    for copy in small:
        copy.start()
    for n in range(levels):
        start_pieces(table_hbm.at[n], table_ref.at[n], 32, sems.at[3])
    start_pieces(coeff_hbm, coeff_ref, 128, sems.at[4])
    pairs = basis_pieces(0, basis_hbm, basis_ref)
    for j, (source, target) in enumerate(pairs):
        start_pieces(source, target, 64, sems.at[6 + j])
    start_pieces(potential_hbm, potential_ref, 8, sems.at[5])
    for copy in small:
        copy.wait()
    wait_all(table_hbm, table_ref, sems.at[3])
    row = lax.broadcasted_iota(jnp.int32, (width, 128), 0)
    for s in range(slots):
        rows = slice(s * width, (s + 1) * width)
        live = jnp.where(row < width - pad_ref[s], 1.0, 0.0).astype(BF16)
        rolled = pltpu.roll(table_ref[level_ref[s]], shift_ref[s], 1)
        for p in range(0, points, 128):
            rolled_ref[rows, p : p + 128] = rolled[:, p : p + 128] * live
    wait_all(coeff_hbm, coeff_ref, sems.at[4])
    turned_ref[...] = coeff_ref[...].T
    out_ref[...] = chunk_of(turned_ref, rolled_ref, wide, wide - 1).astype(BF16).T
    for j, (source, target) in enumerate(pairs):
        wait_all(source, target, sems.at[6 + j])
    wait_all(potential_hbm, potential_ref, sems.at[5])


def first(wide, chips, level, pad, shift, coeff, tables, basis, potential):
    rows, columns = coeff.shape
    points = tables.shape[2]
    slots = pad.shape[0]
    inputs = (level, pad, shift, coeff, tables, basis, potential)
    return call(
        functools.partial(first_kernel, wide, chips),
        "forward_first",
        (
            array((points // wide, columns), BF16),
            array((columns, rows), BF16),
            array((rows, points), BF16),
            array((chips // 2, columns, basis.shape[1]), BF16),
            array(potential.shape, F32),
        ),
        [HBM] * 7,
        (VMEM,) * 5,
        [
            pltpu.SMEM((slots,), jnp.int32),
            pltpu.SMEM((slots,), jnp.int32),
            pltpu.SMEM((slots,), jnp.int32),
            pltpu.VMEM(coeff.shape, coeff.dtype),
            pltpu.VMEM(tables.shape, tables.dtype),
            pltpu.SemaphoreType.DMA((6 + chips,)),
        ],
        flops=2 * rows * points // wide * columns,
        moved=4 * MIB,
    )(*(in_hbm(value) for value in inputs))


def chunk_kernel(wide, chips, k, turned_ref, rolled_ref, far_ref, near_ref):
    store_halves(chips, chunk_of(turned_ref, rolled_ref, wide, k), far_ref, near_ref)


def chunk(wide, chips, k, turned, rolled):
    columns, rows = turned.shape
    own = rolled.shape[1] // wide
    return call(
        functools.partial(chunk_kernel, wide, chips, k),
        "forward_chunk",
        halves(own, columns),
        [VMEM] * 2,
        (VMEM,) * 2,
        flops=2 * rows * own * columns * LONG,
        moved=MIB * LONG,
    )(turned, rolled)


def last_kernel(wide, turned_ref, rolled_ref, basis_hbm, out_ref, basis_ref, sems):
    count = basis_ref.shape[0]
    pairs = basis_pieces(count, basis_hbm, basis_ref)
    for j, (source, target) in enumerate(pairs):
        start_pieces(source, target, 64, sems.at[j])
    out_ref[...] = chunk_of(turned_ref, rolled_ref, wide, 0).T
    for j, (source, target) in enumerate(pairs):
        wait_all(source, target, sems.at[j])


def last(wide, chips, turned, rolled, basis):
    columns, rows = turned.shape
    own = rolled.shape[1] // wide
    count = chips - chips // 2
    return call(
        functools.partial(last_kernel, wide),
        "forward_own",
        (array((own, columns), F32), array((count, columns, basis.shape[1]), BF16)),
        [VMEM, VMEM, HBM],
        (VMEM,) * 2,
        [pltpu.SemaphoreType.DMA((count,))],
    )(turned, rolled, in_hbm(basis))


def combine_kernel(chips, first, mine_ref, whole_ref, *refs):
    count = chips // 2
    parts, outs = refs[:-count], refs[-count:]
    chip = lax.axis_index("narrow") // 2
    rows = outs[0].shape[0]
    for i in range(count):
        target = chip ^ (first + i)
        span = pl.ds(pl.multiple_of(target * rows, rows), rows)
        total = mine_ref[span, :] + whole_ref[span, :].astype(F32)
        start = pl.multiple_of((target % count) * rows, rows)
        for part in parts:
            total = total + part[pl.ds(start, rows), :].astype(F32)
        outs[i][...] = total.astype(BF16)


def combine(chips, first, mine, whole, parts):
    rows, columns = mine.shape
    count = chips // 2
    return call(
        functools.partial(combine_kernel, chips, first),
        "wide_sum",
        (array((rows // chips, columns), BF16),) * count,
        [VMEM] * (len(parts) + 2),
        (VMEM,) * count,
        moved=MIB,
    )(mine, whole, *parts)


def own_points_kernel(x_ref, basis_ref, out_ref):
    out_ref[...] = dot(x_ref[...], basis_ref[0])


def own_points(x, where):
    basis, _ = where
    rows = x.shape[0]
    points = basis.shape[2]
    return call(
        own_points_kernel,
        "points_own",
        array((rows, points), F32),
        [VMEM] * 2,
        VMEM,
        flops=2 * rows * points * x.shape[1],
        moved=2 * MIB,
    )(x, basis)


def more_points_kernel(j, total_ref, x_ref, basis_ref, out_ref):
    out_ref[...] = total_ref[...] + dot(x_ref[...], basis_ref[j])


def more_points(total, x, where):
    basis, j = where
    rows, points = total.shape
    return call(
        functools.partial(more_points_kernel, j),
        "points_more",
        array((rows, points), F32),
        [VMEM] * 3,
        VMEM,
        flops=2 * rows * points * x.shape[1],
        moved=2 * MIB,
    )(total, x, basis)


def last_points_kernel(j, total_ref, x_ref, basis_ref, mine_ref, theirs_ref):
    core = lax.axis_index("narrow") % 2
    rows = mine_ref.shape[0]
    total = total_ref[...] + dot(x_ref[...], basis_ref[j])
    low, high = total[:rows], total[rows:]
    mine_ref[...] = jnp.where(core == 0, low, high)
    theirs_ref[...] = jnp.where(core == 0, high, low)


def last_points(total, x, where):
    basis, j = where
    rows, points = total.shape
    half = array((rows // 2, points), F32)
    return call(
        functools.partial(last_points_kernel, j),
        "points_last",
        (half, half),
        [VMEM] * 3,
        (VMEM, VMEM),
        flops=2 * rows * points * x.shape[1],
        moved=2 * MIB,
    )(total, x, basis)


def act_kernel(mine_ref, other_ref, potential_ref, out_ref):
    on_grid = mine_ref[...] + other_ref[...]
    out_ref[...] = (potential_ref[...] * on_grid).astype(BF16)


def act(mine, other, potential):
    return call(
        act_kernel, "act", array(mine.shape, BF16), [VMEM] * 3, VMEM, moved=MIB
    )(mine, other, potential)


def first_functions_kernel(leave, mine_ref, other_ref, basis_ref, more_ref, *refs):
    outs, both_ref = refs[:-1], refs[-1]
    core = lax.axis_index("narrow") % 2
    rows = mine_ref.shape[0]
    mine, other = mine_ref[...].astype(F32), other_ref[...].astype(F32)
    both_ref[:rows] = jnp.where(core == 0, mine, other).astype(BF16)
    both_ref[rows:] = jnp.where(core == 0, other, mine).astype(BF16)
    for j, out in zip(leave, outs):
        half = basis_ref.shape[0]
        block = basis_ref[j] if j < half else more_ref[j - half]
        out[...] = dot_turned(both_ref[...], block).astype(BF16)


def first_functions(leave, mine, other, basis, more):
    rows, points = mine.shape
    columns = basis.shape[1]
    return call(
        functools.partial(first_functions_kernel, leave),
        "functions_first",
        (array((2 * rows, columns), BF16),) * len(leave) + (array((2 * rows, points), BF16),),
        [VMEM] * 4,
        (VMEM,) * (len(leave) + 1),
    )(mine, other, basis, more)


def functions_kernel(j, both_ref, basis_ref, out_ref):
    out_ref[...] = dot_turned(both_ref[...], basis_ref[j]).astype(BF16)


def functions(both, where):
    basis, j = where
    rows, points = both.shape
    columns = basis.shape[1]
    return call(
        functools.partial(functions_kernel, j),
        "functions_more",
        array((rows, columns), BF16),
        [VMEM] * 2,
        VMEM,
        flops=2 * rows * points * columns,
        moved=2 * MIB,
    )(both, basis)


def assemble_kernel(*refs):
    parts, out_ref = refs[:-1], refs[-1]
    chip = lax.axis_index("narrow") // 2
    rows = parts[0].shape[0]
    for j, part in enumerate(parts):
        start = pl.multiple_of((chip ^ j) * rows, rows)
        out_ref[pl.ds(start, rows), :] = part[...]


def assemble(parts):
    rows, columns = parts[0].shape
    chips = len(parts)
    return call(
        assemble_kernel,
        "assemble",
        array((rows * chips, columns), BF16),
        [VMEM] * chips,
        VMEM,
        moved=MIB // 4,
    )(*parts)


def diagonal_kernel(pad_ref, coeff_ref, row_ref, column_ref, out_ref):
    slots = pad_ref.shape[0]
    width = coeff_ref.shape[0] // slots
    row = lax.broadcasted_iota(jnp.int32, (width, out_ref.shape[1]), 0)
    for s in range(slots):
        rows = slice(s * width, (s + 1) * width)
        energy = row_ref[rows, :] + column_ref[...]
        diagonal = energy * coeff_ref[rows, :].astype(F32)
        out_ref[rows, :] = jnp.where(row < width - pad_ref[s], diagonal, 0.0)


def diagonal(pad, coeff, row_energy, column_energy):
    smem = pl.BlockSpec(memory_space=pltpu.SMEM)
    return call(
        diagonal_kernel,
        "diagonal",
        array(coeff.shape, F32),
        [smem] + [VMEM] * 3,
        VMEM,
    )(pad, coeff, row_energy[:, None], column_energy[None, :])


def more_kernel(wide, k, total_ref, rolled_ref, grid_ref, out_ref):
    own = rolled_ref.shape[1] // wide
    start = pl.multiple_of((lax.axis_index("wide") ^ k) * own, own)
    out_ref[...] = total_ref[...] + dot(rolled_ref[:, pl.ds(start, own)], grid_ref[...])


def backward_more(wide, k, total, rolled, grid):
    rows, columns = total.shape
    return call(
        functools.partial(more_kernel, wide, k),
        "backward_more",
        array(total.shape, F32),
        [VMEM] * 3,
        VMEM,
        flops=2 * rows * columns * rolled.shape[1] // wide,
        moved=3 * MIB,
    )(total, rolled, grid)


def end_kernel(wide, k, total_ref, rolled_ref, grid_ref, out_hbm, out_ref, sems):
    own = rolled_ref.shape[1] // wide
    start = pl.multiple_of((lax.axis_index("wide") ^ k) * own, own)
    steps = sems.shape[0]
    rows = rolled_ref.shape[0] // steps
    copies = []
    for i in range(steps):
        span = pl.ds(i * rows, rows)
        part = dot(rolled_ref[span, pl.ds(start, own)], grid_ref[...])
        out_ref[span, :] = total_ref[span, :] + part
        copies.append(pltpu.make_async_copy(out_ref.at[span, :], out_hbm.at[span, :], sems.at[i]))
        copies[-1].start()
    for copy in copies:
        copy.wait()


def backward_end(wide, k, total, rolled, grid):
    rows, columns = total.shape
    return call(
        functools.partial(end_kernel, wide, k),
        "backward_end",
        array(total.shape, F32),
        [VMEM] * 3,
        HBM,
        [pltpu.VMEM(total.shape, F32), pltpu.SemaphoreType.DMA((8,))],
        flops=2 * rows * columns * rolled.shape[1] // wide,
        moved=4 * MIB,
    )(total, rolled, grid)


def exchange(value, step, size, axis):
    moved = lax.ppermute(value, axis, [(i, i ^ step) for i in range(size)])
    return pltpu.with_memory_space_constraint(moved, pltpu.VMEM)


def body(
    wide,
    narrow,
    coeff,
    groupb_row_energy,
    groupa_energy,
    groupb_basis_values,
    basis_a,
    potential,
    slot_sparse_level,
    block_pad,
    slot_grid_offset,
):
    chips = narrow // 2
    tables = jnp.swapaxes(groupb_basis_values, 1, 2)
    half = chips // 2
    order = list(range(1, wide - 1))
    whole, turned, rolled, basis, pot = first(
        wide,
        chips,
        slot_sparse_level,
        block_pad,
        slot_grid_offset,
        coeff,
        tables,
        basis_a,
        potential,
    )
    whole = exchange(whole, wide - 1, wide, "wide")
    sent = {k: chunk(wide, chips, k, turned, rolled) for k in order}
    far_parts = [exchange(sent[k][0], k, wide, "wide") for k in order]
    near_parts = [exchange(sent[k][1], k, wide, "wide") for k in order]
    mine, more = last(wide, chips, turned, rolled, basis_a)
    where = {j: (basis, j) if j < half else (more, j - half) for j in range(chips)}
    pieces = combine(chips, half, mine, whole, far_parts)
    xs = {j: exchange(pieces[j - half], 2 * j, narrow, "narrow") for j in range(half, chips)}
    pieces = combine(chips, 0, mine, whole, near_parts)
    for j in range(1, half):
        xs[j] = exchange(pieces[j], 2 * j, narrow, "narrow")
    total = own_points(pieces[0], where[0])
    visits = list(range(half, chips)) + list(range(1, half))
    for j in visits[:-1]:
        total = more_points(total, xs[j], where[j])
    mine, theirs = last_points(total, xs[visits[-1]], where[visits[-1]])
    acted = act(mine, exchange(theirs, 1, narrow, "narrow"), pot)
    other = exchange(acted, 1, narrow, "narrow")
    leave = list(reversed(range(1, chips)))
    *out, both = first_functions(leave, acted, other, basis, more)
    blocks = {j: exchange(out[i], 2 * j, narrow, "narrow") for i, j in enumerate(leave)}
    grid = assemble([functions(both, where[0])] + [blocks[j] for j in range(1, chips)])
    steps = [wide - 1] + order
    grids = {k: exchange(grid, k, wide, "wide") for k in steps}
    total = diagonal(block_pad, coeff, groupb_row_energy, groupa_energy)
    total = backward_more(wide, 0, total, rolled, grid)
    for k in steps[:-1]:
        total = backward_more(wide, k, total, rolled, grids[k])
    return backward_end(wide, steps[-1], total, rolled, grids[steps[-1]])


def solution(mesh):
    return jax.shard_map(
        functools.partial(body, mesh.shape["wide"], mesh.shape["narrow"]),
        mesh=mesh,
        in_specs=(
            P("wide", "narrow"),
            P("wide"),
            P("narrow"),
            P(),
            P(),
            P(("wide", "narrow"), None),
            P("wide"),
            P("wide"),
            P("wide"),
        ),
        out_specs=P("wide", "narrow"),
        check_vma=False,
    )
```

```python
import functools

import jax
import jax.numpy as jnp
from jax import lax
from jax.experimental import pallas as pl
from jax.experimental.pallas import tpu as pltpu
from jax.sharding import PartitionSpec as P

MIB = 1024 * 1024
HBM = pl.BlockSpec(memory_space=pltpu.HBM)
VMEM = pl.BlockSpec(memory_space=pltpu.VMEM)
BF16 = jnp.bfloat16
F32 = jnp.float32
LONG = 8


def call(kernel, name, out_shape, in_specs, out_specs, scratch=(), flops=0, moved=0, mib=16):
    return pl.pallas_call(
        kernel,
        out_shape=out_shape,
        in_specs=in_specs,
        out_specs=out_specs,
        scratch_shapes=scratch,
        compiler_params=pltpu.CompilerParams(vmem_limit_bytes=mib * MIB),
        cost_estimate=pl.CostEstimate(flops=flops, bytes_accessed=moved, transcendentals=0),
        name=name,
    )


def in_hbm(value):
    return pltpu.with_memory_space_constraint(value, pltpu.HBM)


def array(shape, dtype):
    return jax.ShapeDtypeStruct(shape, dtype)


def dot(left, right):
    return jnp.dot(left, right, preferred_element_type=F32)


def dot_turned(left, right):
    return lax.dot_general(left, right, (((1,), (1,)), ((), ())), preferred_element_type=F32)


def chunk_of(turned_ref, rolled_ref, wide, k):
    own = rolled_ref.shape[1] // wide
    start = pl.multiple_of((lax.axis_index("wide") ^ k) * own, own)
    return dot(turned_ref[...], rolled_ref[:, pl.ds(start, own)])


def store_halves(chips, total, far_ref, near_ref):
    upper = lax.axis_index("narrow") // 2 >= chips // 2
    rows = far_ref.shape[0]
    turned = total.astype(BF16).T.astype(F32)
    low, high = turned[:rows], turned[rows:]
    far_ref[...] = jnp.where(upper, low, high).astype(BF16)
    near_ref[...] = jnp.where(upper, high, low).astype(BF16)


def start_pieces(source, target, rows, sem):
    for r in range(0, source.shape[0], rows):
        span = pl.ds(r, rows)
        pltpu.make_async_copy(source.at[span], target.at[span], sem).start()


def wait_all(source, target, sem):
    pltpu.make_async_copy(source, target, sem).wait()


def basis_pieces(first, basis_hbm, basis_ref):
    count, columns, _ = basis_ref.shape
    place = lax.axis_index("narrow")
    core, chip = place % 2, place // 2
    pairs = []
    for j in range(count):
        start = pl.multiple_of(((chip ^ (first + j)) * 2 + core) * columns, columns)
        pairs.append((basis_hbm.at[pl.ds(start, columns)], basis_ref.at[j]))
    return pairs


def halves(rows, columns):
    return (array((rows // 2, columns), BF16),) * 2


def first_kernel(
    wide,
    chips,
    level_hbm,
    pad_hbm,
    shift_hbm,
    coeff_hbm,
    table_hbm,
    basis_hbm,
    potential_hbm,
    out_ref,
    turned_ref,
    rolled_ref,
    basis_ref,
    potential_ref,
    level_ref,
    pad_ref,
    shift_ref,
    coeff_ref,
    table_ref,
    sems,
):
    slots = pad_ref.shape[0]
    levels, width, points = table_ref.shape
    small = [
        pltpu.make_async_copy(source, target, sems.at[i])
        for i, (source, target) in enumerate(
            ((level_hbm, level_ref), (shift_hbm, shift_ref), (pad_hbm, pad_ref))
        )
    ]
    for copy in small:
        copy.start()
    for n in range(levels):
        start_pieces(table_hbm.at[n], table_ref.at[n], 32, sems.at[3])
    start_pieces(coeff_hbm, coeff_ref, 128, sems.at[4])
    pairs = basis_pieces(0, basis_hbm, basis_ref)
    for j, (source, target) in enumerate(pairs):
        start_pieces(source, target, 64, sems.at[6 + j])
    start_pieces(potential_hbm, potential_ref, 8, sems.at[5])
    for copy in small:
        copy.wait()
    wait_all(table_hbm, table_ref, sems.at[3])
    row = lax.broadcasted_iota(jnp.int32, (width, 128), 0)
    for s in range(slots):
        rows = slice(s * width, (s + 1) * width)
        live = jnp.where(row < width - pad_ref[s], 1.0, 0.0).astype(BF16)
        rolled = pltpu.roll(table_ref[level_ref[s]], shift_ref[s], 1)
        for p in range(0, points, 128):
            rolled_ref[rows, p : p + 128] = rolled[:, p : p + 128] * live
    wait_all(coeff_hbm, coeff_ref, sems.at[4])
    turned_ref[...] = coeff_ref[...].T
    out_ref[...] = chunk_of(turned_ref, rolled_ref, wide, wide - 1).astype(BF16).T
    for j, (source, target) in enumerate(pairs):
        wait_all(source, target, sems.at[6 + j])
    wait_all(potential_hbm, potential_ref, sems.at[5])


def first(wide, chips, level, pad, shift, coeff, tables, basis, potential):
    rows, columns = coeff.shape
    points = tables.shape[2]
    slots = pad.shape[0]
    inputs = (level, pad, shift, coeff, tables, basis, potential)
    return call(
        functools.partial(first_kernel, wide, chips),
        "forward_first",
        (
            array((points // wide, columns), BF16),
            array((columns, rows), BF16),
            array((rows, points), BF16),
            array((chips // 2, columns, basis.shape[1]), BF16),
            array(potential.shape, F32),
        ),
        [HBM] * 7,
        (VMEM,) * 5,
        [
            pltpu.SMEM((slots,), jnp.int32),
            pltpu.SMEM((slots,), jnp.int32),
            pltpu.SMEM((slots,), jnp.int32),
            pltpu.VMEM(coeff.shape, coeff.dtype),
            pltpu.VMEM(tables.shape, tables.dtype),
            pltpu.SemaphoreType.DMA((6 + chips,)),
        ],
        flops=2 * rows * points // wide * columns,
        moved=4 * MIB,
    )(*(in_hbm(value) for value in inputs))


def chunk_kernel(wide, chips, k, turned_ref, rolled_ref, far_ref, near_ref):
    store_halves(chips, chunk_of(turned_ref, rolled_ref, wide, k), far_ref, near_ref)


def chunk(wide, chips, k, turned, rolled):
    columns, rows = turned.shape
    own = rolled.shape[1] // wide
    return call(
        functools.partial(chunk_kernel, wide, chips, k),
        "forward_chunk",
        halves(own, columns),
        [VMEM] * 2,
        (VMEM,) * 2,
        flops=2 * rows * own * columns * LONG,
        moved=MIB * LONG,
    )(turned, rolled)


def last_kernel(wide, turned_ref, rolled_ref, basis_hbm, out_ref, basis_ref, sems):
    count = basis_ref.shape[0]
    pairs = basis_pieces(count, basis_hbm, basis_ref)
    for j, (source, target) in enumerate(pairs):
        start_pieces(source, target, 64, sems.at[j])
    out_ref[...] = chunk_of(turned_ref, rolled_ref, wide, 0).T
    for j, (source, target) in enumerate(pairs):
        wait_all(source, target, sems.at[j])


def last(wide, chips, turned, rolled, basis):
    columns, rows = turned.shape
    own = rolled.shape[1] // wide
    count = chips - chips // 2
    return call(
        functools.partial(last_kernel, wide),
        "forward_own",
        (array((own, columns), F32), array((count, columns, basis.shape[1]), BF16)),
        [VMEM, VMEM, HBM],
        (VMEM,) * 2,
        [pltpu.SemaphoreType.DMA((count,))],
    )(turned, rolled, in_hbm(basis))


def combine_kernel(chips, first, mine_ref, whole_ref, *refs):
    count = chips // 2
    parts, outs = refs[:-count], refs[-count:]
    chip = lax.axis_index("narrow") // 2
    rows = outs[0].shape[0]
    for i in range(count):
        target = chip ^ (first + i)
        span = pl.ds(pl.multiple_of(target * rows, rows), rows)
        total = mine_ref[span, :] + whole_ref[span, :].astype(F32)
        start = pl.multiple_of((target % count) * rows, rows)
        for part in parts:
            total = total + part[pl.ds(start, rows), :].astype(F32)
        outs[i][...] = total.astype(BF16)


def combine(chips, first, mine, whole, parts):
    rows, columns = mine.shape
    count = chips // 2
    return call(
        functools.partial(combine_kernel, chips, first),
        "wide_sum",
        (array((rows // chips, columns), BF16),) * count,
        [VMEM] * (len(parts) + 2),
        (VMEM,) * count,
        moved=MIB,
    )(mine, whole, *parts)


def own_points_kernel(x_ref, basis_ref, out_ref):
    out_ref[...] = dot(x_ref[...], basis_ref[0])


def own_points(x, where):
    basis, _ = where
    rows = x.shape[0]
    points = basis.shape[2]
    return call(
        own_points_kernel,
        "points_own",
        array((rows, points), F32),
        [VMEM] * 2,
        VMEM,
        flops=2 * rows * points * x.shape[1],
        moved=2 * MIB,
    )(x, basis)


def more_points_kernel(j, total_ref, x_ref, basis_ref, out_ref):
    out_ref[...] = total_ref[...] + dot(x_ref[...], basis_ref[j])


def more_points(total, x, where):
    basis, j = where
    rows, points = total.shape
    return call(
        functools.partial(more_points_kernel, j),
        "points_more",
        array((rows, points), F32),
        [VMEM] * 3,
        VMEM,
        flops=2 * rows * points * x.shape[1],
        moved=2 * MIB,
    )(total, x, basis)


def last_points_kernel(j, total_ref, x_ref, basis_ref, mine_ref, theirs_ref):
    core = lax.axis_index("narrow") % 2
    rows = mine_ref.shape[0]
    total = total_ref[...] + dot(x_ref[...], basis_ref[j])
    low, high = total[:rows], total[rows:]
    mine_ref[...] = jnp.where(core == 0, low, high)
    theirs_ref[...] = jnp.where(core == 0, high, low)


def last_points(total, x, where):
    basis, j = where
    rows, points = total.shape
    half = array((rows // 2, points), F32)
    return call(
        functools.partial(last_points_kernel, j),
        "points_last",
        (half, half),
        [VMEM] * 3,
        (VMEM, VMEM),
        flops=2 * rows * points * x.shape[1],
        moved=2 * MIB,
    )(total, x, basis)


def act_kernel(mine_ref, other_ref, potential_ref, out_ref):
    on_grid = mine_ref[...] + other_ref[...]
    out_ref[...] = (potential_ref[...] * on_grid).astype(BF16)


def act(mine, other, potential):
    return call(
        act_kernel, "act", array(mine.shape, BF16), [VMEM] * 3, VMEM, moved=MIB
    )(mine, other, potential)


def first_functions_kernel(leave, mine_ref, other_ref, basis_ref, more_ref, *refs):
    outs, both_ref = refs[:-1], refs[-1]
    core = lax.axis_index("narrow") % 2
    rows = mine_ref.shape[0]
    mine, other = mine_ref[...].astype(F32), other_ref[...].astype(F32)
    both_ref[:rows] = jnp.where(core == 0, mine, other).astype(BF16)
    both_ref[rows:] = jnp.where(core == 0, other, mine).astype(BF16)
    for j, out in zip(leave, outs):
        half = basis_ref.shape[0]
        block = basis_ref[j] if j < half else more_ref[j - half]
        out[...] = dot_turned(both_ref[...], block).astype(BF16)


def first_functions(leave, mine, other, basis, more):
    rows, points = mine.shape
    columns = basis.shape[1]
    return call(
        functools.partial(first_functions_kernel, leave),
        "functions_first",
        (array((2 * rows, columns), BF16),) * len(leave) + (array((2 * rows, points), BF16),),
        [VMEM] * 4,
        (VMEM,) * (len(leave) + 1),
    )(mine, other, basis, more)


def functions_kernel(j, both_ref, basis_ref, out_ref):
    out_ref[...] = dot_turned(both_ref[...], basis_ref[j]).astype(BF16)


def functions(both, where):
    basis, j = where
    rows, points = both.shape
    columns = basis.shape[1]
    return call(
        functools.partial(functions_kernel, j),
        "functions_more",
        array((rows, columns), BF16),
        [VMEM] * 2,
        VMEM,
        flops=2 * rows * points * columns,
        moved=2 * MIB,
    )(both, basis)


def assemble_kernel(count, *refs):
    parts, outs = refs[:count], refs[count:]
    chip = lax.axis_index("narrow") // 2
    rows = parts[0].shape[0]
    for j, part in enumerate(parts):
        span = pl.ds(pl.multiple_of((chip ^ j) * rows, rows), rows)
        for out in outs:
            out[span, :] = part[...]


def assemble(copies, parts):
    rows, columns = parts[0].shape
    chips = len(parts)
    return call(
        functools.partial(assemble_kernel, chips),
        "assemble",
        (array((rows * chips, columns), BF16),) * copies,
        [VMEM] * chips,
        (VMEM,) * copies,
    )(*parts)


def diagonal_kernel(pad_ref, coeff_ref, row_ref, column_ref, out_ref):
    slots = pad_ref.shape[0]
    width = coeff_ref.shape[0] // slots
    row = lax.broadcasted_iota(jnp.int32, (width, out_ref.shape[1]), 0)
    for s in range(slots):
        rows = slice(s * width, (s + 1) * width)
        energy = row_ref[rows, :] + column_ref[...]
        diagonal = energy * coeff_ref[rows, :].astype(F32)
        out_ref[rows, :] = jnp.where(row < width - pad_ref[s], diagonal, 0.0)


def diagonal(pad, coeff, row_energy, column_energy):
    smem = pl.BlockSpec(memory_space=pltpu.SMEM)
    return call(
        diagonal_kernel,
        "diagonal",
        array(coeff.shape, F32),
        [smem] + [VMEM] * 3,
        VMEM,
    )(pad, coeff, row_energy[:, None], column_energy[None, :])


def more_kernel(wide, k, total_ref, rolled_ref, grid_ref, out_ref):
    own = rolled_ref.shape[1] // wide
    start = pl.multiple_of((lax.axis_index("wide") ^ k) * own, own)
    out_ref[...] = total_ref[...] + dot(rolled_ref[:, pl.ds(start, own)], grid_ref[...])


def backward_more(wide, k, total, rolled, grid):
    rows, columns = total.shape
    return call(
        functools.partial(more_kernel, wide, k),
        "backward_more",
        array(total.shape, F32),
        [VMEM] * 3,
        VMEM,
        flops=2 * rows * columns * rolled.shape[1] // wide,
        moved=3 * MIB,
    )(total, rolled, grid)


def end_kernel(wide, k, total_ref, rolled_ref, grid_ref, out_hbm, out_ref, sems):
    own = rolled_ref.shape[1] // wide
    start = pl.multiple_of((lax.axis_index("wide") ^ k) * own, own)
    steps = sems.shape[0]
    rows = rolled_ref.shape[0] // steps
    copies = []
    for i in range(steps):
        span = pl.ds(i * rows, rows)
        part = dot(rolled_ref[span, pl.ds(start, own)], grid_ref[...])
        out_ref[span, :] = total_ref[span, :] + part
        copies.append(pltpu.make_async_copy(out_ref.at[span, :], out_hbm.at[span, :], sems.at[i]))
        copies[-1].start()
    for copy in copies:
        copy.wait()


def backward_end(wide, k, total, rolled, grid):
    rows, columns = total.shape
    return call(
        functools.partial(end_kernel, wide, k),
        "backward_end",
        array(total.shape, F32),
        [VMEM] * 3,
        HBM,
        [pltpu.VMEM(total.shape, F32), pltpu.SemaphoreType.DMA((8,))],
        flops=2 * rows * columns * rolled.shape[1] // wide,
        moved=4 * MIB,
    )(total, rolled, grid)


def exchange(value, step, size, axis):
    return lax.ppermute(value, axis, [(i, i ^ step) for i in range(size)])


def body(
    wide,
    narrow,
    coeff,
    groupb_row_energy,
    groupa_energy,
    groupb_basis_values,
    basis_a,
    potential,
    slot_sparse_level,
    block_pad,
    slot_grid_offset,
):
    chips = narrow // 2
    tables = jnp.swapaxes(groupb_basis_values, 1, 2)
    half = chips // 2
    order = list(range(1, wide - 1))
    whole, turned, rolled, basis, pot = first(
        wide,
        chips,
        slot_sparse_level,
        block_pad,
        slot_grid_offset,
        coeff,
        tables,
        basis_a,
        potential,
    )
    whole = exchange(whole, wide - 1, wide, "wide")
    sent = {k: chunk(wide, chips, k, turned, rolled) for k in order}
    far_parts = [exchange(sent[k][0], k, wide, "wide") for k in order]
    near_parts = [exchange(sent[k][1], k, wide, "wide") for k in order]
    mine, more = last(wide, chips, turned, rolled, basis_a)
    where = {j: (basis, j) if j < half else (more, j - half) for j in range(chips)}
    pieces = combine(chips, half, mine, whole, far_parts)
    xs = {j: exchange(pieces[j - half], 2 * j, narrow, "narrow") for j in range(half, chips)}
    pieces = combine(chips, 0, mine, whole, near_parts)
    for j in range(1, half):
        xs[j] = exchange(pieces[j], 2 * j, narrow, "narrow")
    total = own_points(pieces[0], where[0])
    visits = list(range(half, chips)) + list(range(1, half))
    for j in visits[:-1]:
        total = more_points(total, xs[j], where[j])
    mine, theirs = last_points(total, xs[visits[-1]], where[visits[-1]])
    acted = act(mine, exchange(theirs, 1, narrow, "narrow"), pot)
    other = exchange(acted, 1, narrow, "narrow")
    leave = list(reversed(range(1, chips)))
    *out, both = first_functions(leave, acted, other, basis, more)
    blocks = {j: exchange(out[i], 2 * j, narrow, "narrow") for i, j in enumerate(leave)}
    grid, *sources = assemble(
        wide, [functions(both, where[0])] + [blocks[j] for j in range(1, chips)]
    )
    steps = [wide - 1] + order
    grids = {k: exchange(source, k, wide, "wide") for k, source in zip(steps, sources)}
    total = diagonal(block_pad, coeff, groupb_row_energy, groupa_energy)
    total = backward_more(wide, 0, total, rolled, grid)
    for k in steps[:-1]:
        total = backward_more(wide, k, total, rolled, grids[k])
    return backward_end(wide, steps[-1], total, rolled, grids[steps[-1]])


def solution(mesh):
    return jax.shard_map(
        functools.partial(body, mesh.shape["wide"], mesh.shape["narrow"]),
        mesh=mesh,
        in_specs=(
            P("wide", "narrow"),
            P("wide"),
            P("narrow"),
            P(),
            P(),
            P(("wide", "narrow"), None),
            P("wide"),
            P("wide"),
            P("wide"),
        ),
        out_specs=P("wide", "narrow"),
        check_vma=False,
    )
```

```python
import functools

import jax
import jax.numpy as jnp
from jax import lax
from jax.experimental import pallas as pl
from jax.experimental.pallas import tpu as pltpu
from jax.sharding import PartitionSpec as P

MIB = 1024 * 1024
HBM = pl.BlockSpec(memory_space=pltpu.HBM)
VMEM = pl.BlockSpec(memory_space=pltpu.VMEM)
BF16 = jnp.bfloat16
F32 = jnp.float32
LONG = 8


def call(kernel, name, out_shape, in_specs, out_specs, scratch=(), flops=0, moved=0, mib=16):
    return pl.pallas_call(
        kernel,
        out_shape=out_shape,
        in_specs=in_specs,
        out_specs=out_specs,
        scratch_shapes=scratch,
        compiler_params=pltpu.CompilerParams(vmem_limit_bytes=mib * MIB),
        cost_estimate=pl.CostEstimate(flops=flops, bytes_accessed=moved, transcendentals=0),
        name=name,
    )


def in_hbm(value):
    return pltpu.with_memory_space_constraint(value, pltpu.HBM)


def array(shape, dtype):
    return jax.ShapeDtypeStruct(shape, dtype)


def dot(left, right):
    return jnp.dot(left, right, preferred_element_type=F32)


def dot_turned(left, right):
    return lax.dot_general(left, right, (((1,), (1,)), ((), ())), preferred_element_type=F32)


def chunk_of(turned_ref, rolled_ref, wide, k):
    own = rolled_ref.shape[1] // wide
    start = pl.multiple_of((lax.axis_index("wide") ^ k) * own, own)
    return dot(turned_ref[...], rolled_ref[:, pl.ds(start, own)])


def store_halves(chips, total, far_ref, near_ref):
    upper = lax.axis_index("narrow") // 2 >= chips // 2
    rows = far_ref.shape[0]
    turned = total.astype(BF16).T.astype(F32)
    low, high = turned[:rows], turned[rows:]
    far_ref[...] = jnp.where(upper, low, high).astype(BF16)
    near_ref[...] = jnp.where(upper, high, low).astype(BF16)


def start_pieces(source, target, rows, sem):
    for r in range(0, source.shape[0], rows):
        span = pl.ds(r, rows)
        pltpu.make_async_copy(source.at[span], target.at[span], sem).start()


def wait_all(source, target, sem):
    pltpu.make_async_copy(source, target, sem).wait()


def basis_pieces(first, basis_hbm, basis_ref):
    count, columns, _ = basis_ref.shape
    place = lax.axis_index("narrow")
    core, chip = place % 2, place // 2
    pairs = []
    for j in range(count):
        start = pl.multiple_of(((chip ^ (first + j)) * 2 + core) * columns, columns)
        pairs.append((basis_hbm.at[pl.ds(start, columns)], basis_ref.at[j]))
    return pairs


def halves(rows, columns):
    return (array((rows // 2, columns), BF16),) * 2


def first_kernel(
    wide,
    chips,
    level_hbm,
    pad_hbm,
    shift_hbm,
    coeff_hbm,
    table_hbm,
    basis_hbm,
    potential_hbm,
    out_ref,
    turned_ref,
    rolled_ref,
    basis_ref,
    potential_ref,
    level_ref,
    pad_ref,
    shift_ref,
    coeff_ref,
    table_ref,
    sems,
):
    slots = pad_ref.shape[0]
    levels, width, points = table_ref.shape
    small = [
        pltpu.make_async_copy(source, target, sems.at[i])
        for i, (source, target) in enumerate(
            ((level_hbm, level_ref), (shift_hbm, shift_ref), (pad_hbm, pad_ref))
        )
    ]
    for copy in small:
        copy.start()
    for n in range(levels):
        start_pieces(table_hbm.at[n], table_ref.at[n], 32, sems.at[3])
    start_pieces(coeff_hbm, coeff_ref, 128, sems.at[4])
    pairs = basis_pieces(0, basis_hbm, basis_ref)
    for j, (source, target) in enumerate(pairs):
        start_pieces(source, target, 64, sems.at[6 + j])
    start_pieces(potential_hbm, potential_ref, 8, sems.at[5])
    for copy in small:
        copy.wait()
    wait_all(table_hbm, table_ref, sems.at[3])
    row = lax.broadcasted_iota(jnp.int32, (width, 128), 0)
    for s in range(slots):
        rows = slice(s * width, (s + 1) * width)
        live = jnp.where(row < width - pad_ref[s], 1.0, 0.0).astype(BF16)
        rolled = pltpu.roll(table_ref[level_ref[s]], shift_ref[s], 1)
        for p in range(0, points, 128):
            rolled_ref[rows, p : p + 128] = rolled[:, p : p + 128] * live
    wait_all(coeff_hbm, coeff_ref, sems.at[4])
    turned_ref[...] = coeff_ref[...].T
    out_ref[...] = chunk_of(turned_ref, rolled_ref, wide, wide - 1).astype(BF16).T
    for j, (source, target) in enumerate(pairs):
        wait_all(source, target, sems.at[6 + j])
    wait_all(potential_hbm, potential_ref, sems.at[5])


def first(wide, chips, level, pad, shift, coeff, tables, basis, potential):
    rows, columns = coeff.shape
    points = tables.shape[2]
    slots = pad.shape[0]
    inputs = (level, pad, shift, coeff, tables, basis, potential)
    return call(
        functools.partial(first_kernel, wide, chips),
        "forward_first",
        (
            array((points // wide, columns), BF16),
            array((columns, rows), BF16),
            array((rows, points), BF16),
            array((chips // 2, columns, basis.shape[1]), BF16),
            array(potential.shape, F32),
        ),
        [HBM] * 7,
        (VMEM,) * 5,
        [
            pltpu.SMEM((slots,), jnp.int32),
            pltpu.SMEM((slots,), jnp.int32),
            pltpu.SMEM((slots,), jnp.int32),
            pltpu.VMEM(coeff.shape, coeff.dtype),
            pltpu.VMEM(tables.shape, tables.dtype),
            pltpu.SemaphoreType.DMA((6 + chips,)),
        ],
        flops=2 * rows * points // wide * columns,
        moved=4 * MIB,
    )(*(in_hbm(value) for value in inputs))


def chunk_kernel(wide, chips, k, turned_ref, rolled_ref, far_ref, near_ref):
    store_halves(chips, chunk_of(turned_ref, rolled_ref, wide, k), far_ref, near_ref)


def chunk(wide, chips, k, turned, rolled):
    columns, rows = turned.shape
    own = rolled.shape[1] // wide
    return call(
        functools.partial(chunk_kernel, wide, chips, k),
        "forward_chunk",
        halves(own, columns),
        [VMEM] * 2,
        (VMEM,) * 2,
        flops=2 * rows * own * columns * LONG,
        moved=MIB * LONG,
    )(turned, rolled)


def last_kernel(wide, turned_ref, rolled_ref, basis_hbm, out_ref, basis_ref, sems):
    count = basis_ref.shape[0]
    pairs = basis_pieces(count, basis_hbm, basis_ref)
    for j, (source, target) in enumerate(pairs):
        start_pieces(source, target, 64, sems.at[j])
    out_ref[...] = chunk_of(turned_ref, rolled_ref, wide, 0).T
    for j, (source, target) in enumerate(pairs):
        wait_all(source, target, sems.at[j])


def last(wide, chips, turned, rolled, basis):
    columns, rows = turned.shape
    own = rolled.shape[1] // wide
    count = chips - chips // 2
    return call(
        functools.partial(last_kernel, wide),
        "forward_own",
        (array((own, columns), F32), array((count, columns, basis.shape[1]), BF16)),
        [VMEM, VMEM, HBM],
        (VMEM,) * 2,
        [pltpu.SemaphoreType.DMA((count,))],
    )(turned, rolled, in_hbm(basis))


def combine_kernel(chips, first, mine_ref, whole_ref, *refs):
    count = chips // 2
    parts, outs = refs[:-count], refs[-count:]
    chip = lax.axis_index("narrow") // 2
    rows = outs[0].shape[0]
    for i in range(count):
        target = chip ^ (first + i)
        span = pl.ds(pl.multiple_of(target * rows, rows), rows)
        total = mine_ref[span, :] + whole_ref[span, :].astype(F32)
        start = pl.multiple_of((target % count) * rows, rows)
        for part in parts:
            total = total + part[pl.ds(start, rows), :].astype(F32)
        outs[i][...] = total.astype(BF16)


def combine(chips, first, mine, whole, parts):
    rows, columns = mine.shape
    count = chips // 2
    return call(
        functools.partial(combine_kernel, chips, first),
        "wide_sum",
        (array((rows // chips, columns), BF16),) * count,
        [VMEM] * (len(parts) + 2),
        (VMEM,) * count,
        moved=MIB,
    )(mine, whole, *parts)


def own_points_kernel(x_ref, basis_ref, out_ref):
    out_ref[...] = dot(x_ref[...], basis_ref[0])


def own_points(x, where):
    basis, _ = where
    rows = x.shape[0]
    points = basis.shape[2]
    return call(
        own_points_kernel,
        "points_own",
        array((rows, points), F32),
        [VMEM] * 2,
        VMEM,
        flops=2 * rows * points * x.shape[1],
        moved=2 * MIB,
    )(x, basis)


def more_points_kernel(j, total_ref, x_ref, basis_ref, out_ref):
    out_ref[...] = total_ref[...] + dot(x_ref[...], basis_ref[j])


def more_points(total, x, where):
    basis, j = where
    rows, points = total.shape
    return call(
        functools.partial(more_points_kernel, j),
        "points_more",
        array((rows, points), F32),
        [VMEM] * 3,
        VMEM,
        flops=2 * rows * points * x.shape[1],
        moved=2 * MIB,
    )(total, x, basis)


def last_points_kernel(j, total_ref, x_ref, basis_ref, mine_ref, theirs_ref):
    core = lax.axis_index("narrow") % 2
    rows = mine_ref.shape[0]
    total = total_ref[...] + dot(x_ref[...], basis_ref[j])
    low, high = total[:rows], total[rows:]
    mine_ref[...] = jnp.where(core == 0, low, high)
    theirs_ref[...] = jnp.where(core == 0, high, low)


def last_points(total, x, where):
    basis, j = where
    rows, points = total.shape
    half = array((rows // 2, points), F32)
    return call(
        functools.partial(last_points_kernel, j),
        "points_last",
        (half, half),
        [VMEM] * 3,
        (VMEM, VMEM),
        flops=2 * rows * points * x.shape[1],
        moved=2 * MIB,
    )(total, x, basis)


def act_kernel(mine_ref, other_ref, potential_ref, out_ref):
    on_grid = mine_ref[...] + other_ref[...]
    out_ref[...] = (potential_ref[...] * on_grid).astype(BF16)


def act(mine, other, potential):
    return call(
        act_kernel, "act", array(mine.shape, BF16), [VMEM] * 3, VMEM, moved=MIB
    )(mine, other, potential)


def first_functions_kernel(leave, mine_ref, other_ref, basis_ref, more_ref, *refs):
    outs, both_ref = refs[:-1], refs[-1]
    core = lax.axis_index("narrow") % 2
    rows = mine_ref.shape[0]
    mine, other = mine_ref[...].astype(F32), other_ref[...].astype(F32)
    both_ref[:rows] = jnp.where(core == 0, mine, other).astype(BF16)
    both_ref[rows:] = jnp.where(core == 0, other, mine).astype(BF16)
    for j, out in zip(leave, outs):
        half = basis_ref.shape[0]
        block = basis_ref[j] if j < half else more_ref[j - half]
        out[...] = dot_turned(both_ref[...], block).astype(BF16)


def first_functions(leave, mine, other, basis, more):
    rows, points = mine.shape
    columns = basis.shape[1]
    return call(
        functools.partial(first_functions_kernel, leave),
        "functions_first",
        (array((2 * rows, columns), BF16),) * len(leave) + (array((2 * rows, points), BF16),),
        [VMEM] * 4,
        (VMEM,) * (len(leave) + 1),
    )(mine, other, basis, more)


def functions_kernel(j, both_ref, basis_ref, out_ref):
    out_ref[...] = dot_turned(both_ref[...], basis_ref[j]).astype(BF16)


def functions(both, where):
    basis, j = where
    rows, points = both.shape
    columns = basis.shape[1]
    return call(
        functools.partial(functions_kernel, j),
        "functions_more",
        array((rows, columns), BF16),
        [VMEM] * 2,
        VMEM,
        flops=2 * rows * points * columns,
        moved=2 * MIB,
    )(both, basis)


def assemble_kernel(*refs):
    parts, out_ref = refs[:-1], refs[-1]
    chip = lax.axis_index("narrow") // 2
    rows = parts[0].shape[0]
    for j, part in enumerate(parts):
        start = pl.multiple_of((chip ^ j) * rows, rows)
        out_ref[pl.ds(start, rows), :] = part[...]


def assemble(parts):
    rows, columns = parts[0].shape
    chips = len(parts)
    return call(
        assemble_kernel,
        "assemble",
        array((rows * chips, columns), BF16),
        [VMEM] * chips,
        VMEM,
        moved=MIB // 4,
    )(*parts)


def diagonal_kernel(pad_ref, coeff_ref, row_ref, column_ref, out_ref):
    slots = pad_ref.shape[0]
    width = coeff_ref.shape[0] // slots
    row = lax.broadcasted_iota(jnp.int32, (width, out_ref.shape[1]), 0)
    for s in range(slots):
        rows = slice(s * width, (s + 1) * width)
        energy = row_ref[rows, :] + column_ref[...]
        diagonal = energy * coeff_ref[rows, :].astype(F32)
        out_ref[rows, :] = jnp.where(row < width - pad_ref[s], diagonal, 0.0)


def diagonal(pad, coeff, row_energy, column_energy):
    smem = pl.BlockSpec(memory_space=pltpu.SMEM)
    return call(
        diagonal_kernel,
        "diagonal",
        array(coeff.shape, F32),
        [smem] + [VMEM] * 3,
        VMEM,
    )(pad, coeff, row_energy[:, None], column_energy[None, :])


def more_kernel(wide, k, total_ref, rolled_ref, grid_ref, out_ref):
    own = rolled_ref.shape[1] // wide
    start = pl.multiple_of((lax.axis_index("wide") ^ k) * own, own)
    out_ref[...] = total_ref[...] + dot(rolled_ref[:, pl.ds(start, own)], grid_ref[...])


def backward_more(wide, k, total, rolled, grid):
    rows, columns = total.shape
    return call(
        functools.partial(more_kernel, wide, k),
        "backward_more",
        array(total.shape, F32),
        [VMEM] * 3,
        VMEM,
        flops=2 * rows * columns * rolled.shape[1] // wide,
        moved=3 * MIB,
    )(total, rolled, grid)


def end_kernel(wide, k, total_ref, rolled_ref, grid_ref, out_hbm, out_ref, sems):
    own = rolled_ref.shape[1] // wide
    start = pl.multiple_of((lax.axis_index("wide") ^ k) * own, own)
    steps = sems.shape[0]
    rows = rolled_ref.shape[0] // steps
    copies = []
    for i in range(steps):
        span = pl.ds(i * rows, rows)
        part = dot(rolled_ref[span, pl.ds(start, own)], grid_ref[...])
        out_ref[span, :] = total_ref[span, :] + part
        copies.append(pltpu.make_async_copy(out_ref.at[span, :], out_hbm.at[span, :], sems.at[i]))
        copies[-1].start()
    for copy in copies:
        copy.wait()


def backward_end(wide, k, total, rolled, grid):
    rows, columns = total.shape
    return call(
        functools.partial(end_kernel, wide, k),
        "backward_end",
        array(total.shape, F32),
        [VMEM] * 3,
        HBM,
        [pltpu.VMEM(total.shape, F32), pltpu.SemaphoreType.DMA((8,))],
        flops=2 * rows * columns * rolled.shape[1] // wide,
        moved=4 * MIB,
    )(total, rolled, grid)


def exchange(value, step, size, axis):
    return lax.ppermute(value, axis, [(i, i ^ step) for i in range(size)])


def body(
    wide,
    narrow,
    coeff,
    groupb_row_energy,
    groupa_energy,
    groupb_basis_values,
    basis_a,
    potential,
    slot_sparse_level,
    block_pad,
    slot_grid_offset,
):
    chips = narrow // 2
    tables = jnp.swapaxes(groupb_basis_values, 1, 2)
    half = chips // 2
    order = list(range(1, wide - 1))
    whole, turned, rolled, basis, pot = first(
        wide,
        chips,
        slot_sparse_level,
        block_pad,
        slot_grid_offset,
        coeff,
        tables,
        basis_a,
        potential,
    )
    whole = exchange(whole, wide - 1, wide, "wide")
    sent = {k: chunk(wide, chips, k, turned, rolled) for k in order}
    far_parts = [exchange(sent[k][0], k, wide, "wide") for k in order]
    near_parts = [exchange(sent[k][1], k, wide, "wide") for k in order]
    mine, more = last(wide, chips, turned, rolled, basis_a)
    where = {j: (basis, j) if j < half else (more, j - half) for j in range(chips)}
    pieces = combine(chips, half, mine, whole, far_parts)
    xs = {j: exchange(pieces[j - half], 2 * j, narrow, "narrow") for j in range(half, chips)}
    pieces = combine(chips, 0, mine, whole, near_parts)
    for j in range(1, half):
        xs[j] = exchange(pieces[j], 2 * j, narrow, "narrow")
    total = own_points(pieces[0], where[0])
    visits = list(range(half, chips)) + list(range(1, half))
    for j in visits[:-1]:
        total = more_points(total, xs[j], where[j])
    mine, theirs = last_points(total, xs[visits[-1]], where[visits[-1]])
    acted = act(mine, exchange(theirs, 1, narrow, "narrow"), pot)
    other = exchange(acted, 1, narrow, "narrow")
    leave = list(reversed(range(1, chips)))
    *out, both = first_functions(leave, acted, other, basis, more)
    blocks = {j: exchange(out[i], 2 * j, narrow, "narrow") for i, j in enumerate(leave)}
    grid = assemble([functions(both, where[0])] + [blocks[j] for j in range(1, chips)])
    steps = order[:1] + [wide - 1] + order[1:]
    grids = {k: exchange(grid, k, wide, "wide") for k in steps}
    total = diagonal(block_pad, coeff, groupb_row_energy, groupa_energy)
    total = backward_more(wide, 0, total, rolled, grid)
    for k in steps[:-1]:
        total = backward_more(wide, k, total, rolled, grids[k])
    return backward_end(wide, steps[-1], total, rolled, grids[steps[-1]])


def solution(mesh):
    return jax.shard_map(
        functools.partial(body, mesh.shape["wide"], mesh.shape["narrow"]),
        mesh=mesh,
        in_specs=(
            P("wide", "narrow"),
            P("wide"),
            P("narrow"),
            P(),
            P(),
            P(("wide", "narrow"), None),
            P("wide"),
            P("wide"),
            P("wide"),
        ),
        out_specs=P("wide", "narrow"),
        check_vma=False,
    )
```

```python
import functools

import jax
import jax.numpy as jnp
from jax import lax
from jax.experimental import pallas as pl
from jax.experimental.pallas import tpu as pltpu
from jax.sharding import PartitionSpec as P

MIB = 1024 * 1024
HBM = pl.BlockSpec(memory_space=pltpu.HBM)
VMEM = pl.BlockSpec(memory_space=pltpu.VMEM)
BF16 = jnp.bfloat16
F32 = jnp.float32
LONG = 8


def call(kernel, name, out_shape, in_specs, out_specs, scratch=(), flops=0, moved=0, mib=16):
    return pl.pallas_call(
        kernel,
        out_shape=out_shape,
        in_specs=in_specs,
        out_specs=out_specs,
        scratch_shapes=scratch,
        compiler_params=pltpu.CompilerParams(vmem_limit_bytes=mib * MIB),
        cost_estimate=pl.CostEstimate(flops=flops, bytes_accessed=moved, transcendentals=0),
        name=name,
    )


def in_hbm(value):
    return pltpu.with_memory_space_constraint(value, pltpu.HBM)


def array(shape, dtype):
    return jax.ShapeDtypeStruct(shape, dtype)


def dot(left, right):
    return jnp.dot(left, right, preferred_element_type=F32)


def dot_turned(left, right):
    return lax.dot_general(left, right, (((1,), (1,)), ((), ())), preferred_element_type=F32)


def chunk_of(turned_ref, rolled_ref, wide, k):
    own = rolled_ref.shape[1] // wide
    start = pl.multiple_of((lax.axis_index("wide") ^ k) * own, own)
    return dot(turned_ref[...], rolled_ref[:, pl.ds(start, own)])


def store_halves(chips, total, far_ref, near_ref):
    upper = lax.axis_index("narrow") // 2 >= chips // 2
    rows = far_ref.shape[0]
    turned = total.astype(BF16).T.astype(F32)
    low, high = turned[:rows], turned[rows:]
    far_ref[...] = jnp.where(upper, low, high).astype(BF16)
    near_ref[...] = jnp.where(upper, high, low).astype(BF16)


def start_pieces(source, target, rows, sem):
    for r in range(0, source.shape[0], rows):
        span = pl.ds(r, rows)
        pltpu.make_async_copy(source.at[span], target.at[span], sem).start()


def wait_all(source, target, sem):
    pltpu.make_async_copy(source, target, sem).wait()


def basis_pieces(first, basis_hbm, basis_ref):
    count, columns, _ = basis_ref.shape
    place = lax.axis_index("narrow")
    core, chip = place % 2, place // 2
    pairs = []
    for j in range(count):
        start = pl.multiple_of(((chip ^ (first + j)) * 2 + core) * columns, columns)
        pairs.append((basis_hbm.at[pl.ds(start, columns)], basis_ref.at[j]))
    return pairs


def halves(rows, columns):
    return (array((rows // 2, columns), BF16),) * 2


def first_kernel(
    wide,
    chips,
    level_hbm,
    pad_hbm,
    shift_hbm,
    coeff_hbm,
    table_hbm,
    basis_hbm,
    potential_hbm,
    out_ref,
    turned_ref,
    rolled_ref,
    basis_ref,
    potential_ref,
    level_ref,
    pad_ref,
    shift_ref,
    coeff_ref,
    table_ref,
    sems,
):
    slots = pad_ref.shape[0]
    levels, width, points = table_ref.shape
    small = [
        pltpu.make_async_copy(source, target, sems.at[i])
        for i, (source, target) in enumerate(
            ((level_hbm, level_ref), (shift_hbm, shift_ref), (pad_hbm, pad_ref))
        )
    ]
    for copy in small:
        copy.start()
    for n in range(levels):
        start_pieces(table_hbm.at[n], table_ref.at[n], 32, sems.at[3])
    start_pieces(coeff_hbm, coeff_ref, 128, sems.at[4])
    pairs = basis_pieces(0, basis_hbm, basis_ref)
    for j, (source, target) in enumerate(pairs):
        start_pieces(source, target, 64, sems.at[6 + j])
    start_pieces(potential_hbm, potential_ref, 8, sems.at[5])
    for copy in small:
        copy.wait()
    wait_all(table_hbm, table_ref, sems.at[3])
    row = lax.broadcasted_iota(jnp.int32, (width, 128), 0)
    for s in range(slots):
        rows = slice(s * width, (s + 1) * width)
        live = jnp.where(row < width - pad_ref[s], 1.0, 0.0).astype(BF16)
        rolled = pltpu.roll(table_ref[level_ref[s]], shift_ref[s], 1)
        for p in range(0, points, 128):
            rolled_ref[rows, p : p + 128] = rolled[:, p : p + 128] * live
    wait_all(coeff_hbm, coeff_ref, sems.at[4])
    turned_ref[...] = coeff_ref[...].T
    out_ref[...] = chunk_of(turned_ref, rolled_ref, wide, wide - 1).astype(BF16).T
    for j, (source, target) in enumerate(pairs):
        wait_all(source, target, sems.at[6 + j])
    wait_all(potential_hbm, potential_ref, sems.at[5])


def first(wide, chips, level, pad, shift, coeff, tables, basis, potential):
    rows, columns = coeff.shape
    points = tables.shape[2]
    slots = pad.shape[0]
    inputs = (level, pad, shift, coeff, tables, basis, potential)
    return call(
        functools.partial(first_kernel, wide, chips),
        "forward_first",
        (
            array((points // wide, columns), BF16),
            array((columns, rows), BF16),
            array((rows, points), BF16),
            array((chips // 2, columns, basis.shape[1]), BF16),
            array(potential.shape, F32),
        ),
        [HBM] * 7,
        (VMEM,) * 5,
        [
            pltpu.SMEM((slots,), jnp.int32),
            pltpu.SMEM((slots,), jnp.int32),
            pltpu.SMEM((slots,), jnp.int32),
            pltpu.VMEM(coeff.shape, coeff.dtype),
            pltpu.VMEM(tables.shape, tables.dtype),
            pltpu.SemaphoreType.DMA((6 + chips,)),
        ],
        flops=2 * rows * points // wide * columns,
        moved=4 * MIB,
    )(*(in_hbm(value) for value in inputs))


def chunk_kernel(wide, chips, k, turned_ref, rolled_ref, far_ref, near_ref):
    store_halves(chips, chunk_of(turned_ref, rolled_ref, wide, k), far_ref, near_ref)


def chunk(wide, chips, k, turned, rolled):
    columns, rows = turned.shape
    own = rolled.shape[1] // wide
    return call(
        functools.partial(chunk_kernel, wide, chips, k),
        "forward_chunk",
        halves(own, columns),
        [VMEM] * 2,
        (VMEM,) * 2,
        flops=2 * rows * own * columns * LONG,
        moved=MIB * LONG,
    )(turned, rolled)


def last_kernel(wide, turned_ref, rolled_ref, basis_hbm, out_ref, basis_ref, sems):
    count = basis_ref.shape[0]
    pairs = basis_pieces(count, basis_hbm, basis_ref)
    for j, (source, target) in enumerate(pairs):
        start_pieces(source, target, 64, sems.at[j])
    out_ref[...] = chunk_of(turned_ref, rolled_ref, wide, 0).T
    for j, (source, target) in enumerate(pairs):
        wait_all(source, target, sems.at[j])


def last(wide, chips, turned, rolled, basis):
    columns, rows = turned.shape
    own = rolled.shape[1] // wide
    count = chips - chips // 2
    return call(
        functools.partial(last_kernel, wide),
        "forward_own",
        (array((own, columns), F32), array((count, columns, basis.shape[1]), BF16)),
        [VMEM, VMEM, HBM],
        (VMEM,) * 2,
        [pltpu.SemaphoreType.DMA((count,))],
    )(turned, rolled, in_hbm(basis))


def combine_kernel(chips, first, mine_ref, whole_ref, *refs):
    count = chips // 2
    parts, outs = refs[:-count], refs[-count:]
    chip = lax.axis_index("narrow") // 2
    rows = outs[0].shape[0]
    for i in range(count):
        target = chip ^ (first + i)
        span = pl.ds(pl.multiple_of(target * rows, rows), rows)
        total = mine_ref[span, :] + whole_ref[span, :].astype(F32)
        start = pl.multiple_of((target % count) * rows, rows)
        for part in parts:
            total = total + part[pl.ds(start, rows), :].astype(F32)
        outs[i][...] = total.astype(BF16)


def combine(chips, first, mine, whole, parts):
    rows, columns = mine.shape
    count = chips // 2
    return call(
        functools.partial(combine_kernel, chips, first),
        "wide_sum",
        (array((rows // chips, columns), BF16),) * count,
        [VMEM] * (len(parts) + 2),
        (VMEM,) * count,
        moved=MIB,
    )(mine, whole, *parts)


def own_points_kernel(x_ref, basis_ref, out_ref):
    out_ref[...] = dot(x_ref[...], basis_ref[0])


def own_points(x, where):
    basis, _ = where
    rows = x.shape[0]
    points = basis.shape[2]
    return call(
        own_points_kernel,
        "points_own",
        array((rows, points), F32),
        [VMEM] * 2,
        VMEM,
        flops=2 * rows * points * x.shape[1],
        moved=2 * MIB,
    )(x, basis)


def more_points_kernel(j, total_ref, x_ref, basis_ref, out_ref):
    out_ref[...] = total_ref[...] + dot(x_ref[...], basis_ref[j])


def more_points(total, x, where):
    basis, j = where
    rows, points = total.shape
    return call(
        functools.partial(more_points_kernel, j),
        "points_more",
        array((rows, points), F32),
        [VMEM] * 3,
        VMEM,
        flops=2 * rows * points * x.shape[1],
        moved=2 * MIB,
    )(total, x, basis)


def last_points_kernel(j, total_ref, x_ref, basis_ref, mine_ref, theirs_ref):
    core = lax.axis_index("narrow") % 2
    rows = mine_ref.shape[0]
    total = total_ref[...] + dot(x_ref[...], basis_ref[j])
    low, high = total[:rows], total[rows:]
    mine_ref[...] = jnp.where(core == 0, low, high)
    theirs_ref[...] = jnp.where(core == 0, high, low)


def last_points(total, x, where):
    basis, j = where
    rows, points = total.shape
    half = array((rows // 2, points), F32)
    return call(
        functools.partial(last_points_kernel, j),
        "points_last",
        (half, half),
        [VMEM] * 3,
        (VMEM, VMEM),
        flops=2 * rows * points * x.shape[1],
        moved=2 * MIB,
    )(total, x, basis)


def act_kernel(mine_ref, other_ref, potential_ref, out_ref):
    on_grid = mine_ref[...] + other_ref[...]
    out_ref[...] = (potential_ref[...] * on_grid).astype(BF16)


def act(mine, other, potential):
    return call(
        act_kernel, "act", array(mine.shape, BF16), [VMEM] * 3, VMEM, moved=MIB
    )(mine, other, potential)


def first_functions_kernel(leave, mine_ref, other_ref, basis_ref, more_ref, *refs):
    outs, both_ref = refs[:-1], refs[-1]
    core = lax.axis_index("narrow") % 2
    rows = mine_ref.shape[0]
    mine, other = mine_ref[...].astype(F32), other_ref[...].astype(F32)
    both_ref[:rows] = jnp.where(core == 0, mine, other).astype(BF16)
    both_ref[rows:] = jnp.where(core == 0, other, mine).astype(BF16)
    for j, out in zip(leave, outs):
        half = basis_ref.shape[0]
        block = basis_ref[j] if j < half else more_ref[j - half]
        out[...] = dot_turned(both_ref[...], block).astype(BF16)


def first_functions(leave, mine, other, basis, more):
    rows, points = mine.shape
    columns = basis.shape[1]
    return call(
        functools.partial(first_functions_kernel, leave),
        "functions_first",
        (array((2 * rows, columns), BF16),) * len(leave) + (array((2 * rows, points), BF16),),
        [VMEM] * 4,
        (VMEM,) * (len(leave) + 1),
    )(mine, other, basis, more)


def functions_kernel(j, both_ref, basis_ref, out_ref):
    out_ref[...] = dot_turned(both_ref[...], basis_ref[j]).astype(BF16)


def functions(both, where):
    basis, j = where
    rows, points = both.shape
    columns = basis.shape[1]
    return call(
        functools.partial(functions_kernel, j),
        "functions_more",
        array((rows, columns), BF16),
        [VMEM] * 2,
        VMEM,
        flops=2 * rows * points * columns,
        moved=2 * MIB,
    )(both, basis)


def assemble_kernel(visits, *refs):
    parts, out_ref = refs[:-1], refs[-1]
    chip = lax.axis_index("narrow") // 2
    rows = parts[0].shape[0]
    for j, part in zip(visits, parts):
        start = pl.multiple_of((chip ^ j) * rows, rows)
        out_ref[pl.ds(start, rows), :] = part[...]


def assemble(visits, parts):
    rows, columns = parts[0].shape
    chips = len(parts)
    return call(
        functools.partial(assemble_kernel, visits),
        "assemble",
        array((rows * chips, columns), BF16),
        [VMEM] * chips,
        VMEM,
        moved=MIB // 4,
    )(*parts)


def diagonal_kernel(pad_ref, coeff_ref, row_ref, column_ref, out_ref):
    slots = pad_ref.shape[0]
    width = coeff_ref.shape[0] // slots
    row = lax.broadcasted_iota(jnp.int32, (width, out_ref.shape[1]), 0)
    for s in range(slots):
        rows = slice(s * width, (s + 1) * width)
        energy = row_ref[rows, :] + column_ref[...]
        diagonal = energy * coeff_ref[rows, :].astype(F32)
        out_ref[rows, :] = jnp.where(row < width - pad_ref[s], diagonal, 0.0)


def diagonal(pad, coeff, row_energy, column_energy):
    smem = pl.BlockSpec(memory_space=pltpu.SMEM)
    return call(
        diagonal_kernel,
        "diagonal",
        array(coeff.shape, F32),
        [smem] + [VMEM] * 3,
        VMEM,
    )(pad, coeff, row_energy[:, None], column_energy[None, :])


def more_kernel(wide, k, total_ref, rolled_ref, grid_ref, out_ref):
    own = rolled_ref.shape[1] // wide
    start = pl.multiple_of((lax.axis_index("wide") ^ k) * own, own)
    out_ref[...] = total_ref[...] + dot(rolled_ref[:, pl.ds(start, own)], grid_ref[...])


def backward_more(wide, k, total, rolled, grid):
    rows, columns = total.shape
    return call(
        functools.partial(more_kernel, wide, k),
        "backward_more",
        array(total.shape, F32),
        [VMEM] * 3,
        VMEM,
        flops=2 * rows * columns * rolled.shape[1] // wide,
        moved=3 * MIB,
    )(total, rolled, grid)


def end_kernel(wide, k, total_ref, rolled_ref, grid_ref, out_hbm, out_ref, sems):
    own = rolled_ref.shape[1] // wide
    start = pl.multiple_of((lax.axis_index("wide") ^ k) * own, own)
    steps = sems.shape[0]
    rows = rolled_ref.shape[0] // steps
    copies = []
    for i in range(steps):
        span = pl.ds(i * rows, rows)
        part = dot(rolled_ref[span, pl.ds(start, own)], grid_ref[...])
        out_ref[span, :] = total_ref[span, :] + part
        copies.append(pltpu.make_async_copy(out_ref.at[span, :], out_hbm.at[span, :], sems.at[i]))
        copies[-1].start()
    for copy in copies:
        copy.wait()


def backward_end(wide, k, total, rolled, grid):
    rows, columns = total.shape
    return call(
        functools.partial(end_kernel, wide, k),
        "backward_end",
        array(total.shape, F32),
        [VMEM] * 3,
        HBM,
        [pltpu.VMEM(total.shape, F32), pltpu.SemaphoreType.DMA((8,))],
        flops=2 * rows * columns * rolled.shape[1] // wide,
        moved=4 * MIB,
    )(total, rolled, grid)


def exchange(value, step, size, axis):
    return lax.ppermute(value, axis, [(i, i ^ step) for i in range(size)])


def body(
    wide,
    narrow,
    coeff,
    groupb_row_energy,
    groupa_energy,
    groupb_basis_values,
    basis_a,
    potential,
    slot_sparse_level,
    block_pad,
    slot_grid_offset,
):
    chips = narrow // 2
    tables = jnp.swapaxes(groupb_basis_values, 1, 2)
    half = chips // 2
    order = list(range(1, wide - 1))
    whole, turned, rolled, basis, pot = first(
        wide,
        chips,
        slot_sparse_level,
        block_pad,
        slot_grid_offset,
        coeff,
        tables,
        basis_a,
        potential,
    )
    whole = exchange(whole, wide - 1, wide, "wide")
    sent = {k: chunk(wide, chips, k, turned, rolled) for k in order}
    far_parts = [exchange(sent[k][0], k, wide, "wide") for k in order]
    near_parts = [exchange(sent[k][1], k, wide, "wide") for k in order]
    mine, more = last(wide, chips, turned, rolled, basis_a)
    where = {j: (basis, j) if j < half else (more, j - half) for j in range(chips)}
    pieces = combine(chips, half, mine, whole, far_parts)
    xs = {j: exchange(pieces[j - half], 2 * j, narrow, "narrow") for j in range(half, chips)}
    pieces = combine(chips, 0, mine, whole, near_parts)
    for j in range(1, half):
        xs[j] = exchange(pieces[j], 2 * j, narrow, "narrow")
    total = own_points(pieces[0], where[0])
    visits = list(range(half, chips)) + list(range(1, half))
    for j in visits[:-1]:
        total = more_points(total, xs[j], where[j])
    mine, theirs = last_points(total, xs[visits[-1]], where[visits[-1]])
    acted = act(mine, exchange(theirs, 1, narrow, "narrow"), pot)
    other = exchange(acted, 1, narrow, "narrow")
    leave = visits
    *out, both = first_functions(leave, acted, other, basis, more)
    blocks = {j: exchange(out[i], 2 * j, narrow, "narrow") for i, j in enumerate(leave)}
    grid = assemble([0] + leave, [functions(both, where[0])] + [blocks[j] for j in leave])
    steps = [wide - 1] + order
    grids = {k: exchange(grid, k, wide, "wide") for k in steps}
    total = diagonal(block_pad, coeff, groupb_row_energy, groupa_energy)
    total = backward_more(wide, 0, total, rolled, grid)
    for k in steps[:-1]:
        total = backward_more(wide, k, total, rolled, grids[k])
    return backward_end(wide, steps[-1], total, rolled, grids[steps[-1]])


def solution(mesh):
    return jax.shard_map(
        functools.partial(body, mesh.shape["wide"], mesh.shape["narrow"]),
        mesh=mesh,
        in_specs=(
            P("wide", "narrow"),
            P("wide"),
            P("narrow"),
            P(),
            P(),
            P(("wide", "narrow"), None),
            P("wide"),
            P("wide"),
            P("wide"),
        ),
        out_specs=P("wide", "narrow"),
        check_vma=False,
    )
```

```python
import functools

import jax
import jax.numpy as jnp
from jax import lax
from jax.experimental import pallas as pl
from jax.experimental.pallas import tpu as pltpu
from jax.sharding import PartitionSpec as P

MIB = 1024 * 1024
HBM = pl.BlockSpec(memory_space=pltpu.HBM)
VMEM = pl.BlockSpec(memory_space=pltpu.VMEM)
BF16 = jnp.bfloat16
F32 = jnp.float32
LONG = 8


def call(kernel, name, out_shape, in_specs, out_specs, scratch=(), flops=0, moved=0, mib=16):
    return pl.pallas_call(
        kernel,
        out_shape=out_shape,
        in_specs=in_specs,
        out_specs=out_specs,
        scratch_shapes=scratch,
        compiler_params=pltpu.CompilerParams(vmem_limit_bytes=mib * MIB),
        cost_estimate=pl.CostEstimate(flops=flops, bytes_accessed=moved, transcendentals=0),
        name=name,
    )


def in_hbm(value):
    return pltpu.with_memory_space_constraint(value, pltpu.HBM)


def array(shape, dtype):
    return jax.ShapeDtypeStruct(shape, dtype)


def dot(left, right):
    return jnp.dot(left, right, preferred_element_type=F32)


def dot_turned(left, right):
    return lax.dot_general(left, right, (((1,), (1,)), ((), ())), preferred_element_type=F32)


def chunk_of(turned_ref, rolled_ref, wide, k):
    own = rolled_ref.shape[1] // wide
    start = pl.multiple_of((lax.axis_index("wide") ^ k) * own, own)
    return dot(turned_ref[...], rolled_ref[:, pl.ds(start, own)])


def store_halves(chips, total, far_ref, near_ref):
    upper = lax.axis_index("narrow") // 2 >= chips // 2
    rows = far_ref.shape[0]
    turned = total.astype(BF16).T.astype(F32)
    low, high = turned[:rows], turned[rows:]
    far_ref[...] = jnp.where(upper, low, high).astype(BF16)
    near_ref[...] = jnp.where(upper, high, low).astype(BF16)


def start_pieces(source, target, rows, sem):
    for r in range(0, source.shape[0], rows):
        span = pl.ds(r, rows)
        pltpu.make_async_copy(source.at[span], target.at[span], sem).start()


def wait_all(source, target, sem):
    pltpu.make_async_copy(source, target, sem).wait()


def basis_pieces(first, basis_hbm, basis_ref):
    count, columns, _ = basis_ref.shape
    place = lax.axis_index("narrow")
    core, chip = place % 2, place // 2
    pairs = []
    for j in range(count):
        start = pl.multiple_of(((chip ^ (first + j)) * 2 + core) * columns, columns)
        pairs.append((basis_hbm.at[pl.ds(start, columns)], basis_ref.at[j]))
    return pairs


def halves(rows, columns):
    return (array((rows // 2, columns), BF16),) * 2


def first_kernel(
    wide,
    chips,
    level_hbm,
    pad_hbm,
    shift_hbm,
    coeff_hbm,
    table_hbm,
    basis_hbm,
    potential_hbm,
    out_ref,
    turned_ref,
    rolled_ref,
    basis_ref,
    potential_ref,
    level_ref,
    pad_ref,
    shift_ref,
    coeff_ref,
    table_ref,
    sems,
):
    slots = pad_ref.shape[0]
    levels, width, points = table_ref.shape
    small = [
        pltpu.make_async_copy(source, target, sems.at[i])
        for i, (source, target) in enumerate(
            ((level_hbm, level_ref), (shift_hbm, shift_ref), (pad_hbm, pad_ref))
        )
    ]
    for copy in small:
        copy.start()
    for n in range(levels):
        start_pieces(table_hbm.at[n], table_ref.at[n], 32, sems.at[3])
    start_pieces(coeff_hbm, coeff_ref, 128, sems.at[4])
    pairs = basis_pieces(0, basis_hbm, basis_ref)
    for j, (source, target) in enumerate(pairs):
        start_pieces(source, target, 64, sems.at[6 + j])
    start_pieces(potential_hbm, potential_ref, 8, sems.at[5])
    for copy in small:
        copy.wait()
    wait_all(table_hbm, table_ref, sems.at[3])
    row = lax.broadcasted_iota(jnp.int32, (width, 128), 0)
    for s in range(slots):
        rows = slice(s * width, (s + 1) * width)
        live = jnp.where(row < width - pad_ref[s], 1.0, 0.0).astype(BF16)
        rolled = pltpu.roll(table_ref[level_ref[s]], shift_ref[s], 1)
        for p in range(0, points, 128):
            rolled_ref[rows, p : p + 128] = rolled[:, p : p + 128] * live
    wait_all(coeff_hbm, coeff_ref, sems.at[4])
    turned_ref[...] = coeff_ref[...].T
    out_ref[...] = chunk_of(turned_ref, rolled_ref, wide, wide - 1).astype(BF16).T
    for j, (source, target) in enumerate(pairs):
        wait_all(source, target, sems.at[6 + j])
    wait_all(potential_hbm, potential_ref, sems.at[5])


def first(wide, chips, level, pad, shift, coeff, tables, basis, potential):
    rows, columns = coeff.shape
    points = tables.shape[2]
    slots = pad.shape[0]
    inputs = (level, pad, shift, coeff, tables, basis, potential)
    return call(
        functools.partial(first_kernel, wide, chips),
        "forward_first",
        (
            array((points // wide, columns), BF16),
            array((columns, rows), BF16),
            array((rows, points), BF16),
            array((chips // 2, columns, basis.shape[1]), BF16),
            array(potential.shape, F32),
        ),
        [HBM] * 7,
        (VMEM,) * 5,
        [
            pltpu.SMEM((slots,), jnp.int32),
            pltpu.SMEM((slots,), jnp.int32),
            pltpu.SMEM((slots,), jnp.int32),
            pltpu.VMEM(coeff.shape, coeff.dtype),
            pltpu.VMEM(tables.shape, tables.dtype),
            pltpu.SemaphoreType.DMA((6 + chips,)),
        ],
        flops=2 * rows * points // wide * columns,
        moved=4 * MIB,
    )(*(in_hbm(value) for value in inputs))


def chunk_kernel(wide, chips, k, turned_ref, rolled_ref, far_ref, near_ref):
    store_halves(chips, chunk_of(turned_ref, rolled_ref, wide, k), far_ref, near_ref)


def chunk(wide, chips, k, turned, rolled):
    columns, rows = turned.shape
    own = rolled.shape[1] // wide
    return call(
        functools.partial(chunk_kernel, wide, chips, k),
        "forward_chunk",
        halves(own, columns),
        [VMEM] * 2,
        (VMEM,) * 2,
        flops=2 * rows * own * columns * LONG,
        moved=MIB * LONG,
    )(turned, rolled)


def last_kernel(wide, turned_ref, rolled_ref, basis_hbm, out_ref, basis_ref, sems):
    count = basis_ref.shape[0]
    pairs = basis_pieces(count, basis_hbm, basis_ref)
    for j, (source, target) in enumerate(pairs):
        start_pieces(source, target, 64, sems.at[j])
    out_ref[...] = chunk_of(turned_ref, rolled_ref, wide, 0).T
    for j, (source, target) in enumerate(pairs):
        wait_all(source, target, sems.at[j])


def last(wide, chips, turned, rolled, basis):
    columns, rows = turned.shape
    own = rolled.shape[1] // wide
    count = chips - chips // 2
    return call(
        functools.partial(last_kernel, wide),
        "forward_own",
        (array((own, columns), F32), array((count, columns, basis.shape[1]), BF16)),
        [VMEM, VMEM, HBM],
        (VMEM,) * 2,
        [pltpu.SemaphoreType.DMA((count,))],
    )(turned, rolled, in_hbm(basis))


def combine_kernel(chips, first, mine_ref, whole_ref, *refs):
    count = chips // 2
    parts, outs = refs[:-count], refs[-count:]
    chip = lax.axis_index("narrow") // 2
    rows = outs[0].shape[0]
    for i in range(count):
        target = chip ^ (first + i)
        span = pl.ds(pl.multiple_of(target * rows, rows), rows)
        total = mine_ref[span, :] + whole_ref[span, :].astype(F32)
        start = pl.multiple_of((target % count) * rows, rows)
        for part in parts:
            total = total + part[pl.ds(start, rows), :].astype(F32)
        outs[i][...] = total.astype(BF16)


def combine(chips, first, mine, whole, parts):
    rows, columns = mine.shape
    count = chips // 2
    return call(
        functools.partial(combine_kernel, chips, first),
        "wide_sum",
        (array((rows // chips, columns), BF16),) * count,
        [VMEM] * (len(parts) + 2),
        (VMEM,) * count,
        moved=MIB,
    )(mine, whole, *parts)


def own_points_kernel(x_ref, basis_ref, out_ref):
    out_ref[...] = dot(x_ref[...], basis_ref[0])


def own_points(x, where):
    basis, _ = where
    rows = x.shape[0]
    points = basis.shape[2]
    return call(
        own_points_kernel,
        "points_own",
        array((rows, points), F32),
        [VMEM] * 2,
        VMEM,
        flops=2 * rows * points * x.shape[1],
        moved=2 * MIB,
    )(x, basis)


def more_points_kernel(j, total_ref, x_ref, basis_ref, out_ref):
    out_ref[...] = total_ref[...] + dot(x_ref[...], basis_ref[j])


def more_points(total, x, where):
    basis, j = where
    rows, points = total.shape
    return call(
        functools.partial(more_points_kernel, j),
        "points_more",
        array((rows, points), F32),
        [VMEM] * 3,
        VMEM,
        flops=2 * rows * points * x.shape[1],
        moved=2 * MIB,
    )(total, x, basis)


def last_points_kernel(j, total_ref, x_ref, basis_ref, mine_ref, theirs_ref):
    core = lax.axis_index("narrow") % 2
    rows = mine_ref.shape[0]
    total = total_ref[...] + dot(x_ref[...], basis_ref[j])
    low, high = total[:rows], total[rows:]
    mine_ref[...] = jnp.where(core == 0, low, high)
    theirs_ref[...] = jnp.where(core == 0, high, low)


def last_points(total, x, where):
    basis, j = where
    rows, points = total.shape
    half = array((rows // 2, points), F32)
    return call(
        functools.partial(last_points_kernel, j),
        "points_last",
        (half, half),
        [VMEM] * 3,
        (VMEM, VMEM),
        flops=2 * rows * points * x.shape[1],
        moved=2 * MIB,
    )(total, x, basis)


def act_kernel(mine_ref, other_ref, potential_ref, out_ref):
    on_grid = mine_ref[...] + other_ref[...]
    out_ref[...] = (potential_ref[...] * on_grid).astype(BF16)


def act(mine, other, potential):
    return call(
        act_kernel, "act", array(mine.shape, BF16), [VMEM] * 3, VMEM, moved=MIB
    )(mine, other, potential)


def first_functions_kernel(leave, mine_ref, other_ref, basis_ref, more_ref, *refs):
    outs, both_ref = refs[:-1], refs[-1]
    core = lax.axis_index("narrow") % 2
    rows = mine_ref.shape[0]
    mine, other = mine_ref[...].astype(F32), other_ref[...].astype(F32)
    both_ref[:rows] = jnp.where(core == 0, mine, other).astype(BF16)
    both_ref[rows:] = jnp.where(core == 0, other, mine).astype(BF16)
    for j, out in zip(leave, outs):
        half = basis_ref.shape[0]
        block = basis_ref[j] if j < half else more_ref[j - half]
        out[...] = dot_turned(both_ref[...], block).astype(BF16)


def first_functions(leave, mine, other, basis, more):
    rows, points = mine.shape
    columns = basis.shape[1]
    return call(
        functools.partial(first_functions_kernel, leave),
        "functions_first",
        (array((2 * rows, columns), BF16),) * len(leave) + (array((2 * rows, points), BF16),),
        [VMEM] * 4,
        (VMEM,) * (len(leave) + 1),
    )(mine, other, basis, more)


def functions_kernel(j, both_ref, basis_ref, out_ref):
    out_ref[...] = dot_turned(both_ref[...], basis_ref[j]).astype(BF16)


def functions(both, where):
    basis, j = where
    rows, points = both.shape
    columns = basis.shape[1]
    return call(
        functools.partial(functions_kernel, j),
        "functions_more",
        array((rows, columns), BF16),
        [VMEM] * 2,
        VMEM,
        flops=2 * rows * points * columns,
        moved=2 * MIB,
    )(both, basis)


def assemble_kernel(visits, *refs):
    parts, out_ref = refs[:-1], refs[-1]
    chip = lax.axis_index("narrow") // 2
    rows = parts[0].shape[0]
    for j, part in zip(visits, parts):
        start = pl.multiple_of((chip ^ j) * rows, rows)
        out_ref[pl.ds(start, rows), :] = part[...]


def assemble(visits, parts):
    rows, columns = parts[0].shape
    chips = len(parts)
    return call(
        functools.partial(assemble_kernel, visits),
        "assemble",
        array((rows * chips, columns), BF16),
        [VMEM] * chips,
        VMEM,
        moved=MIB // 4,
    )(*parts)


def diagonal_kernel(pad_ref, coeff_ref, row_ref, column_ref, out_ref):
    slots = pad_ref.shape[0]
    width = coeff_ref.shape[0] // slots
    row = lax.broadcasted_iota(jnp.int32, (width, out_ref.shape[1]), 0)
    for s in range(slots):
        rows = slice(s * width, (s + 1) * width)
        energy = row_ref[rows, :] + column_ref[...]
        diagonal = energy * coeff_ref[rows, :].astype(F32)
        out_ref[rows, :] = jnp.where(row < width - pad_ref[s], diagonal, 0.0)


def diagonal(pad, coeff, row_energy, column_energy):
    smem = pl.BlockSpec(memory_space=pltpu.SMEM)
    return call(
        diagonal_kernel,
        "diagonal",
        array(coeff.shape, F32),
        [smem] + [VMEM] * 3,
        VMEM,
    )(pad, coeff, row_energy[:, None], column_energy[None, :])


def more_kernel(wide, k, total_ref, rolled_ref, grid_ref, out_ref):
    own = rolled_ref.shape[1] // wide
    start = pl.multiple_of((lax.axis_index("wide") ^ k) * own, own)
    out_ref[...] = total_ref[...] + dot(rolled_ref[:, pl.ds(start, own)], grid_ref[...])


def backward_more(wide, k, total, rolled, grid):
    rows, columns = total.shape
    return call(
        functools.partial(more_kernel, wide, k),
        "backward_more",
        array(total.shape, F32),
        [VMEM] * 3,
        VMEM,
        flops=2 * rows * columns * rolled.shape[1] // wide,
        moved=3 * MIB,
    )(total, rolled, grid)


def pair_kernel(wide, k, other, total_ref, rolled_ref, grid_hbm, other_ref, out_ref, grid_ref, sem):
    start_pieces(grid_hbm, grid_ref, 32, sem)
    own = rolled_ref.shape[1] // wide
    me = lax.axis_index("wide")
    start = pl.multiple_of((me ^ other) * own, own)
    out_ref[...] = total_ref[...] + dot(rolled_ref[:, pl.ds(start, own)], other_ref[...])
    wait_all(grid_hbm, grid_ref, sem)
    start = pl.multiple_of((me ^ k) * own, own)
    out_ref[...] += dot(rolled_ref[:, pl.ds(start, own)], grid_ref[...])


def backward_pair(wide, k, other, total, rolled, grid, other_grid):
    return call(
        functools.partial(pair_kernel, wide, k, other),
        "backward_pair",
        array(total.shape, F32),
        [VMEM, VMEM, HBM, VMEM],
        VMEM,
        [pltpu.VMEM(grid.shape, grid.dtype), pltpu.SemaphoreType.DMA],
    )(total, rolled, in_hbm(grid), other_grid)


def end_kernel(wide, k, total_ref, rolled_ref, grid_ref, out_hbm, out_ref, sems):
    own = rolled_ref.shape[1] // wide
    start = pl.multiple_of((lax.axis_index("wide") ^ k) * own, own)
    steps = sems.shape[0]
    rows = rolled_ref.shape[0] // steps
    copies = []
    for i in range(steps):
        span = pl.ds(i * rows, rows)
        part = dot(rolled_ref[span, pl.ds(start, own)], grid_ref[...])
        out_ref[span, :] = total_ref[span, :] + part
        copies.append(pltpu.make_async_copy(out_ref.at[span, :], out_hbm.at[span, :], sems.at[i]))
        copies[-1].start()
    for copy in copies:
        copy.wait()


def backward_end(wide, k, total, rolled, grid):
    rows, columns = total.shape
    return call(
        functools.partial(end_kernel, wide, k),
        "backward_end",
        array(total.shape, F32),
        [VMEM] * 3,
        HBM,
        [pltpu.VMEM(total.shape, F32), pltpu.SemaphoreType.DMA((8,))],
        flops=2 * rows * columns * rolled.shape[1] // wide,
        moved=4 * MIB,
    )(total, rolled, grid)


def exchange(value, step, size, axis):
    return lax.ppermute(value, axis, [(i, i ^ step) for i in range(size)])


def body(
    wide,
    narrow,
    coeff,
    groupb_row_energy,
    groupa_energy,
    groupb_basis_values,
    basis_a,
    potential,
    slot_sparse_level,
    block_pad,
    slot_grid_offset,
):
    chips = narrow // 2
    tables = jnp.swapaxes(groupb_basis_values, 1, 2)
    half = chips // 2
    order = list(range(1, wide - 1))
    whole, turned, rolled, basis, pot = first(
        wide,
        chips,
        slot_sparse_level,
        block_pad,
        slot_grid_offset,
        coeff,
        tables,
        basis_a,
        potential,
    )
    whole = exchange(whole, wide - 1, wide, "wide")
    sent = {k: chunk(wide, chips, k, turned, rolled) for k in order}
    far_parts = [exchange(sent[k][0], k, wide, "wide") for k in order]
    near_parts = [exchange(sent[k][1], k, wide, "wide") for k in order]
    mine, more = last(wide, chips, turned, rolled, basis_a)
    where = {j: (basis, j) if j < half else (more, j - half) for j in range(chips)}
    pieces = combine(chips, half, mine, whole, far_parts)
    xs = {j: exchange(pieces[j - half], 2 * j, narrow, "narrow") for j in range(half, chips)}
    pieces = combine(chips, 0, mine, whole, near_parts)
    for j in range(1, half):
        xs[j] = exchange(pieces[j], 2 * j, narrow, "narrow")
    total = own_points(pieces[0], where[0])
    visits = list(range(half, chips)) + list(range(1, half))
    for j in visits[:-1]:
        total = more_points(total, xs[j], where[j])
    mine, theirs = last_points(total, xs[visits[-1]], where[visits[-1]])
    acted = act(mine, exchange(theirs, 1, narrow, "narrow"), pot)
    other = exchange(acted, 1, narrow, "narrow")
    leave = visits
    *out, both = first_functions(leave, acted, other, basis, more)
    blocks = {j: exchange(out[i], 2 * j, narrow, "narrow") for i, j in enumerate(leave)}
    grid = assemble([0] + leave, [functions(both, where[0])] + [blocks[j] for j in leave])
    steps = [wide - 1] + order
    grids = {k: exchange(grid, k, wide, "wide") for k in steps}
    total = diagonal(block_pad, coeff, groupb_row_energy, groupa_energy)
    total = backward_more(wide, 0, total, rolled, grid)
    k, other = steps[:2]
    total = backward_pair(wide, k, other, total, rolled, grids[k], grids[other])
    for k in steps[2:-1]:
        total = backward_more(wide, k, total, rolled, grids[k])
    return backward_end(wide, steps[-1], total, rolled, grids[steps[-1]])


def solution(mesh):
    return jax.shard_map(
        functools.partial(body, mesh.shape["wide"], mesh.shape["narrow"]),
        mesh=mesh,
        in_specs=(
            P("wide", "narrow"),
            P("wide"),
            P("narrow"),
            P(),
            P(),
            P(("wide", "narrow"), None),
            P("wide"),
            P("wide"),
            P("wide"),
        ),
        out_specs=P("wide", "narrow"),
        check_vma=False,
    )
```

```python
import functools

import jax
import jax.numpy as jnp
from jax import lax
from jax.experimental import pallas as pl
from jax.experimental.pallas import tpu as pltpu
from jax.sharding import PartitionSpec as P

MIB = 1024 * 1024
HBM = pl.BlockSpec(memory_space=pltpu.HBM)
VMEM = pl.BlockSpec(memory_space=pltpu.VMEM)
BF16 = jnp.bfloat16
F32 = jnp.float32
LONG = 8


def call(kernel, name, out_shape, in_specs, out_specs, scratch=(), flops=0, moved=0, mib=16):
    return pl.pallas_call(
        kernel,
        out_shape=out_shape,
        in_specs=in_specs,
        out_specs=out_specs,
        scratch_shapes=scratch,
        compiler_params=pltpu.CompilerParams(vmem_limit_bytes=mib * MIB),
        cost_estimate=pl.CostEstimate(flops=flops, bytes_accessed=moved, transcendentals=0),
        name=name,
    )


def in_hbm(value):
    return pltpu.with_memory_space_constraint(value, pltpu.HBM)


def array(shape, dtype):
    return jax.ShapeDtypeStruct(shape, dtype)


def dot(left, right):
    return jnp.dot(left, right, preferred_element_type=F32)


def dot_turned(left, right):
    return lax.dot_general(left, right, (((1,), (1,)), ((), ())), preferred_element_type=F32)


def chunk_of(turned_ref, rolled_ref, wide, k):
    own = rolled_ref.shape[1] // wide
    start = pl.multiple_of((lax.axis_index("wide") ^ k) * own, own)
    return dot(turned_ref[...], rolled_ref[:, pl.ds(start, own)])


def store_halves(chips, total, far_ref, near_ref):
    upper = lax.axis_index("narrow") // 2 >= chips // 2
    rows = far_ref.shape[0]
    turned = total.astype(BF16).T.astype(F32)
    low, high = turned[:rows], turned[rows:]
    far_ref[...] = jnp.where(upper, low, high).astype(BF16)
    near_ref[...] = jnp.where(upper, high, low).astype(BF16)


def start_pieces(source, target, rows, sem):
    for r in range(0, source.shape[0], rows):
        span = pl.ds(r, rows)
        pltpu.make_async_copy(source.at[span], target.at[span], sem).start()


def wait_all(source, target, sem):
    pltpu.make_async_copy(source, target, sem).wait()


def basis_pieces(first, basis_hbm, basis_ref):
    count, columns, _ = basis_ref.shape
    place = lax.axis_index("narrow")
    core, chip = place % 2, place // 2
    pairs = []
    for j in range(count):
        start = pl.multiple_of(((chip ^ (first + j)) * 2 + core) * columns, columns)
        pairs.append((basis_hbm.at[pl.ds(start, columns)], basis_ref.at[j]))
    return pairs


def halves(rows, columns):
    return (array((rows // 2, columns), BF16),) * 2


def first_kernel(
    wide,
    chips,
    level_hbm,
    pad_hbm,
    shift_hbm,
    coeff_hbm,
    table_hbm,
    basis_hbm,
    potential_hbm,
    out_ref,
    turned_ref,
    rolled_ref,
    basis_ref,
    potential_ref,
    level_ref,
    pad_ref,
    shift_ref,
    coeff_ref,
    table_ref,
    sems,
):
    slots = pad_ref.shape[0]
    levels, width, points = table_ref.shape
    small = [
        pltpu.make_async_copy(source, target, sems.at[i])
        for i, (source, target) in enumerate(
            ((level_hbm, level_ref), (shift_hbm, shift_ref), (pad_hbm, pad_ref))
        )
    ]
    for copy in small:
        copy.start()
    for n in range(levels):
        start_pieces(table_hbm.at[n], table_ref.at[n], 32, sems.at[3])
    start_pieces(coeff_hbm, coeff_ref, 128, sems.at[4])
    pairs = basis_pieces(0, basis_hbm, basis_ref)
    for j, (source, target) in enumerate(pairs):
        start_pieces(source, target, 64, sems.at[6 + j])
    start_pieces(potential_hbm, potential_ref, 8, sems.at[5])
    for copy in small:
        copy.wait()
    wait_all(table_hbm, table_ref, sems.at[3])
    row = lax.broadcasted_iota(jnp.int32, (width, 128), 0)
    for s in range(slots):
        rows = slice(s * width, (s + 1) * width)
        live = jnp.where(row < width - pad_ref[s], 1.0, 0.0).astype(BF16)
        rolled = pltpu.roll(table_ref[level_ref[s]], shift_ref[s], 1)
        for p in range(0, points, 128):
            rolled_ref[rows, p : p + 128] = rolled[:, p : p + 128] * live
    wait_all(coeff_hbm, coeff_ref, sems.at[4])
    turned_ref[...] = coeff_ref[...].T
    out_ref[...] = chunk_of(turned_ref, rolled_ref, wide, wide - 1).astype(BF16).T
    for j, (source, target) in enumerate(pairs):
        wait_all(source, target, sems.at[6 + j])
    wait_all(potential_hbm, potential_ref, sems.at[5])


def first(wide, chips, level, pad, shift, coeff, tables, basis, potential):
    rows, columns = coeff.shape
    points = tables.shape[2]
    slots = pad.shape[0]
    inputs = (level, pad, shift, coeff, tables, basis, potential)
    return call(
        functools.partial(first_kernel, wide, chips),
        "forward_first",
        (
            array((points // wide, columns), BF16),
            array((columns, rows), BF16),
            array((rows, points), BF16),
            array((chips // 2, columns, basis.shape[1]), BF16),
            array(potential.shape, F32),
        ),
        [HBM] * 7,
        (VMEM,) * 5,
        [
            pltpu.SMEM((slots,), jnp.int32),
            pltpu.SMEM((slots,), jnp.int32),
            pltpu.SMEM((slots,), jnp.int32),
            pltpu.VMEM(coeff.shape, coeff.dtype),
            pltpu.VMEM(tables.shape, tables.dtype),
            pltpu.SemaphoreType.DMA((6 + chips,)),
        ],
        flops=2 * rows * points // wide * columns,
        moved=4 * MIB,
    )(*(in_hbm(value) for value in inputs))


def chunk_kernel(wide, chips, k, turned_ref, rolled_ref, far_ref, near_ref):
    store_halves(chips, chunk_of(turned_ref, rolled_ref, wide, k), far_ref, near_ref)


def chunk(wide, chips, k, turned, rolled):
    columns, rows = turned.shape
    own = rolled.shape[1] // wide
    return call(
        functools.partial(chunk_kernel, wide, chips, k),
        "forward_chunk",
        halves(own, columns),
        [VMEM] * 2,
        (VMEM,) * 2,
        flops=2 * rows * own * columns * LONG,
        moved=MIB * LONG,
    )(turned, rolled)


def last_kernel(wide, turned_ref, rolled_ref, basis_hbm, out_ref, basis_ref, sems):
    count = basis_ref.shape[0]
    pairs = basis_pieces(count, basis_hbm, basis_ref)
    for j, (source, target) in enumerate(pairs):
        start_pieces(source, target, 64, sems.at[j])
    out_ref[...] = chunk_of(turned_ref, rolled_ref, wide, 0).T
    for j, (source, target) in enumerate(pairs):
        wait_all(source, target, sems.at[j])


def last(wide, chips, turned, rolled, basis):
    columns, rows = turned.shape
    own = rolled.shape[1] // wide
    count = chips - chips // 2
    return call(
        functools.partial(last_kernel, wide),
        "forward_own",
        (array((own, columns), F32), array((count, columns, basis.shape[1]), BF16)),
        [VMEM, VMEM, HBM],
        (VMEM,) * 2,
        [pltpu.SemaphoreType.DMA((count,))],
    )(turned, rolled, in_hbm(basis))


def combine_kernel(chips, first, mine_ref, whole_ref, *refs):
    count = chips // 2
    parts, outs = refs[:-count], refs[-count:]
    chip = lax.axis_index("narrow") // 2
    rows = outs[0].shape[0]
    for i in range(count):
        target = chip ^ (first + i)
        span = pl.ds(pl.multiple_of(target * rows, rows), rows)
        total = mine_ref[span, :] + whole_ref[span, :].astype(F32)
        start = pl.multiple_of((target % count) * rows, rows)
        for part in parts:
            total = total + part[pl.ds(start, rows), :].astype(F32)
        outs[i][...] = total.astype(BF16)


def combine(chips, first, mine, whole, parts):
    rows, columns = mine.shape
    count = chips // 2
    return call(
        functools.partial(combine_kernel, chips, first),
        "wide_sum",
        (array((rows // chips, columns), BF16),) * count,
        [VMEM] * (len(parts) + 2),
        (VMEM,) * count,
        moved=MIB,
    )(mine, whole, *parts)


def own_points_kernel(x_ref, basis_ref, out_ref):
    out_ref[...] = dot(x_ref[...], basis_ref[0])


def own_points(x, where):
    basis, _ = where
    rows = x.shape[0]
    points = basis.shape[2]
    return call(
        own_points_kernel,
        "points_own",
        array((rows, points), F32),
        [VMEM] * 2,
        VMEM,
        flops=2 * rows * points * x.shape[1],
        moved=2 * MIB,
    )(x, basis)


def more_points_kernel(j, total_ref, x_ref, basis_ref, out_ref):
    out_ref[...] = total_ref[...] + dot(x_ref[...], basis_ref[j])


def more_points(total, x, where):
    basis, j = where
    rows, points = total.shape
    return call(
        functools.partial(more_points_kernel, j),
        "points_more",
        array((rows, points), F32),
        [VMEM] * 3,
        VMEM,
        flops=2 * rows * points * x.shape[1],
        moved=2 * MIB,
    )(total, x, basis)


def last_points_kernel(j, total_ref, x_ref, basis_ref, mine_ref, theirs_ref):
    core = lax.axis_index("narrow") % 2
    rows = mine_ref.shape[0]
    total = total_ref[...] + dot(x_ref[...], basis_ref[j])
    low, high = total[:rows], total[rows:]
    mine_ref[...] = jnp.where(core == 0, low, high)
    theirs_ref[...] = jnp.where(core == 0, high, low)


def last_points(total, x, where):
    basis, j = where
    rows, points = total.shape
    half = array((rows // 2, points), F32)
    return call(
        functools.partial(last_points_kernel, j),
        "points_last",
        (half, half),
        [VMEM] * 3,
        (VMEM, VMEM),
        flops=2 * rows * points * x.shape[1],
        moved=2 * MIB,
    )(total, x, basis)


def act_kernel(mine_ref, other_ref, potential_ref, out_ref):
    on_grid = mine_ref[...] + other_ref[...]
    out_ref[...] = (potential_ref[...] * on_grid).astype(BF16)


def act(mine, other, potential):
    return call(
        act_kernel, "act", array(mine.shape, BF16), [VMEM] * 3, VMEM, moved=MIB
    )(mine, other, potential)


def first_functions_kernel(leave, mine_ref, other_ref, basis_ref, more_ref, *refs):
    outs, both_ref = refs[:-1], refs[-1]
    core = lax.axis_index("narrow") % 2
    rows = mine_ref.shape[0]
    mine, other = mine_ref[...].astype(F32), other_ref[...].astype(F32)
    both_ref[:rows] = jnp.where(core == 0, mine, other).astype(BF16)
    both_ref[rows:] = jnp.where(core == 0, other, mine).astype(BF16)
    for j, out in zip(leave, outs):
        half = basis_ref.shape[0]
        block = basis_ref[j] if j < half else more_ref[j - half]
        out[...] = dot_turned(both_ref[...], block).astype(BF16)


def first_functions(leave, mine, other, basis, more):
    rows, points = mine.shape
    columns = basis.shape[1]
    return call(
        functools.partial(first_functions_kernel, leave),
        "functions_first",
        (array((2 * rows, columns), BF16),) * len(leave) + (array((2 * rows, points), BF16),),
        [VMEM] * 4,
        (VMEM,) * (len(leave) + 1),
    )(mine, other, basis, more)


def functions_kernel(j, both_ref, basis_ref, out_ref):
    out_ref[...] = dot_turned(both_ref[...], basis_ref[j]).astype(BF16)


def functions(both, where):
    basis, j = where
    rows, points = both.shape
    columns = basis.shape[1]
    return call(
        functools.partial(functions_kernel, j),
        "functions_more",
        array((rows, columns), BF16),
        [VMEM] * 2,
        VMEM,
        flops=2 * rows * points * columns,
        moved=2 * MIB,
    )(both, basis)


def assemble_kernel(visits, *refs):
    parts, out_ref = refs[:-1], refs[-1]
    chip = lax.axis_index("narrow") // 2
    rows = parts[0].shape[0]
    for j, part in zip(visits, parts):
        start = pl.multiple_of((chip ^ j) * rows, rows)
        out_ref[pl.ds(start, rows), :] = part[...]


def assemble(visits, parts):
    rows, columns = parts[0].shape
    chips = len(parts)
    return call(
        functools.partial(assemble_kernel, visits),
        "assemble",
        array((rows * chips, columns), BF16),
        [VMEM] * chips,
        VMEM,
        moved=MIB // 4,
    )(*parts)


def diagonal_kernel(pad_ref, coeff_ref, row_ref, column_ref, out_ref):
    slots = pad_ref.shape[0]
    width = coeff_ref.shape[0] // slots
    row = lax.broadcasted_iota(jnp.int32, (width, out_ref.shape[1]), 0)
    for s in range(slots):
        rows = slice(s * width, (s + 1) * width)
        energy = row_ref[rows, :] + column_ref[...]
        diagonal = energy * coeff_ref[rows, :].astype(F32)
        out_ref[rows, :] = jnp.where(row < width - pad_ref[s], diagonal, 0.0)


def diagonal(pad, coeff, row_energy, column_energy):
    smem = pl.BlockSpec(memory_space=pltpu.SMEM)
    return call(
        diagonal_kernel,
        "diagonal",
        array(coeff.shape, F32),
        [smem] + [VMEM] * 3,
        VMEM,
    )(pad, coeff, row_energy[:, None], column_energy[None, :])


def more_kernel(wide, k, total_ref, rolled_ref, grid_ref, out_ref):
    own = rolled_ref.shape[1] // wide
    start = pl.multiple_of((lax.axis_index("wide") ^ k) * own, own)
    out_ref[...] = total_ref[...] + dot(rolled_ref[:, pl.ds(start, own)], grid_ref[...])


def backward_more(wide, k, total, rolled, grid):
    rows, columns = total.shape
    return call(
        functools.partial(more_kernel, wide, k),
        "backward_more",
        array(total.shape, F32),
        [VMEM] * 3,
        VMEM,
        flops=2 * rows * columns * rolled.shape[1] // wide,
        moved=3 * MIB,
    )(total, rolled, grid)


def end_kernel(wide, k, total_ref, rolled_ref, grid_ref, out_hbm, out_ref, sems):
    own = rolled_ref.shape[1] // wide
    start = pl.multiple_of((lax.axis_index("wide") ^ k) * own, own)
    steps = sems.shape[0]
    rows = rolled_ref.shape[0] // steps
    for i in range(steps):
        span = pl.ds(i * rows, rows)
        part = dot(rolled_ref[span, pl.ds(start, own)], grid_ref[...])
        out_ref[span, :] = total_ref[span, :] + part
        start_pieces(out_ref.at[span], out_hbm.at[span], rows // 4, sems.at[i])
    for i in range(steps):
        span = pl.ds(i * rows, rows)
        wait_all(out_ref.at[span], out_hbm.at[span], sems.at[i])


def backward_end(wide, k, total, rolled, grid):
    rows, columns = total.shape
    return call(
        functools.partial(end_kernel, wide, k),
        "backward_end",
        array(total.shape, F32),
        [VMEM] * 3,
        HBM,
        [pltpu.VMEM(total.shape, F32), pltpu.SemaphoreType.DMA((4,))],
        flops=2 * rows * columns * rolled.shape[1] // wide,
        moved=4 * MIB,
    )(total, rolled, grid)


def exchange(value, step, size, axis):
    return lax.ppermute(value, axis, [(i, i ^ step) for i in range(size)])


def body(
    wide,
    narrow,
    coeff,
    groupb_row_energy,
    groupa_energy,
    groupb_basis_values,
    basis_a,
    potential,
    slot_sparse_level,
    block_pad,
    slot_grid_offset,
):
    chips = narrow // 2
    tables = jnp.swapaxes(groupb_basis_values, 1, 2)
    half = chips // 2
    order = list(range(1, wide - 1))
    whole, turned, rolled, basis, pot = first(
        wide,
        chips,
        slot_sparse_level,
        block_pad,
        slot_grid_offset,
        coeff,
        tables,
        basis_a,
        potential,
    )
    whole = exchange(whole, wide - 1, wide, "wide")
    sent = {k: chunk(wide, chips, k, turned, rolled) for k in order}
    far_parts = [exchange(sent[k][0], k, wide, "wide") for k in order]
    near_parts = [exchange(sent[k][1], k, wide, "wide") for k in order]
    mine, more = last(wide, chips, turned, rolled, basis_a)
    where = {j: (basis, j) if j < half else (more, j - half) for j in range(chips)}
    pieces = combine(chips, half, mine, whole, far_parts)
    xs = {j: exchange(pieces[j - half], 2 * j, narrow, "narrow") for j in range(half, chips)}
    pieces = combine(chips, 0, mine, whole, near_parts)
    for j in range(1, half):
        xs[j] = exchange(pieces[j], 2 * j, narrow, "narrow")
    total = own_points(pieces[0], where[0])
    visits = list(range(half, chips)) + list(range(1, half))
    for j in visits[:-1]:
        total = more_points(total, xs[j], where[j])
    mine, theirs = last_points(total, xs[visits[-1]], where[visits[-1]])
    acted = act(mine, exchange(theirs, 1, narrow, "narrow"), pot)
    other = exchange(acted, 1, narrow, "narrow")
    leave = visits
    *out, both = first_functions(leave, acted, other, basis, more)
    blocks = {j: exchange(out[i], 2 * j, narrow, "narrow") for i, j in enumerate(leave)}
    grid = assemble([0] + leave, [functions(both, where[0])] + [blocks[j] for j in leave])
    steps = [wide - 1] + order
    grids = {k: exchange(grid, k, wide, "wide") for k in steps}
    total = diagonal(block_pad, coeff, groupb_row_energy, groupa_energy)
    total = backward_more(wide, 0, total, rolled, grid)
    for k in steps[:-1]:
        total = backward_more(wide, k, total, rolled, grids[k])
    return backward_end(wide, steps[-1], total, rolled, grids[steps[-1]])


def solution(mesh):
    return jax.shard_map(
        functools.partial(body, mesh.shape["wide"], mesh.shape["narrow"]),
        mesh=mesh,
        in_specs=(
            P("wide", "narrow"),
            P("wide"),
            P("narrow"),
            P(),
            P(),
            P(("wide", "narrow"), None),
            P("wide"),
            P("wide"),
            P("wide"),
        ),
        out_specs=P("wide", "narrow"),
        check_vma=False,
    )
```
